32 devices in a mesh: dp: 4 (over x, core), expert: 8 (over z, y).
Axes of the slice: x: 2, y: 2, z: 4, core: 2. Of those that a mesh axis runs over, the one named last changes fastest.
Arguments:
- hidden_in: bfloat16 [8192, 1280], P(('dp', 'expert')), may hold values from -6 to 6
- out_grad: bfloat16 [8192, 1280], P(('dp', 'expert')), may hold values from -6 to 6
- segment_ids: int32 [32, 256], P(('dp', 'expert')), may hold values from 0 to 3, never falling along the last dimension, each value on 1 to 128 neighbouring positions
- routes: int32 [8192, 7], P(('dp', 'expert')), may hold values from 0 to 15, all different within a row; in each aligned block of 256 rows (0 to 255, 256 to 511, ...) at most 160 rows name the same one
- attn_gain: bfloat16 [1280], P('expert'), may hold values from 0.099609375 to 1.8984375
- w_query: bfloat16 [1280, 1280], P('expert'), may hold values from -0.15625 to 0.15625
- w_key: bfloat16 [1280, 1280], P('expert'), may hold values from -0.15625 to 0.15625
- w_value: bfloat16 [1280, 1280], P('expert'), may hold values from -0.15625 to 0.15625
- w_out: bfloat16 [1280, 1280], P('expert'), may hold values from -1 to 1
- moe_gain: bfloat16 [1280], P('expert'), may hold values from 0.099609375 to 1.8984375
- w_router: bfloat16 [1280, 16], P('expert'), may hold values from -0.078125 to 0.078125
- shared_gate: bfloat16 [1280, 896], P('expert'), may hold values from -0.15625 to 0.15625
- shared_up: bfloat16 [1280, 896], P('expert'), may hold values from -0.15625 to 0.15625
- shared_down: bfloat16 [896, 1280], P('expert'), may hold values from -0.1875 to 0.1875
- expert_gate: bfloat16 [16, 1280, 896], P('expert'), may hold values from -0.15625 to 0.15625
- expert_up: bfloat16 [16, 1280, 896], P('expert'), may hold values from -0.15625 to 0.15625
- expert_down: bfloat16 [16, 896, 1280], P('expert'), may hold values from -0.375 to 0.375
Outputs:
- output: float32 [8192, 1280], P(('dp', 'expert'))
- input_grad: float32 [8192, 1280], P(('dp', 'expert'))
- attn_gain_grad: float32 [1280], P('expert')
- w_query_grad: float32 [1280, 1280], P('expert')
- w_key_grad: float32 [1280, 1280], P('expert')
- w_value_grad: float32 [1280, 1280], P('expert')
- w_out_grad: float32 [1280, 1280], P('expert')
- moe_gain_grad: float32 [1280], P('expert')
- w_router_grad: float32 [1280, 16], P('expert')
- shared_gate_grad: float32 [1280, 896], P('expert')
- shared_up_grad: float32 [1280, 896], P('expert')
- shared_down_grad: float32 [896, 1280], P('expert')
- expert_gate_grad: float32 [16, 1280, 896], P('expert')
- expert_up_grad: float32 [16, 1280, 896], P('expert')
- expert_down_grad: float32 [16, 896, 1280], P('expert')
The draws below stay inside these ranges and needn't reach their ends.
Inputs may be any that keep to these rules, and one draw needn't show every extreme that they name: `routes`: in the rows of one device every expert is named by at most 160 rows, a bound that some block reaches; a token names 7 different experts. `segment_ids`: document numbers never fall along a sequence; each document has 1 to 128 tokens.
All inputs are finite; a program needn't handle non-finite values.
Results may differ from the reference program's by a relative error of at most 0.02.
Values may be sent and summed in bfloat16 or wider, within the bound.
No kernel may reach another device: no remote copies, remote signals or barrier semaphores. Data moves between devices by JAX's collectives and lax.ppermute only.
A program may use at most 256 MiB of HBM per device.

```python
import math
import jax
import jax.numpy as jnp
import numpy as np
from jax import lax

D = 1280
HEADS = 10
HD = 128
FF = 896
TOP = 7
DOCS = 4
TOK_DEV = 256
EXPERTS = 16
NSEQ = 32
TOKENS = 8192
CAP = 160
N_DP = 4
N_EXPERT = 8


def block_levels(own_key, shape, pieces, low, top_value):
    loudness = 1.0
    for dim, parts in pieces:
        draws = jax.random.uniform(jax.random.fold_in(jax.random.fold_in(own_key, 6), dim), (parts,), jnp.float32, low / len(pieces), top_value / len(pieces))
        loudness = loudness * jnp.repeat(jnp.exp(draws), shape[dim] // parts).reshape((-1,) + (1,) * (len(shape) - 1 - dim))
    return loudness


def split_up(number_of, total, limit, skew):
    portions = [(1 << 20) // math.isqrt(rank ** skew) + 1 for rank in range(2, number_of + 1)]
    surplus, holding = total - limit - (number_of - 1), [1] * (number_of - 1)
    while surplus > 0:
        free = [i for i in range(number_of - 1) if holding[i] < limit]
        mass, budget = sum([portions[i] for i in free]), surplus
        for i in free:
            extra = min(limit - holding[i], max(1, budget * portions[i] // mass), surplus)
            holding[i] = holding[i] + extra
            surplus = surplus - extra
    return np.array([limit] + holding)


def ragged_sizes(stream_key, number_of, total, reach, skew):
    if number_of == 2:
        one = jax.random.randint(stream_key, (), max(1, total - reach), min(reach, total - 1) + 1)
        return jnp.stack([one, total - one])
    lengths = jnp.asarray(split_up(number_of, total, reach, skew), jnp.int32)
    pairs = (number_of - 1) // 2
    giver, receiver = lengths[1:1 + 2 * pairs:2], lengths[2:2 + 2 * pairs:2]
    margin = jnp.minimum(giver - 1, reach - receiver)
    passed = jax.random.randint(jax.random.fold_in(stream_key, 1), (pairs,), 0, 1 << 20) % (margin + 1)
    lengths = lengths.at[1:1 + 2 * pairs:2].set(giver - passed).at[2:2 + 2 * pairs:2].set(receiver + passed)
    return lengths[jax.random.permutation(jax.random.fold_in(stream_key, 2), number_of)]


def assign_block(own_key, own, number, rows, count, top, bound, slope):
    sequence = jax.random.permutation(own_key, count)
    heavy_load, ordinary = shares(count, rows * top, bound, slope, True), shares(count, rows * top, bound, slope, False)
    places = jnp.arange(count)

    def named(lengths, offset_by):
        used = int((lengths > 0).sum())
        fixed = max(1, used // 4)
        shifted = fixed + (places - fixed + offset_by * (used - fixed)) % max(1, count - fixed)
        return jnp.zeros((count,), jnp.int32).at[sequence[jnp.where(places < fixed, places, shifted)]].set(jnp.asarray(lengths, jnp.int32))

    lengths = jnp.where(number % 4 == 0, named(heavy_load, number // 4), named(ordinary, number - number // 4 - 1))
    mixed = jax.random.permutation(jax.random.fold_in(own, 3), count)
    giver, taker = mixed[0:count // 2 * 2:2], mixed[1:count // 2 * 2:2]
    slack = jnp.minimum(lengths[giver] - 1, bound - lengths[taker]) // 2
    slack = jnp.where((giver == sequence[0]) | (taker == sequence[0]) | (lengths[taker] == 0), 0, jnp.maximum(slack, 0))
    shifted = jax.random.randint(jax.random.fold_in(own, 4), (count // 2,), 0, 1 << 20) % (slack + 1)
    lengths = lengths.at[giver].add(-shifted).at[taker].add(shifted)
    members = jnp.searchsorted(jnp.cumsum(lengths), jnp.arange(rows * top), side="right").astype(jnp.int32)
    table = members.reshape(top, rows).T
    table = table[jax.random.permutation(jax.random.fold_in(own, 1), rows)]
    offset_by = jax.random.randint(jax.random.fold_in(own, 2), (rows, 1), 0, top)
    return jnp.take_along_axis(table, (jnp.arange(top)[None, :] + offset_by) % top, axis=1)


def shares(amount, total, bound, skew, full):
    portions = [(1 << 20) // math.isqrt(grade ** skew) + 1 for grade in range(1, amount + 1)]
    largest = bound if full else min(bound, max(-(-total // amount), total * portions[0] // sum(portions)))
    least = 1 if total - largest >= amount - 1 else 0
    given, rest = [largest] + [least] * (amount - 1), total - largest - least * (amount - 1)
    while rest > 0:
        movable = [i for i in range(1, amount) if given[i] < largest] or [i for i in range(1, amount) if given[i] < bound]
        pool, remaining = sum([portions[i] for i in movable]), rest
        for i in movable:
            more = min(bound - given[i], max(1, remaining * portions[i] // pool), rest)
            given[i] = given[i] + more
            rest = rest - more
    return np.array(given)


def centred(rng, extent, deviation, limit, split=(), kind=jnp.bfloat16):
    array = deviation * jax.random.normal(rng, extent, jnp.float32)
    if split:
        array = array * block_levels(rng, extent, split, -0.22, 0.18)
    return jnp.clip(array, -limit, limit).astype(kind)


def setup_inputs(seed: int = 0) -> dict:
    streams_of = jax.random.split(jax.random.key(seed), 18)
    hidden_in = centred(streams_of[0], (TOKENS, D), 1.0, 6.0, ((0, 32),))
    out_grad = centred(streams_of[1], (TOKENS, D), 1.0, 6.0, ((0, 32),))
    segment_ids = jax.vmap(lambda own: jnp.searchsorted(jnp.cumsum(ragged_sizes(own, DOCS, TOK_DEV, TOK_DEV // 2, 0)), jnp.arange(TOK_DEV), side="right"))(jax.random.split(streams_of[2], NSEQ)).reshape((NSEQ, TOK_DEV)).astype(jnp.int32)
    routes_keys = jax.random.split(jax.random.fold_in(streams_of[3], 1), TOKENS // TOK_DEV)
    routes_turns = jax.random.permutation(jax.random.fold_in(streams_of[3], 3), TOKENS // TOK_DEV)
    routes = jax.vmap(lambda own, number: assign_block(jax.random.fold_in(streams_of[3], 2), own, number, TOK_DEV, EXPERTS, TOP, CAP, 1))(routes_keys, routes_turns).reshape((TOKENS, TOP))
    attn_gain = jnp.clip(1.0 + 0.18 * jax.random.normal(streams_of[4], (D,), jnp.float32), 0.099609375, 1.8984375).astype(jnp.bfloat16)
    w_query = centred(streams_of[5], (D, D), D ** -0.5, 0.15625, ((0, 8),))
    w_key = centred(streams_of[6], (D, D), D ** -0.5, 0.15625, ((0, 8),))
    w_value = centred(streams_of[7], (D, D), D ** -0.5, 0.15625, ((0, 8),))
    w_out = centred(streams_of[8], (D, D), (D // 32) ** -0.5, 1.0, ((0, 8),))
    moe_gain = jnp.clip(1.0 + 0.18 * jax.random.normal(streams_of[9], (D,), jnp.float32), 0.099609375, 1.8984375).astype(jnp.bfloat16)
    w_router = centred(streams_of[10], (D, EXPERTS), (4 * D) ** -0.5, 0.078125, ((0, 8),))
    shared_gate = centred(streams_of[11], (D, FF), D ** -0.5, 0.15625, ((0, 8),))
    shared_up = centred(streams_of[12], (D, FF), D ** -0.5, 0.15625, ((0, 8),))
    shared_down = centred(streams_of[13], (FF, D), FF ** -0.5, 0.1875, ((0, 8),))
    expert_gate = centred(streams_of[14], (EXPERTS, D, FF), D ** -0.5, 0.15625, ((0, 8),))
    expert_up = centred(streams_of[15], (EXPERTS, D, FF), D ** -0.5, 0.15625, ((0, 8),))
    expert_down = centred(streams_of[16], (EXPERTS, FF, D), (FF // 4) ** -0.5, 0.375, ((0, 8),))
    return {"hidden_in": hidden_in, "out_grad": out_grad, "segment_ids": segment_ids, "routes": routes, "attn_gain": attn_gain, "w_query": w_query, "w_key": w_key, "w_value": w_value, "w_out": w_out, "moe_gain": moe_gain, "w_router": w_router, "shared_gate": shared_gate, "shared_up": shared_up, "shared_down": shared_down, "expert_gate": expert_gate, "expert_up": expert_up, "expert_down": expert_down}


@jax.custom_vjp
def low(v):
    return lax.optimization_barrier(v.astype(jnp.bfloat16)).astype(jnp.float32)

@jax.custom_vjp
def low_back(v):
    return v

def low_keep(v):
    return (low(v), None)

def low_pass(kept, grad):
    return (grad,)

def back_keep(v):
    return (v, None)

def back_low(kept, grad):
    return (low(grad),)
low.defvjp(low_keep, low_pass)
low_back.defvjp(back_keep, back_low)
epsilon = 1e-06
rope_base = 10000.0
masked_score = -1e+30
highest = lax.Precision.HIGHEST

def matmul_high(left, right):
    return jnp.dot(left, right, precision=highest)

def rms_norm(values, gain_vec):
    inv_rms = lax.rsqrt(lax.optimization_barrier(jnp.mean(values * values, axis=-1, keepdims=True)) + epsilon)
    return values * inv_rms * gain_vec

def rope_tables(length, head_size):
    half_width = head_size // 2
    frequency = rope_base ** (-2.0 * jnp.arange(half_width, dtype=jnp.float32) / head_size)
    angles = jnp.arange(length, dtype=jnp.float32)[:, None] * frequency[None, :]
    cosine_table = jnp.concatenate([jnp.cos(angles), jnp.cos(angles)], axis=-1)[:, None, :]
    sine_table = jnp.concatenate([jnp.sin(angles), jnp.sin(angles)], axis=-1)[:, None, :]
    return (cosine_table, sine_table)

def rotary(values, cosine_table, sine_table):
    half_width = values.shape[-1] // 2
    turned = jnp.concatenate([-values[..., half_width:], values[..., :half_width]], axis=-1)
    return values * cosine_table + turned * sine_table

def attend(packed):
    query, keys, values_in, segment_row = packed
    length = query.shape[0]
    place = jnp.arange(length)
    allowed = (segment_row[:, None] == segment_row[None, :]) & (place[None, :] <= place[:, None])
    raw = jnp.einsum('thd,shd->hts', query, keys, precision=highest) * query.shape[-1] ** (-0.5)
    scores = jnp.where(allowed[None], low_back(raw), masked_score)
    weights = low(jax.nn.softmax(scores, axis=-1))
    mixed = jnp.einsum('hts,shd->thd', weights, values_in, precision=highest)
    return low(low_back(mixed))

def apply_experts(packed):
    rows_in, gate_w, up_w, down_w = packed
    gate_pre = low_back(matmul_high(rows_in, gate_w))
    up_pre = low_back(matmul_high(rows_in, up_w))
    return matmul_high(low(jax.nn.silu(gate_pre) * up_pre), down_w)

def reference(hidden_in, out_grad, segment_ids, routes, attn_gain, w_query, w_key, w_value, w_out, moe_gain, w_router, shared_gate, shared_up, shared_down, expert_gate, expert_up, expert_down):
    seq_count = N_DP * N_EXPERT
    cosine_table, sine_table = rope_tables(TOK_DEV, HD)
    flat_routes = routes.reshape(-1).astype(jnp.int32)
    route_hot = (flat_routes[:, None] == jnp.arange(EXPERTS, dtype=jnp.int32)[None, :]).astype(jnp.int32)
    route_hot = route_hot.reshape(seq_count, TOK_DEV * TOP, EXPERTS)
    slot_rank = lax.optimization_barrier(jnp.sum((jnp.cumsum(route_hot, axis=1) - route_hot) * route_hot, axis=-1)).reshape(-1)
    owner = jnp.arange(TOKENS * TOP, dtype=jnp.int32) // (TOK_DEV * TOP)
    buffer_row = (owner * CAP + slot_rank).astype(jnp.int32)
    choose = (routes[:, :, None] == jnp.arange(EXPERTS, dtype=jnp.int32)[None, None, :]).astype(jnp.float32)

    def forward_layer(layer_inputs, first_norm_gain, query_matrix, key_matrix, value_matrix, output_weight, second_norm_gain, router_weight, shared_gate_weight, shared_up_weight, shared_down_weight, expert_gate_weight, expert_up_weight, expert_down_weight):
        normed_attn = low(rms_norm(layer_inputs, first_norm_gain))
        q_pre = matmul_high(normed_attn, query_matrix).reshape(seq_count, TOK_DEV, HEADS, HD)
        k_pre = matmul_high(normed_attn, key_matrix).reshape(seq_count, TOK_DEV, HEADS, HD)
        v_pre = matmul_high(normed_attn, value_matrix).reshape(seq_count, TOK_DEV, HEADS, HD)
        query = low(rotary(low_back(q_pre), cosine_table, sine_table))
        keys = low(rotary(low_back(k_pre), cosine_table, sine_table))
        values_all = low(low_back(v_pre))
        attended = lax.map(jax.checkpoint(attend), (query, keys, values_all, segment_ids))
        attn_out = low_back(matmul_high(attended.reshape(TOKENS, D), output_weight))
        residual = layer_inputs + attn_out
        normed_moe = low(rms_norm(residual, second_norm_gain))
        logits = low_back(matmul_high(normed_moe, router_weight))
        picked = lax.optimization_barrier(jnp.sum(choose * logits[:, None, :], axis=-1))
        gate_probs = jax.nn.softmax(picked, axis=-1)
        shared_gate_pre = low_back(matmul_high(normed_moe, shared_gate_weight))
        shared_up_pre = low_back(matmul_high(normed_moe, shared_up_weight))
        shared_hidden = low(jax.nn.silu(shared_gate_pre) * shared_up_pre)
        shared_out = low_back(matmul_high(shared_hidden, shared_down_weight))
        pair_in = low_back(jnp.broadcast_to(normed_moe[:, None, :], (TOKENS, TOP, D)).reshape(TOKENS * TOP, D))
        holding_buffer = jnp.zeros((EXPERTS, seq_count * CAP, D), jnp.float32).at[flat_routes, buffer_row].set(pair_in)
        layer_results = lax.map(jax.checkpoint(apply_experts), (holding_buffer, expert_gate_weight, expert_up_weight, expert_down_weight))
        pair_out = low(low_back(layer_results[flat_routes, buffer_row])).reshape(TOKENS, TOP, D)
        routed = lax.optimization_barrier(jnp.sum(gate_probs[:, :, None] * pair_out, axis=1))
        return residual + shared_out + routed
    params = (hidden_in.astype(jnp.float32), attn_gain.astype(jnp.float32), w_query.astype(jnp.float32), w_key.astype(jnp.float32), w_value.astype(jnp.float32), w_out.astype(jnp.float32), moe_gain.astype(jnp.float32), w_router.astype(jnp.float32), shared_gate.astype(jnp.float32), shared_up.astype(jnp.float32), shared_down.astype(jnp.float32), expert_gate.astype(jnp.float32), expert_up.astype(jnp.float32), expert_down.astype(jnp.float32))
    output, pull_back = jax.vjp(forward_layer, *params)
    input_grad, attn_gain_grad, w_query_grad, w_key_grad, w_value_grad, w_out_grad, moe_gain_grad, w_router_grad, shared_gate_grad, shared_up_grad, shared_down_grad, expert_gate_grad, expert_up_grad, expert_down_grad = pull_back(out_grad.astype(jnp.float32))
    return (output, input_grad, attn_gain_grad, w_query_grad, w_key_grad, w_value_grad, w_out_grad, moe_gain_grad, w_router_grad, shared_gate_grad, shared_up_grad, shared_down_grad, expert_gate_grad, expert_up_grad, expert_down_grad)
```

```python
import functools

import jax
import jax.numpy as jnp
import numpy as np
from jax import lax
from jax.experimental import pallas as pl
from jax.experimental.pallas import tpu as pltpu
from jax.sharding import PartitionSpec as P

HD = 128
LANES = 128
EPS = 1e-06
ROPE_BASE = 10000.0
MASKED = -1e30
BF = jnp.bfloat16
F32 = jnp.float32
VMEM = pltpu.VMEM
SMEM = pltpu.SMEM
MIB = 1 << 20


def dot(a, b):
    return jnp.dot(a, b, preferred_element_type=F32)


def dot_nt(a, b):
    return lax.dot_general(a, b, (((1,), (1,)), ((), ())), preferred_element_type=F32)


def dot_tn(a, b):
    return lax.dot_general(a, b, (((0,), (0,)), ((), ())), preferred_element_type=F32)


def sigmoid(v):
    return 1.0 / (1.0 + jnp.exp(-v))


def whole(space=VMEM):
    return pl.BlockSpec(memory_space=space)


def anywhere():
    return pl.BlockSpec(memory_space=pl.ANY)


def params(mib):
    return pltpu.CompilerParams(vmem_limit_bytes=mib * MIB)


def cost(flops, nbytes):
    return pl.CostEstimate(flops=int(flops), bytes_accessed=int(nbytes), transcendentals=0)


def shape(dims, dtype):
    return jax.ShapeDtypeStruct(dims, dtype)


def cycle(n):
    return list(range(0, n, 2)) + list(range(1, n, 2))[::-1]


def ring_perm(nd, ne):
    ring = cycle(ne)
    pos = {e: i for i, e in enumerate(ring)}
    pairs = []
    for d in range(nd):
        for e in range(ne):
            step = 1 if d % 2 == 0 else -1
            pairs.append((d * ne + e, d * ne + ring[(pos[e] + step) % ne]))
    return pairs


def ring_order(ne):
    ring = cycle(ne)
    pos = {e: i for i, e in enumerate(ring)}
    table = np.zeros((2, ne, ne), np.int32)
    for c in range(2):
        step = 1 if c == 0 else -1
        for e in range(ne):
            for s in range(ne):
                table[c, e, s] = ring[(pos[e] - step * s) % ne]
    return table


def load_rows(idx_ref, pieces, w_ref, sems, height):
    copies = []
    for i, piece in enumerate(pieces):
        start = pl.multiple_of(idx_ref[i] * height, 16)
        copy = pltpu.make_async_copy(piece, w_ref.at[pl.ds(start, height), :], sems.at[i])
        copy.start()
        copies.append(copy)
    return copies


def load_halves(idx_ref, pieces, w_ref, sems, height, width):
    copies = []
    for i, piece in enumerate(pieces):
        owner = idx_ref[i] // 2
        half = idx_ref[i] % 2
        copy = pltpu.make_async_copy(
            piece,
            w_ref.at[
                pl.ds(pl.multiple_of(owner * height, 16), height),
                pl.ds(pl.multiple_of(half * width, LANES), width),
            ],
            sems.at[i],
        )
        copy.start()
        copies.append(copy)
    return copies


def rope(u, cos, sin):
    return u * cos + pltpu.roll(u, HD // 2, 1) * sin


def rope_back(u, cos, sin):
    return u * cos - pltpu.roll(u, HD // 2, 1) * sin


def allowed_mask(seg_col, seg_row):
    n = seg_row.shape[1]
    rows = lax.broadcasted_iota(jnp.int32, (n, n), 0)
    cols = lax.broadcasted_iota(jnp.int32, (n, n), 1)
    return (seg_col == seg_row) & (cols <= rows)


def head_probs(q, k, allowed):
    s = dot_nt(q, k) * (HD ** -0.5)
    s = jnp.where(allowed, s, MASKED)
    e = jnp.exp(s - jnp.max(s, axis=1, keepdims=True))
    return e / jnp.sum(e, axis=1, keepdims=True)


def attn_forward(n_exp, idx_ref, hid_ref, segc_ref, segr_ref, routes_ref, cos_ref, sin_ref, *rest):
    n = idx_ref.shape[0]
    pieces = rest[:n]
    xn_ref, q_ref, k_ref, v_ref, att_ref, res_ref, pay_ref, gate_ref, gains_ref, w_ref, sems = rest[n:]
    height = pieces[0].shape[0]
    tok, d = hid_ref.shape
    copies = load_rows(idx_ref, pieces, w_ref, sems, height)
    x = hid_ref[...].astype(F32)
    inv = lax.rsqrt(jnp.mean(x * x, axis=1, keepdims=True) + EPS)
    cos = cos_ref[...]
    sin = sin_ref[...]
    allowed = allowed_mask(segc_ref[...], segr_ref[...])
    for copy in copies:
        copy.wait()
    aux = w_ref[:, 4 * d : 4 * d + LANES]
    turned = aux.astype(F32).T
    gains = turned[n_exp : n_exp + 8, :]
    gains_ref[...] = gains
    xn = (x * inv * gains[0:1, :]).astype(BF)
    xn_ref[...] = xn
    pair = 2 * HD
    for c in range(0, d, pair):
        qp = dot(xn, w_ref[:, c : c + pair])
        kp = dot(xn, w_ref[:, d + c : d + c + pair])
        vp = dot(xn, w_ref[:, 2 * d + c : 2 * d + c + pair])
        v_ref[:, c : c + pair] = vp.astype(BF)
        for o in range(0, pair, HD):
            q = rope(qp[:, o : o + HD], cos, sin).astype(BF)
            k = rope(kp[:, o : o + HD], cos, sin).astype(BF)
            q_ref[:, c + o : c + o + HD] = q
            k_ref[:, c + o : c + o + HD] = k
            probs = head_probs(q, k, allowed).astype(BF)
            att_ref[:, c + o : c + o + HD] = dot(probs, vp[:, o : o + HD].astype(BF)).astype(BF)
    res = x + dot(att_ref[...], w_ref[:, 3 * d : 4 * d])
    res_ref[...] = res
    inv2 = lax.rsqrt(jnp.mean(res * res, axis=1, keepdims=True) + EPS)
    act = (res * inv2 * gains[1:2, :]).astype(BF)
    logits = dot(act, aux)
    lane = lax.broadcasted_iota(jnp.int32, (tok, LANES), 1)
    routes = routes_ref[...]
    chosen = routes[:, 0:1] == lane
    for j in range(1, routes.shape[1]):
        chosen = chosen | (routes[:, j : j + 1] == lane)
    logits = jnp.where(chosen, logits, MASKED)
    e = jnp.where(chosen, jnp.exp(logits - jnp.max(logits, axis=1, keepdims=True)), 0.0)
    gate = e / jnp.sum(e, axis=1, keepdims=True)
    gate_ref[...] = gate
    gate_t = gate.T[0:n_exp, :]
    high = gate_t.astype(BF)
    pay_ref[0:tok, :] = act
    pay_ref[tok : tok + n_exp, :] = jnp.zeros((n_exp, d), BF)
    pay_ref[tok : tok + n_exp, 0:tok] = high
    pay_ref[tok : tok + n_exp, tok : 2 * tok] = (gate_t - high.astype(F32)).astype(BF)


def expert_block(nb, cap, n_exp, aliased, scal_ref, *refs):
    pays = refs[:nb]
    grads = refs[nb : 2 * nb]
    wg_ref, wu_ref, wd_ref = refs[2 * nb : 2 * nb + 3]
    outs = refs[2 * nb + 3 + aliased :]
    xr_ref, gr_ref, gh_ref, dg_ref, du_ref = outs[:5]
    in_refs = outs[5 : 5 + nb]
    out_refs = outs[5 + nb : 5 + 2 * nb]
    in_acc, out_acc, gg_acc = outs[5 + 2 * nb :]
    step = pl.program_id(0)
    steps = pl.num_programs(0)
    ge = scal_ref[step]
    tok = grads[0].shape[0]
    rowid = lax.broadcasted_iota(jnp.int32, (n_exp, tok), 0)
    tri = (
        lax.broadcasted_iota(jnp.int32, (tok, tok), 0)
        < lax.broadcasted_iota(jnp.int32, (tok, tok), 1)
    )
    tri = jnp.where(tri, 1.0, 0.0).astype(BF)
    slots = lax.broadcasted_iota(jnp.int32, (cap, tok), 0)
    masks, picks, gates = [], [], []
    for b in range(nb):
        gt = pays[b][tok : tok + n_exp, 0:tok].astype(F32)
        gt = gt + pays[b][tok : tok + n_exp, tok : 2 * tok].astype(F32)
        g = jnp.sum(jnp.where(rowid == ge, gt, 0.0), axis=0, keepdims=True)
        sel = jnp.where(g > 0.0, 1.0, 0.0)
        rank = dot(jnp.broadcast_to(sel, (8, tok)).astype(BF), tri)[0:1, :]
        slot = jnp.where(g > 0.0, rank, -1.0).astype(jnp.int32)
        mask = slots == slot
        pick = jnp.where(mask, 1.0, 0.0).astype(BF)
        gates.append(jnp.sum(jnp.where(mask, g, 0.0), axis=1, keepdims=True))
        masks.append(mask)
        picks.append(pick)
        xr_ref[0, b * cap : (b + 1) * cap, :] = dot(pick, pays[b][0:tok, :]).astype(BF)
        gr_ref[0, b * cap : (b + 1) * cap, :] = dot(pick, grads[b][...]).astype(BF)
    gs = jnp.concatenate(gates, axis=0)
    eg = dot(xr_ref[0], wg_ref[0])
    eu = dot(xr_ref[0], wu_ref[0])
    hu = dot_nt(gr_ref[0], wd_ref[0])
    sig = sigmoid(eg)
    h = eg * sig * eu
    gg = jnp.sum(h.astype(BF).astype(F32) * hu, axis=1, keepdims=True)
    gh_ref[0] = (gs * h).astype(BF)
    hg = gs * hu
    dg_ref[0] = (hg * eu * sig * (1.0 + eg * (1.0 - sig))).astype(BF)
    du_ref[0] = (hg * eg * sig).astype(BF)
    xi = (dot_nt(dg_ref[0], wg_ref[0]) + dot_nt(du_ref[0], wu_ref[0])).astype(BF)
    yo = dot(gh_ref[0], wd_ref[0]).astype(BF)
    for b in range(nb):
        rows = slice(b * cap, (b + 1) * cap)
        inp = dot_tn(picks[b], xi[rows])
        outp = dot_tn(picks[b], yo[rows])
        row = jnp.sum(jnp.where(masks[b], gg[rows], 0.0), axis=0, keepdims=True)
        ggm = jnp.where(rowid == ge, row, 0.0)

        @pl.when(step == 0)
        def _():
            in_acc[b] = inp
            out_acc[b] = outp
            gg_acc[b] = ggm

        @pl.when(step > 0)
        def _():
            in_acc[b] += inp
            out_acc[b] += outp
            gg_acc[b] += ggm

        @pl.when(step == steps - 1)
        def _():
            out_refs[b][...] = out_acc[b].astype(BF)
            in_refs[b][0:tok, :] = in_acc[b].astype(BF)
            total = gg_acc[b]
            high = total.astype(BF)
            in_refs[b][tok : tok + n_exp, :] = jnp.zeros((n_exp, in_acc.shape[2]), BF)
            in_refs[b][tok : tok + n_exp, 0:tok] = high
            in_refs[b][tok : tok + n_exp, tok : 2 * tok] = (total - high.astype(F32)).astype(BF)


def shared_expert(idx_ref, gidx_ref, pay_ref, grad_ref, res_ref, *rest):
    n = idx_ref.shape[0]
    gus = rest[:n]
    dns = rest[n : 2 * n]
    (base_ref, back_ref, gum_ref, gut_ref, dnm_ref, dnt_ref, wgu, wdn, dgu, ddn, sems, sems_out) = rest[2 * n :]
    tok, d = grad_ref.shape
    ff = wdn.shape[0]
    c1 = load_rows(idx_ref, gus, wgu, sems.at[0], gus[0].shape[0])
    c2 = load_halves(idx_ref, dns, wdn, sems.at[1], dns[0].shape[0], dns[0].shape[1])
    act = pay_ref[0:tok, :]
    act_t = act.T
    for copy in c1:
        copy.wait()
    g = dot(act, wgu[:, 0:ff])
    u = dot(act, wgu[:, ff : 2 * ff])
    sig = sigmoid(g)
    h = (g * sig * u).astype(BF)
    for copy in c2:
        copy.wait()
    base_ref[...] = res_ref[...] + dot(h, wdn[...])
    grad = grad_ref[...]
    hg = dot_nt(grad, wdn[...])
    dg = (hg * u * sig * (1.0 + g * (1.0 - sig))).astype(BF)
    du = (hg * g * sig).astype(BF)
    dgu[:, 0:ff] = dot(act_t, dg).astype(BF)
    dgu[:, ff : 2 * ff] = dot(act_t, du).astype(BF)
    ddn[...] = dot_tn(h, grad).astype(BF)
    copies = []
    half = n // 2
    hr = gus[0].shape[0]
    hd, wd = dns[0].shape
    for i in range(n):
        at = gidx_ref[i]
        gu_out = (gum_ref if i < half else gut_ref).at[i % half]
        dn_out = (dnm_ref if i < half else dnt_ref).at[i % half]
        copies.append(
            pltpu.make_async_copy(
                dgu.at[pl.ds(pl.multiple_of(at * hr, 16), hr), :], gu_out, sems_out.at[0, i]
            )
        )
        copies.append(
            pltpu.make_async_copy(
                ddn.at[
                    pl.ds(pl.multiple_of((at // 2) * hd, 16), hd),
                    pl.ds(pl.multiple_of((at % 2) * wd, LANES), wd),
                ],
                dn_out,
                sems_out.at[1, i],
            )
        )
    for copy in copies:
        copy.start()
    back_ref[...] = dot_nt(dg, wgu[:, 0:ff]) + dot_nt(du, wgu[:, ff : 2 * ff])
    for copy in copies:
        copy.wait()


def attn_backward(
    n_exp, idx_ref, gidx_ref, hid_ref, grad_ref, segc_ref, segr_ref, cos_ref, sin_ref, xn_ref, q_ref, k_ref,
    v_ref, att_ref, res_ref, pay_ref, gate_ref, gains_ref, back_ref, rs_ref, own_ref, *rest
):
    n = idx_ref.shape[0]
    pieces = rest[:n]
    ig_ref, mine_ref, theirs_ref, w_ref, dw_ref, dq_ref, dk_ref, dv_ref, sems, sems_out = rest[n:]
    height = pieces[0].shape[0]
    tok, d = hid_ref.shape
    copies = load_rows(idx_ref, pieces, w_ref, sems, height)
    gains = gains_ref[...]
    gain1 = gains[0:1, :]
    gain2 = gains[1:2, :]
    rows = rs_ref[...].astype(F32) + own_ref[...].astype(F32)
    tail = rows[tok : tok + n_exp, :]
    ggt = tail[:, 0:tok] + tail[:, tok : 2 * tok]
    ggt = jnp.concatenate([ggt, jnp.zeros((LANES - n_exp, tok), F32)], axis=0)
    gg = ggt.T
    gate = gate_ref[...]
    picked = gate * (gg - jnp.sum(gate * gg, axis=1, keepdims=True))
    logit_grad = picked.astype(BF)
    act_t = pay_ref[0:tok, :].T
    aux_grad = dot(act_t, logit_grad)
    grad = grad_ref[...].astype(F32)
    res = res_ref[...]
    inv2 = lax.rsqrt(jnp.mean(res * res, axis=1, keepdims=True) + EPS)
    for copy in copies:
        copy.wait()
    moe_in = rows[0:tok, :] + back_ref[...] + dot_nt(logit_grad, w_ref[:, 4 * d : 4 * d + LANES])
    weighted = moe_in * gain2
    gg2 = jnp.sum(moe_in * res * inv2, axis=0, keepdims=True)
    inner = jnp.mean(weighted * res, axis=1, keepdims=True)
    rgrad = grad + inv2 * weighted - res * (inv2 * inv2 * inv2 * inner)
    low = rgrad.astype(BF)
    dw_ref[:, 3 * d : 4 * d] = dot(att_ref[...].T, low).astype(BF)
    allowed = allowed_mask(segc_ref[...], segr_ref[...])
    cos = cos_ref[...]
    sin = sin_ref[...]
    scale = HD ** -0.5
    pair = 2 * HD
    for c in range(0, d, pair):
        agp = dot_nt(low, w_ref[c : c + pair, 3 * d : 4 * d]).astype(BF)
        for o in range(0, pair, HD):
            cols = slice(c + o, c + o + HD)
            q = q_ref[:, cols]
            k = k_ref[:, cols]
            ag = agp[:, o : o + HD]
            probs = head_probs(q, k, allowed)
            dv_ref[:, cols] = dot_tn(probs.astype(BF), ag).astype(BF)
            dp = dot_nt(ag, v_ref[:, cols])
            ds = (probs * (dp - jnp.sum(probs * dp, axis=1, keepdims=True))).astype(BF)
            dq = dot(ds, k) * scale
            dk = dot_tn(ds, q) * scale
            dq_ref[:, cols] = rope_back(dq, cos, sin).astype(BF)
            dk_ref[:, cols] = rope_back(dk, cos, sin).astype(BF)
    back = dot_nt(dq_ref[...], w_ref[:, 0:d])
    back += dot_nt(dk_ref[...], w_ref[:, d : 2 * d])
    back += dot_nt(dv_ref[...], w_ref[:, 2 * d : 3 * d])
    x = hid_ref[...].astype(F32)
    inv = lax.rsqrt(jnp.mean(x * x, axis=1, keepdims=True) + EPS)
    weighted = back * gain1
    gg1 = jnp.sum(back * x * inv, axis=0, keepdims=True)
    inner = jnp.mean(weighted * x, axis=1, keepdims=True)
    ig_ref[...] = rgrad + inv * weighted - x * (inv * inv * inv * inner)
    rowid = lax.broadcasted_iota(jnp.int32, (LANES, d), 0)
    gain_rows = jnp.where(rowid == n_exp, gg1, 0.0) + jnp.where(rowid == n_exp + 1, gg2, 0.0)
    dw_ref[:, 4 * d : 4 * d + LANES] = (aux_grad + gain_rows.T).astype(BF)
    xn_t = xn_ref[...].T
    dw_ref[:, 0:d] = dot(xn_t, dq_ref[...]).astype(BF)
    dw_ref[:, d : 2 * d] = dot(xn_t, dk_ref[...]).astype(BF)
    dw_ref[:, 2 * d : 3 * d] = dot(xn_t, dv_ref[...]).astype(BF)
    half = n // 2
    outs = []
    for i in range(n):
        out = (mine_ref if i < half else theirs_ref).at[i % half]
        start = pl.multiple_of(gidx_ref[i] * height, 16)
        copy = pltpu.make_async_copy(dw_ref.at[pl.ds(start, height), :], out, sems_out.at[i])
        copy.start()
        outs.append(copy)
    for copy in outs:
        copy.wait()


def body(
    nd,
    ne,
    hidden_in,
    out_grad,
    segment_ids,
    routes,
    attn_gain,
    w_query,
    w_key,
    w_value,
    w_out,
    moe_gain,
    w_router,
    shared_gate,
    shared_up,
    shared_down,
    expert_gate,
    expert_up,
    expert_down,
):
    tok, d = hidden_in.shape
    n_exp = w_router.shape[1]
    n_loc = expert_gate.shape[0]
    ff = expert_gate.shape[2]
    top_k = routes.shape[1]
    cap = min(tok, 8 * ((10 * tok * top_k + 56 * n_exp - 1) // (56 * n_exp)))
    extra = tok + n_exp
    hr = d // ne // 2
    hdn = shared_down.shape[0]
    hw = d // 2
    wide = 4 * d + LANES

    me = lax.axis_index("expert")
    core = lax.axis_index("dp") % 2
    perm = ring_perm(nd, ne)
    both = ("dp", "expert")

    def ring(v):
        return lax.ppermute(v, both, perm)

    def swap(v, bit):
        return lax.ppermute(v, "dp", [(i, i ^ bit) for i in range(nd)])

    table = jnp.asarray(ring_order(ne))
    mine_order = lax.dynamic_slice(table, (core, me, 0), (1, 1, ne)).reshape(ne)
    other_order = lax.dynamic_slice(table, (1 - core, me, 0), (1, 1, ne)).reshape(ne)
    idx = jnp.concatenate([mine_order * 2 + core, other_order * 2 + 1 - core])
    gidx = jnp.concatenate(
        [jnp.roll(mine_order, -1) * 2 + core, jnp.roll(other_order, -1) * 2 + 1 - core]
    )
    scal = jnp.stack([me * n_loc + 1 - core, me * n_loc + core, 1 - core, core]).astype(jnp.int32)

    def gather(first, other):
        own = [first]
        for _ in range(ne - 1):
            own.append(ring(own[-1]))
        return own + [other] + [swap(v, 1) for v in own[1:]]

    aux = jnp.concatenate(
        [
            w_router,
            attn_gain[:, None],
            moe_gain[:, None],
            jnp.zeros((w_router.shape[0], LANES - n_exp - 2), BF),
        ],
        axis=1,
    )
    dense = jnp.concatenate([w_query, w_key, w_value, w_out, aux], axis=1)
    dense = dense.reshape(2, hr, wide)
    w1 = gather(
        lax.dynamic_index_in_dim(dense, core, 0, False),
        lax.dynamic_index_in_dim(dense, 1 - core, 0, False),
    )
    gu = jnp.concatenate([shared_gate, shared_up], axis=1).reshape(2, hr, 2 * ff)
    w2 = gather(
        lax.dynamic_index_in_dim(gu, core, 0, False),
        lax.dynamic_index_in_dim(gu, 1 - core, 0, False),
    )
    w3 = gather(
        lax.dynamic_slice(shared_down, (0, core * hw), (hdn, hw)),
        lax.dynamic_slice(shared_down, (0, (1 - core) * hw), (hdn, hw)),
    )
    grads = [out_grad]
    for _ in range(ne - 1):
        grads.append(ring(grads[-1]))

    half = HD // 2
    freq = ROPE_BASE ** (-2.0 * np.arange(half) / HD)
    ang = np.arange(tok)[:, None] * freq[None, :]
    cos = jnp.asarray(np.concatenate([np.cos(ang), np.cos(ang)], 1).astype(np.float32))
    sin = jnp.asarray(np.concatenate([-np.sin(ang), np.sin(ang)], 1).astype(np.float32))
    seg_row = segment_ids
    seg_col = segment_ids.reshape(tok, 1)

    xn, q, k, v, att, res, pay, gate, gains = pl.pallas_call(
        functools.partial(attn_forward, n_exp),
        out_shape=(
            shape((tok, d), BF),
            shape((tok, d), BF),
            shape((tok, d), BF),
            shape((tok, d), BF),
            shape((tok, d), BF),
            shape((tok, d), F32),
            shape((extra, d), BF),
            shape((tok, LANES), F32),
            shape((8, d), F32),
        ),
        in_specs=[whole(SMEM)] + [whole()] * 6 + [anywhere()] * (2 * ne),
        out_specs=[whole()] * 9,
        scratch_shapes=[VMEM((d, wide), BF), pltpu.SemaphoreType.DMA((2 * ne,))],
        compiler_params=params(40),
        cost_estimate=cost(2 * tok * d * d * 4, d * wide * 2),
        name="attn_forward",
    )(idx, hidden_in, seg_col, seg_row, routes, cos, sin, *w1)

    base, sback, gum, gut, dnm, dnt = pl.pallas_call(
        shared_expert,
        out_shape=(
            shape((tok, d), F32),
            shape((tok, d), F32),
            shape((ne, hr, 2 * ff), BF),
            shape((ne, hr, 2 * ff), BF),
            shape((ne, hdn, hw), BF),
            shape((ne, hdn, hw), BF),
        ),
        in_specs=[whole(SMEM)] * 2 + [whole()] * 3 + [anywhere()] * (4 * ne),
        out_specs=[whole()] * 2 + [anywhere()] * 4,
        scratch_shapes=[
            VMEM((d, 2 * ff), BF),
            VMEM((ff, d), BF),
            VMEM((d, 2 * ff), BF),
            VMEM((ff, d), BF),
            pltpu.SemaphoreType.DMA((2, 2 * ne)),
            pltpu.SemaphoreType.DMA((2, 2 * ne)),
        ],
        compiler_params=params(40),
        cost_estimate=cost(2 * tok * d * ff * 9, 4 * d * 3 * ff),
        name="shared_expert",
    )(idx, gidx, pay, out_grad, res, *w2, *w3)

    pays = [pay]
    for _ in range(ne - 1):
        pays.append(ring(pays[-1]))
    nb = 2
    calls = ne // nb
    rows = ne * cap
    saved_shapes = [
        shape((n_loc, rows, d), BF),
        shape((n_loc, rows, d), BF),
        shape((n_loc, rows, ff), BF),
        shape((n_loc, rows, ff), BF),
        shape((n_loc, rows, ff), BF),
    ]
    saved = ()
    in_parts, out_parts = [], []
    for i in range(calls):
        blocks = [i * nb + b for b in range(nb)]

        def at(e, s, i=i):
            return (e, i, 0)

        def zero2(e, s):
            return (0, 0)

        def weight(e, s):
            return (s[n_loc + e], 0, 0)

        outs = pl.pallas_call(
            functools.partial(expert_block, nb, cap, n_exp, len(saved)),
            out_shape=tuple(saved_shapes)
            + (shape((extra, d), BF),) * nb
            + (shape((tok, d), BF),) * nb,
            grid_spec=pltpu.PrefetchScalarGridSpec(
                num_scalar_prefetch=1,
                grid=(n_loc,),
                in_specs=[pl.BlockSpec((extra, d), zero2)] * nb
                + [pl.BlockSpec((tok, d), zero2)] * nb
                + [
                    pl.BlockSpec((1, d, ff), weight),
                    pl.BlockSpec((1, d, ff), weight),
                    pl.BlockSpec((1, ff, d), weight),
                ]
                + [anywhere()] * len(saved),
                out_specs=[
                    pl.BlockSpec((1, nb * cap, d), at),
                    pl.BlockSpec((1, nb * cap, d), at),
                    pl.BlockSpec((1, nb * cap, ff), at),
                    pl.BlockSpec((1, nb * cap, ff), at),
                    pl.BlockSpec((1, nb * cap, ff), at),
                ]
                + [pl.BlockSpec((extra, d), zero2)] * nb
                + [pl.BlockSpec((tok, d), zero2)] * nb,
                scratch_shapes=[
                    VMEM((nb, tok, d), F32),
                    VMEM((nb, tok, d), F32),
                    VMEM((nb, n_exp, tok), F32),
                ],
            ),
            input_output_aliases={1 + 2 * nb + 3 + j: j for j in range(len(saved))},
            compiler_params=params(48),
            cost_estimate=cost(nb * cap * n_loc * d * ff * 12, 3 * n_loc * d * ff * 2),
            name="expert_block",
        )(
            scal,
            *[pays[b] for b in blocks],
            *[grads[b] for b in blocks],
            expert_gate,
            expert_up,
            expert_down,
            *saved,
        )
        saved = outs[:5]
        in_parts += list(outs[5 : 5 + nb])
        out_parts += list(outs[5 + nb :])

    def scatter(parts, others=None):
        total = lambda s: (
            parts[s].astype(F32) + others[s].astype(F32) if others is not None else parts[s].astype(F32)
        )
        acc = total(0).astype(BF)
        for s in range(1, ne):
            got = ring(acc)
            if s == ne - 1:
                return got, s
            acc = (got.astype(F32) + total(s)).astype(BF)

    ordered_in = in_parts[1:] + in_parts[:1]
    ordered_out = out_parts[1:] + out_parts[:1]
    rs_in, _ = scatter(ordered_in)

    input_grad, dmine, dtheirs = pl.pallas_call(
        functools.partial(attn_backward, n_exp),
        out_shape=(
            shape((tok, d), F32),
            shape((ne, hr, wide), BF),
            shape((ne, hr, wide), BF),
        ),
        in_specs=[whole(SMEM)] * 2 + [whole()] * 18 + [anywhere()] * (2 * ne),
        out_specs=[whole()] + [anywhere()] * 2,
        scratch_shapes=[
            VMEM((d, wide), BF),
            VMEM((d, wide), BF),
            VMEM((tok, d), BF),
            VMEM((tok, d), BF),
            VMEM((tok, d), BF),
            pltpu.SemaphoreType.DMA((2 * ne,)),
            pltpu.SemaphoreType.DMA((2 * ne,)),
        ],
        compiler_params=params(56),
        cost_estimate=cost(2 * tok * d * d * 8, 2 * d * wide * 2),
        name="attn_backward",
    )(
        idx, gidx, hidden_in, out_grad, seg_col, seg_row, cos, sin, xn, q, k, v, att, res, pay, gate, gains,
        sback, rs_in, in_parts[0], *w1,
    )

    rs_out, _ = scatter(ordered_out)
    output = base + rs_out.astype(F32) + out_parts[0].astype(F32)

    def over_copies(v):
        bit = 2
        while bit < nd:
            low = v.astype(BF)
            v = low.astype(F32) + swap(low, bit).astype(F32)
            bit *= 2
        return v

    def expert_grads(left, right):
        theirs = dot_tn(left[0], right[0]).astype(BF)
        got = swap(theirs, 1)
        mine = dot_tn(left[1], right[1]) + got.astype(F32)
        mine = over_copies(mine).astype(BF)
        other = swap(mine, 1)
        pick = core == 0
        return jnp.stack(
            [jnp.where(pick, mine, other), jnp.where(pick, other, mine)]
        ).astype(F32)

    xr, gr, gh, dg, du = saved
    down_w = expert_grads(gh, gr)
    gate_w = expert_grads(xr, dg)
    up_w = expert_grads(xr, du)

    def dense_sum(mine, theirs, axis):
        others = swap(theirs, 1)
        got, last = scatter(mine, others)
        total = got.astype(F32) + mine[last].astype(F32) + others[last].astype(F32)
        total = over_copies(total).astype(BF)
        other = swap(total, 1)
        pick = core == 0
        both_halves = [jnp.where(pick, total, other), jnp.where(pick, other, total)]
        return jnp.concatenate(both_halves, axis=axis).astype(F32)

    g_gu = dense_sum(gum, gut, 0)
    g_dn = dense_sum(dnm, dnt, 1)
    g_d = dense_sum(dmine, dtheirs, 0)
    return (
        output,
        input_grad,
        g_d[:, 4 * d + n_exp],
        g_d[:, 0:d],
        g_d[:, d : 2 * d],
        g_d[:, 2 * d : 3 * d],
        g_d[:, 3 * d : 4 * d],
        g_d[:, 4 * d + n_exp + 1],
        g_d[:, 4 * d : 4 * d + n_exp],
        g_gu[:, 0:ff],
        g_gu[:, ff : 2 * ff],
        g_dn,
        gate_w,
        up_w,
        down_w,
    )


def solution(mesh):
    nd = mesh.shape["dp"]
    ne = mesh.shape["expert"]
    tokens = P(("dp", "expert"), None)
    vector = P("expert")
    matrix = P("expert", None)
    cube = P("expert", None, None)
    return jax.shard_map(
        functools.partial(body, nd, ne),
        mesh=mesh,
        in_specs=(tokens,) * 4
        + (vector, matrix, matrix, matrix, matrix, vector)
        + (matrix,) * 4
        + (cube,) * 3,
        out_specs=(tokens, tokens, vector, matrix, matrix, matrix, matrix, vector)
        + (matrix,) * 4
        + (cube,) * 3,
        check_vma=False,
    )
```

```python
import functools

import jax
import jax.numpy as jnp
import numpy as np
from jax import lax
from jax.experimental import pallas as pl
from jax.experimental.pallas import tpu as pltpu
from jax.sharding import PartitionSpec as P

HD = 128
LANES = 128
EPS = 1e-06
ROPE_BASE = 10000.0
MASKED = -1e30
BF = jnp.bfloat16
F32 = jnp.float32
VMEM = pltpu.VMEM
SMEM = pltpu.SMEM
MIB = 1 << 20


def dot(a, b):
    return jnp.dot(a, b, preferred_element_type=F32)


def dot_nt(a, b):
    return lax.dot_general(a, b, (((1,), (1,)), ((), ())), preferred_element_type=F32)


def dot_tn(a, b):
    return lax.dot_general(a, b, (((0,), (0,)), ((), ())), preferred_element_type=F32)


def sigmoid(v):
    return 1.0 / (1.0 + jnp.exp(-v))


def whole(space=VMEM):
    return pl.BlockSpec(memory_space=space)


def anywhere():
    return pl.BlockSpec(memory_space=pl.ANY)


def far():
    return pl.BlockSpec(memory_space=pltpu.HBM)


def params(mib):
    return pltpu.CompilerParams(vmem_limit_bytes=mib * MIB)


def cost(flops, nbytes):
    return pl.CostEstimate(flops=int(flops), bytes_accessed=int(nbytes), transcendentals=0)


def shape(dims, dtype):
    return jax.ShapeDtypeStruct(dims, dtype)


def hbm(dims, dtype):
    return pltpu.HBM(dims, dtype)


def cycle(n):
    return list(range(0, n, 2)) + list(range(1, n, 2))[::-1]


def ring_perm(nd, ne):
    ring = cycle(ne)
    pos = {e: i for i, e in enumerate(ring)}
    pairs = []
    for d in range(nd):
        for e in range(ne):
            step = 1 if d % 2 == 0 else -1
            pairs.append((d * ne + e, d * ne + ring[(pos[e] + step) % ne]))
    return pairs


def ring_order(ne):
    ring = cycle(ne)
    pos = {e: i for i, e in enumerate(ring)}
    table = np.zeros((2, ne, ne), np.int32)
    for c in range(2):
        step = 1 if c == 0 else -1
        for e in range(ne):
            for s in range(ne):
                table[c, e, s] = ring[(pos[e] - step * s) % ne]
    return table


def place_pieces(kinds, spots, aliased, idx_ref, *refs):
    n = len(kinds)
    pieces = refs[:n]
    outs = refs[n + aliased : -1]
    sems = refs[-1]
    copies = []
    for i, kind in enumerate(kinds):
        height, width = pieces[i].shape
        at = idx_ref[spots[i]]
        out = outs[kind[1]]
        if kind[0] == "rows":
            start = pl.multiple_of(at * height, 16)
            dst = out.at[pl.ds(start, height), kind[2] : kind[2] + width]
        else:
            row = pl.multiple_of((at // 2) * height, 16)
            col = pl.multiple_of((at % 2) * width, LANES)
            dst = out.at[pl.ds(row, height), pl.ds(col, width)]
        copies.append(pltpu.make_async_copy(pieces[i], dst, sems.at[i]))
    for copy in copies:
        copy.start()
    for copy in copies:
        copy.wait()


def place_call(kinds, spots, idx, pieces, targets, into):
    n = len(kinds)
    return pl.pallas_call(
        functools.partial(place_pieces, kinds, spots, len(into)),
        out_shape=targets,
        in_specs=[whole(SMEM)] + [whole()] * n + [far()] * len(into),
        out_specs=[far()] * len(targets),
        scratch_shapes=[pltpu.SemaphoreType.DMA((n,))],
        input_output_aliases={1 + n + j: j for j in range(len(into))},
        compiler_params=params(8),
        cost_estimate=cost(0, sum(p.size for p in pieces) * 4),
        name="place_pieces",
    )(idx, *pieces, *into)


def emit_rows(start, aliased, scal_ref, mine_ref, other_ref, *refs):
    outs = refs[aliased : -2]
    buf, sems = refs[-2:]
    height = mine_ref.shape[0]
    width = outs[0].shape[2]
    buf[0] = mine_ref[...].astype(F32)
    buf[1] = other_ref[...].astype(F32)
    copies = []
    for side in range(2):
        expert = scal_ref[3 - side]
        for j, out in enumerate(outs):
            copies.append(
                pltpu.make_async_copy(
                    buf.at[side, :, j * width : (j + 1) * width],
                    out.at[expert, pl.ds(start, height), :],
                    sems.at[side, j],
                )
            )
    for copy in copies:
        copy.start()
    for copy in copies:
        copy.wait()


def emit_call(start, scal, mine, other, targets, into):
    return pl.pallas_call(
        functools.partial(emit_rows, start, len(into)),
        out_shape=targets,
        in_specs=[whole(SMEM)] + [whole()] * 2 + [far()] * len(into),
        out_specs=[far()] * len(targets),
        scratch_shapes=[
            VMEM((2,) + mine.shape, F32),
            pltpu.SemaphoreType.DMA((2, len(targets))),
        ],
        input_output_aliases={3 + j: j for j in range(len(into))},
        compiler_params=params(12),
        cost_estimate=cost(0, mine.size * 12),
        name="emit_rows",
    )(scal, mine, other, *into)


def stored_at(i, tok, d):
    row = d + tok * (i // 4)
    col = d * (i % 4)
    return slice(row, row + tok), slice(col, col + d)


def rope(u, cos, sin):
    return u * cos + pltpu.roll(u, HD // 2, 1) * sin


def rope_back(u, cos, sin):
    return u * cos - pltpu.roll(u, HD // 2, 1) * sin


def allowed_mask(seg_col, seg_row):
    n = seg_row.shape[1]
    rows = lax.broadcasted_iota(jnp.int32, (n, n), 0)
    cols = lax.broadcasted_iota(jnp.int32, (n, n), 1)
    return (seg_col == seg_row) & (cols <= rows)


def head_probs(q, k, allowed):
    s = dot_nt(q, k) * (HD ** -0.5)
    s = jnp.where(allowed, s, MASKED)
    e = jnp.exp(s - jnp.max(s, axis=1, keepdims=True))
    return e / jnp.sum(e, axis=1, keepdims=True)


def attn_forward(n_exp, hid_ref, segc_ref, segr_ref, routes_ref, cos_ref, sin_ref, store_in, *rest):
    store, res_hbm, gate_hbm, pay_ref, gains_ref, w_ref, xn_ref, q_ref, k_ref, v_ref, att_ref = rest[:11]
    res_ref, gate_ref, sems, sems_out = rest[11:]
    tok, d = hid_ref.shape
    wide = w_ref.shape[1]
    saves = [
        pltpu.make_async_copy(ref, store.at[stored_at(i, tok, d)], sems_out.at[i])
        for i, ref in enumerate((xn_ref, q_ref, k_ref, v_ref, att_ref))
    ]
    saves.append(pltpu.make_async_copy(res_ref, res_hbm, sems_out.at[5]))
    saves.append(pltpu.make_async_copy(gate_ref, gate_hbm, sems_out.at[6]))
    spans = [(4 * d, wide)] + [(i * d, (i + 1) * d) for i in range(4)]
    loads = [
        pltpu.make_async_copy(store.at[0:d, lo:hi], w_ref.at[:, lo:hi], sems.at[i])
        for i, (lo, hi) in enumerate(spans)
    ]
    for load in loads:
        load.start()
    x = hid_ref[...].astype(F32)
    inv = lax.rsqrt(jnp.mean(x * x, axis=1, keepdims=True) + EPS)
    cos = cos_ref[...]
    sin = sin_ref[...]
    allowed = allowed_mask(segc_ref[...], segr_ref[...])
    loads[0].wait()
    aux = w_ref[:, 4 * d : 4 * d + LANES]
    turned = aux.astype(F32).T
    gains = turned[n_exp : n_exp + 8, :]
    gains_ref[...] = gains
    xn = (x * inv * gains[0:1, :]).astype(BF)
    xn_ref[...] = xn
    saves[0].start()
    for load in loads[1:4]:
        load.wait()
    pair = 2 * HD
    for c in range(0, d, pair):
        qp = dot(xn, w_ref[:, c : c + pair])
        kp = dot(xn, w_ref[:, d + c : d + c + pair])
        vp = dot(xn, w_ref[:, 2 * d + c : 2 * d + c + pair])
        v_ref[:, c : c + pair] = vp.astype(BF)
        for o in range(0, pair, HD):
            q = rope(qp[:, o : o + HD], cos, sin).astype(BF)
            k = rope(kp[:, o : o + HD], cos, sin).astype(BF)
            q_ref[:, c + o : c + o + HD] = q
            k_ref[:, c + o : c + o + HD] = k
            probs = head_probs(q, k, allowed).astype(BF)
            att_ref[:, c + o : c + o + HD] = dot(probs, vp[:, o : o + HD].astype(BF)).astype(BF)
    for save in saves[1:5]:
        save.start()
    loads[4].wait()
    res = x + dot(att_ref[...], w_ref[:, 3 * d : 4 * d])
    res_ref[...] = res
    saves[5].start()
    inv2 = lax.rsqrt(jnp.mean(res * res, axis=1, keepdims=True) + EPS)
    act = (res * inv2 * gains[1:2, :]).astype(BF)
    logits = dot(act, aux)
    lane = lax.broadcasted_iota(jnp.int32, (tok, LANES), 1)
    routes = routes_ref[...]
    chosen = routes[:, 0:1] == lane
    for j in range(1, routes.shape[1]):
        chosen = chosen | (routes[:, j : j + 1] == lane)
    logits = jnp.where(chosen, logits, MASKED)
    e = jnp.where(chosen, jnp.exp(logits - jnp.max(logits, axis=1, keepdims=True)), 0.0)
    gate = e / jnp.sum(e, axis=1, keepdims=True)
    gate_ref[...] = gate
    saves[6].start()
    gate_t = gate.T[0:n_exp, :]
    high = gate_t.astype(BF)
    pay_ref[0:tok, :] = act
    pay_ref[tok : tok + n_exp, :] = jnp.zeros((n_exp, d), BF)
    pay_ref[tok : tok + n_exp, 0:tok] = high
    pay_ref[tok : tok + n_exp, tok : 2 * tok] = (gate_t - high.astype(F32)).astype(BF)
    for save in saves:
        save.wait()


def expert_block(first, nb, cap, n_exp, aliased, scal_ref, *refs):
    pays = refs[:nb]
    grads = refs[nb : 2 * nb]
    wg_hbm, wu_hbm, wd_hbm = refs[2 * nb : 2 * nb + 3]
    outs = refs[2 * nb + 3 + aliased :]
    saved = outs[:4]
    in_refs = outs[4 : 4 + nb]
    out_refs = outs[4 + nb : 4 + 2 * nb]
    wgu_ref, wd_ref, xr_ref, gr_ref, gh_ref, dgu_ref, sems_w, sems = outs[4 + 2 * nb :]
    n_loc, _, ff2 = wgu_ref.shape
    ff = ff2 // 2
    tok, d = grads[0].shape
    loads = []
    for e in range(n_loc):
        three = (
            pltpu.make_async_copy(wg_hbm.at[scal_ref[n_loc + e]], wgu_ref.at[e, :, 0:ff], sems_w.at[e, 0]),
            pltpu.make_async_copy(wu_hbm.at[scal_ref[n_loc + e]], wgu_ref.at[e, :, ff:ff2], sems_w.at[e, 1]),
            pltpu.make_async_copy(wd_hbm.at[scal_ref[n_loc + e]], wd_ref.at[e], sems_w.at[e, 2]),
        )
        for copy in three:
            copy.start()
        loads.append(three)
    rowid = lax.broadcasted_iota(jnp.int32, (n_exp, tok), 0)
    tri = (
        lax.broadcasted_iota(jnp.int32, (tok, tok), 0)
        < lax.broadcasted_iota(jnp.int32, (tok, tok), 1)
    )
    tri = jnp.where(tri, 1.0, 0.0).astype(BF)
    slots = lax.broadcasted_iota(jnp.int32, (cap, tok), 0)
    gates = []
    for b in range(nb):
        gt = pays[b][tok : tok + n_exp, 0:tok].astype(F32)
        gt = gt + pays[b][tok : tok + n_exp, tok : 2 * tok].astype(F32)
        for e in range(n_loc):
            gates.append(jnp.sum(jnp.where(rowid == scal_ref[e], gt, 0.0), axis=0, keepdims=True))
    used = len(gates)
    stack = jnp.concatenate(gates + [jnp.zeros((-used % 8, tok), F32)] * (used % 8 > 0), axis=0)
    ranks = dot(jnp.where(stack > 0.0, 1.0, 0.0).astype(BF), tri)
    masks, picks, gs = {}, {}, {}
    for b in range(nb):
        for e in range(n_loc):
            at = b * n_loc + e
            g = gates[at]
            slot = jnp.where(g > 0.0, ranks[at : at + 1, :], -1.0).astype(jnp.int32)
            mask = slots == slot
            pick = jnp.where(mask, 1.0, 0.0).astype(BF)
            masks[b, e] = mask
            picks[b, e] = pick
            gs[b, e] = jnp.sum(jnp.where(mask, g, 0.0), axis=1, keepdims=True)
            rows = slice(b * cap, (b + 1) * cap)
            xr_ref[e, rows, :] = dot(pick, pays[b][0:tok, :]).astype(BF)
            gr_ref[e, rows, :] = dot(pick, grads[b][...]).astype(BF)
    copies = []

    def save(j, e, ref):
        copy = pltpu.make_async_copy(
            ref.at[e], saved[j].at[e, pl.ds(first * cap, nb * cap), :], sems.at[j, e]
        )
        copy.start()
        copies.append(copy)

    ggm = [jnp.zeros((n_exp, tok), F32) for _ in range(nb)]
    xis, yos = [], []
    for e in range(n_loc):
        save(0, e, xr_ref)
        save(1, e, gr_ref)
        loads[e][0].wait()
        loads[e][1].wait()
        egu = dot(xr_ref[e], wgu_ref[e])
        loads[e][2].wait()
        hu = dot_nt(gr_ref[e], wd_ref[e])
        gate = jnp.concatenate([gs[b, e] for b in range(nb)], axis=0)
        eg = egu[:, 0:ff]
        eu = egu[:, ff:ff2]
        sig = sigmoid(eg)
        act = eg * sig
        h = act * eu
        gg = jnp.sum(h.astype(BF).astype(F32) * hu, axis=1, keepdims=True)
        gh_ref[e] = (gate * h).astype(BF)
        save(2, e, gh_ref)
        hg = gate * hu
        dgu_ref[e, :, 0:ff] = (hg * eu * (sig + act * (1.0 - sig))).astype(BF)
        dgu_ref[e, :, ff:ff2] = (hg * act).astype(BF)
        save(3, e, dgu_ref)
        yos.append(dot(gh_ref[e], wd_ref[e]).astype(BF))
        xis.append(dot_nt(dgu_ref[e], wgu_ref[e]).astype(BF))
        for b in range(nb):
            row = jnp.sum(jnp.where(masks[b, e], gg[b * cap : (b + 1) * cap], 0.0), axis=0, keepdims=True)
            ggm[b] = ggm[b] + jnp.where(rowid == scal_ref[e], row, 0.0)
    for b in range(nb):
        rows = slice(b * cap, (b + 1) * cap)
        pick = jnp.concatenate([picks[b, e] for e in range(n_loc)], axis=0)
        in_refs[b][0:tok, :] = dot_tn(pick, jnp.concatenate([v[rows] for v in xis], axis=0)).astype(BF)
        out_refs[b][...] = dot_tn(pick, jnp.concatenate([v[rows] for v in yos], axis=0)).astype(BF)
        high = ggm[b].astype(BF)
        in_refs[b][tok : tok + n_exp, :] = jnp.zeros((n_exp, d), BF)
        in_refs[b][tok : tok + n_exp, 0:tok] = high
        in_refs[b][tok : tok + n_exp, tok : 2 * tok] = (ggm[b] - high.astype(F32)).astype(BF)
    for copy in copies:
        copy.wait()


def expert_call(first, nb, cap, n_exp, scal, pays, grads, weights, saved):
    extra, d = pays[0].shape
    tok = grads[0].shape[0]
    n_loc, _, ff = weights[0].shape
    rows = cap * (extra - tok) // n_loc
    saved_shapes = (
        hbm((n_loc, rows, d), BF),
        hbm((n_loc, rows, d), BF),
        hbm((n_loc, rows, ff), BF),
        hbm((n_loc, rows, 2 * ff), BF),
    )
    outs = pl.pallas_call(
        functools.partial(expert_block, first, nb, cap, n_exp, len(saved)),
        out_shape=saved_shapes + (shape((extra, d), BF),) * nb + (shape((tok, d), BF),) * nb,
        in_specs=[whole(SMEM)] + [whole()] * (2 * nb) + [far()] * (3 + len(saved)),
        out_specs=[far()] * 4 + [whole()] * (2 * nb),
        scratch_shapes=[
            VMEM((n_loc, d, 2 * ff), BF),
            VMEM((n_loc, ff, d), BF),
            VMEM((n_loc, nb * cap, d), BF),
            VMEM((n_loc, nb * cap, d), BF),
            VMEM((n_loc, nb * cap, ff), BF),
            VMEM((n_loc, nb * cap, 2 * ff), BF),
            pltpu.SemaphoreType.DMA((n_loc, 3)),
            pltpu.SemaphoreType.DMA((4, n_loc)),
        ],
        input_output_aliases={1 + 2 * nb + 3 + j: j for j in range(len(saved))},
        compiler_params=params(40),
        cost_estimate=cost(nb * cap * n_loc * d * ff * 12, 3 * n_loc * d * ff * 2),
        name="expert_block",
    )(scal, *pays, *grads, *weights, *saved)
    return outs[:4], list(outs[4 : 4 + nb]), list(outs[4 + nb :])


def shared_expert(gidx_ref, pay_ref, grad_ref, res_ref, gu_hbm, dn_hbm, *rest):
    n = gidx_ref.shape[0]
    (base_ref, back_ref, gum_ref, gut_ref, dnm_ref, dnt_ref, wgu, wdn, dgu, ddn, sems, sems_out) = rest
    tok, d = grad_ref.shape
    ff = wdn.shape[0]
    c1 = pltpu.make_async_copy(gu_hbm, wgu, sems.at[0])
    c2 = pltpu.make_async_copy(dn_hbm, wdn, sems.at[1])
    c1.start()
    c2.start()
    act = pay_ref[0:tok, :]
    act_t = act.T
    c1.wait()
    g = dot(act, wgu[:, 0:ff])
    u = dot(act, wgu[:, ff : 2 * ff])
    sig = sigmoid(g)
    h = (g * sig * u).astype(BF)
    c2.wait()
    base_ref[...] = res_ref[...] + dot(h, wdn[...])
    grad = grad_ref[...]
    hg = dot_nt(grad, wdn[...])
    dg = (hg * u * sig * (1.0 + g * (1.0 - sig))).astype(BF)
    du = (hg * g * sig).astype(BF)
    dgu[:, 0:ff] = dot(act_t, dg).astype(BF)
    dgu[:, ff : 2 * ff] = dot(act_t, du).astype(BF)
    ddn[...] = dot_tn(h, grad).astype(BF)
    copies = []
    half = n // 2
    _, hr, _ = gum_ref.shape
    _, hd, wd = dnm_ref.shape
    for i in range(n):
        at = gidx_ref[i]
        gu_out = (gum_ref if i < half else gut_ref).at[i % half]
        dn_out = (dnm_ref if i < half else dnt_ref).at[i % half]
        copies.append(
            pltpu.make_async_copy(
                dgu.at[pl.ds(pl.multiple_of(at * hr, 16), hr), :], gu_out, sems_out.at[0, i]
            )
        )
        copies.append(
            pltpu.make_async_copy(
                ddn.at[
                    pl.ds(pl.multiple_of((at // 2) * hd, 16), hd),
                    pl.ds(pl.multiple_of((at % 2) * wd, LANES), wd),
                ],
                dn_out,
                sems_out.at[1, i],
            )
        )
    for copy in copies:
        copy.start()
    back_ref[...] = dot_nt(dg, wgu[:, 0:ff]) + dot_nt(du, wgu[:, ff : 2 * ff])
    for copy in copies:
        copy.wait()


def attn_backward(
    n_exp, gidx_ref, hid_ref, grad_ref, segc_ref, segr_ref, cos_ref, sin_ref, gate_ref, gains_ref,
    back_ref, rs_ref, own_ref, *rest
):
    n = gidx_ref.shape[0]
    store, pay_hbm, res_hbm = rest[:3]
    ig_ref, ml_ref, mr_ref, tl_ref, tr_ref, w_ref, dw_ref, dq_ref, dk_ref, dv_ref = rest[3:13]
    xn_ref, q_ref, k_ref, v_ref, att_ref, pay_ref, res_ref, sems_in, sems_out = rest[13:]
    _, height, split = ml_ref.shape
    tok, d = hid_ref.shape
    sources = [store.at[stored_at(i, tok, d)] for i in range(5)] + [pay_hbm, res_hbm]
    sources.append(store.at[0:d, :])
    loads = [
        pltpu.make_async_copy(src, ref, sems_in.at[i])
        for i, (src, ref) in enumerate(
            zip(sources, (xn_ref, q_ref, k_ref, v_ref, att_ref, pay_ref, res_ref, w_ref))
        )
    ]
    for i in (5, 6, 7, 4, 1, 2, 3, 0):
        loads[i].start()
    loads[5].wait()
    gains = gains_ref[...]
    gain1 = gains[0:1, :]
    gain2 = gains[1:2, :]
    rows = rs_ref[...].astype(F32) + own_ref[...].astype(F32)
    tail = rows[tok : tok + n_exp, :]
    ggt = tail[:, 0:tok] + tail[:, tok : 2 * tok]
    ggt = jnp.concatenate([ggt, jnp.zeros((LANES - n_exp, tok), F32)], axis=0)
    gg = ggt.T
    gate = gate_ref[...]
    picked = gate * (gg - jnp.sum(gate * gg, axis=1, keepdims=True))
    logit_grad = picked.astype(BF)
    act_t = pay_ref[0:tok, :].T
    aux_grad = dot(act_t, logit_grad)
    grad = grad_ref[...].astype(F32)
    loads[6].wait()
    res = res_ref[...]
    inv2 = lax.rsqrt(jnp.mean(res * res, axis=1, keepdims=True) + EPS)
    loads[7].wait()
    moe_in = rows[0:tok, :] + back_ref[...] + dot_nt(logit_grad, w_ref[:, 4 * d : 4 * d + LANES])
    weighted = moe_in * gain2
    gg2 = jnp.sum(moe_in * res * inv2, axis=0, keepdims=True)
    inner = jnp.mean(weighted * res, axis=1, keepdims=True)
    rgrad = grad + inv2 * weighted - res * (inv2 * inv2 * inv2 * inner)
    low = rgrad.astype(BF)
    for i in (4, 1, 2, 3, 0):
        loads[i].wait()
    dw_ref[:, 3 * d : 4 * d] = dot(att_ref[...].T, low).astype(BF)
    allowed = allowed_mask(segc_ref[...], segr_ref[...])
    cos = cos_ref[...]
    sin = sin_ref[...]
    scale = HD ** -0.5
    pair = 2 * HD
    for c in range(0, d, pair):
        agp = dot_nt(low, w_ref[c : c + pair, 3 * d : 4 * d]).astype(BF)
        for o in range(0, pair, HD):
            cols = slice(c + o, c + o + HD)
            q = q_ref[:, cols]
            k = k_ref[:, cols]
            ag = agp[:, o : o + HD]
            probs = head_probs(q, k, allowed)
            dv_ref[:, cols] = dot_tn(probs.astype(BF), ag).astype(BF)
            dp = dot_nt(ag, v_ref[:, cols])
            ds = (probs * (dp - jnp.sum(probs * dp, axis=1, keepdims=True))).astype(BF)
            dq = dot(ds, k) * scale
            dk = dot_tn(ds, q) * scale
            dq_ref[:, cols] = rope_back(dq, cos, sin).astype(BF)
            dk_ref[:, cols] = rope_back(dk, cos, sin).astype(BF)
    back = dot_nt(dq_ref[...], w_ref[:, 0:d])
    back += dot_nt(dk_ref[...], w_ref[:, d : 2 * d])
    back += dot_nt(dv_ref[...], w_ref[:, 2 * d : 3 * d])
    x = hid_ref[...].astype(F32)
    inv = lax.rsqrt(jnp.mean(x * x, axis=1, keepdims=True) + EPS)
    weighted = back * gain1
    gg1 = jnp.sum(back * x * inv, axis=0, keepdims=True)
    inner = jnp.mean(weighted * x, axis=1, keepdims=True)
    ig_ref[...] = rgrad + inv * weighted - x * (inv * inv * inv * inner)
    rowid = lax.broadcasted_iota(jnp.int32, (LANES, d), 0)
    gain_rows = jnp.where(rowid == n_exp, gg1, 0.0) + jnp.where(rowid == n_exp + 1, gg2, 0.0)
    dw_ref[:, 4 * d : 4 * d + LANES] = (aux_grad + gain_rows.T).astype(BF)
    xn_t = xn_ref[...].T
    dw_ref[:, 0:d] = dot(xn_t, dq_ref[...]).astype(BF)
    dw_ref[:, d : 2 * d] = dot(xn_t, dk_ref[...]).astype(BF)
    dw_ref[:, 2 * d : 3 * d] = dot(xn_t, dv_ref[...]).astype(BF)
    half = n // 2
    outs = []
    for i in range(n):
        start = pl.multiple_of(gidx_ref[i] * height, 16)
        for j, (mine_ref, theirs_ref) in enumerate(((ml_ref, tl_ref), (mr_ref, tr_ref))):
            out = (mine_ref if i < half else theirs_ref).at[i % half]
            cols = slice(0, split) if j == 0 else slice(split, dw_ref.shape[1])
            copy = pltpu.make_async_copy(dw_ref.at[pl.ds(start, height), cols], out, sems_out.at[j, i])
            copy.start()
            outs.append(copy)
    for copy in outs:
        copy.wait()


def body(
    nd,
    ne,
    hidden_in,
    out_grad,
    segment_ids,
    routes,
    attn_gain,
    w_query,
    w_key,
    w_value,
    w_out,
    moe_gain,
    w_router,
    shared_gate,
    shared_up,
    shared_down,
    expert_gate,
    expert_up,
    expert_down,
):
    tok, d = hidden_in.shape
    n_exp = w_router.shape[1]
    n_loc = expert_gate.shape[0]
    ff = expert_gate.shape[2]
    top_k = routes.shape[1]
    cap = min(tok, 8 * ((10 * tok * top_k + 56 * n_exp - 1) // (56 * n_exp)))
    extra = tok + n_exp
    hr = d // ne // 2
    hdn = shared_down.shape[0]
    hw = d // 2
    wide = 4 * d + LANES

    me = lax.axis_index("expert")
    core = lax.axis_index("dp") % 2
    perm = ring_perm(nd, ne)
    both = ("dp", "expert")

    def ring(v):
        return lax.ppermute(v, both, perm)

    def after(v, *others):
        return lax.optimization_barrier((v,) + others)[0]

    def swap(v, bit):
        return lax.ppermute(v, "dp", [(i, i ^ bit) for i in range(nd)])

    table = jnp.asarray(ring_order(ne))
    mine_order = lax.dynamic_slice(table, (core, me, 0), (1, 1, ne)).reshape(ne)
    other_order = lax.dynamic_slice(table, (1 - core, me, 0), (1, 1, ne)).reshape(ne)
    idx = jnp.concatenate([mine_order * 2 + core, other_order * 2 + 1 - core])
    gidx = jnp.concatenate(
        [jnp.roll(mine_order, -1) * 2 + core, jnp.roll(other_order, -1) * 2 + 1 - core]
    )
    scal = jnp.stack([me * n_loc + 1 - core, me * n_loc + core, 1 - core, core]).astype(jnp.int32)

    def fence(*vs):
        return list(lax.optimization_barrier(tuple(vs)))

    def halves(v):
        v = v.reshape(2, v.shape[0] // 2, v.shape[1])
        return (
            lax.dynamic_index_in_dim(v, core, 0, False),
            lax.dynamic_index_in_dim(v, 1 - core, 0, False),
        )

    def sides(v):
        return (
            lax.dynamic_slice(v, (0, core * hw), (hdn, hw)),
            lax.dynamic_slice(v, (0, (1 - core) * hw), (hdn, hw)),
        )

    split = 2 * d
    aux = jnp.concatenate(
        [
            w_router,
            attn_gain[:, None],
            moe_gain[:, None],
            jnp.zeros((w_router.shape[0], LANES - n_exp - 2), BF),
        ],
        axis=1,
    )
    left, left_other = halves(jnp.concatenate([w_query, w_key], axis=1))
    right, right_other = halves(jnp.concatenate([w_value, w_out, aux], axis=1))
    store_shape = (hbm((d + 2 * tok, wide), BF),)
    kinds = [("rows", 0, 0), ("rows", 0, split)] * 2
    store = place_call(
        kinds, [0, 0, ne, ne], idx, [left, right, left_other, right_other], store_shape, ()
    )
    for i in range(1, ne):
        left = ring(left)
        right = ring(right)
        placed = place_call(
            kinds, [i, i, ne + i, ne + i], idx, [left, right, swap(left, 1), swap(right, 1)], store_shape, store
        )
        if i + 1 < ne:
            left = fence(left, *store)[0]
            right = fence(right, *store)[0]
        store = placed

    half = HD // 2
    freq = ROPE_BASE ** (-2.0 * np.arange(half) / HD)
    ang = np.arange(tok)[:, None] * freq[None, :]
    cos = jnp.asarray(np.concatenate([np.cos(ang), np.cos(ang)], 1).astype(np.float32))
    sin = jnp.asarray(np.concatenate([-np.sin(ang), np.sin(ang)], 1).astype(np.float32))
    seg_row = segment_ids
    seg_col = segment_ids.reshape(tok, 1)

    gu_own, gu_other = halves(jnp.concatenate([shared_gate, shared_up], axis=1))
    dn_own, dn_other = sides(shared_down)
    g0, gu_own, dn_own, left, right = fence(out_grad, gu_own, dn_own, left, right)
    grads = [g0, ring(g0)]
    gus = [gu_own, ring(gu_own)]
    dns = [dn_own, ring(dn_own)]
    store, res, gate, pay, gains = pl.pallas_call(
        functools.partial(attn_forward, n_exp),
        out_shape=store_shape
        + (
            hbm((tok, d), F32),
            hbm((tok, LANES), F32),
            shape((extra, d), BF),
            shape((8, d), F32),
        ),
        in_specs=[whole()] * 6 + [far()],
        out_specs=[far()] * 3 + [whole()] * 2,
        scratch_shapes=[VMEM((d, wide), BF)]
        + [VMEM((tok, d), BF)] * 5
        + [
            VMEM((tok, d), F32),
            VMEM((tok, LANES), F32),
            pltpu.SemaphoreType.DMA((5,)),
            pltpu.SemaphoreType.DMA((7,)),
        ],
        input_output_aliases={6: 0},
        compiler_params=params(36),
        cost_estimate=cost(2 * tok * d * d * 4, d * wide * 2),
        name="attn_forward",
    )(hidden_in, seg_col, seg_row, routes, cos, sin, *store)
    pay, grads[1], gus[1], dns[1] = fence(pay, grads[1], gus[1], dns[1])

    pays = [pay]
    saved = ()
    in_parts, out_parts = [], []
    for i in range(ne):
        if i + 1 < ne:
            pays.append(ring(pays[i]))
        if i + 2 < ne:
            grads.append(ring(grads[i + 1]))
        saved, ins, outs = expert_call(
            i, 1, cap, n_exp, scal, pays[i : i + 1], grads[i : i + 1],
            (expert_gate, expert_up, expert_down), saved,
        )
        moved = ([pays[-1]] if i + 1 < ne else []) + ([grads[-1]] if i + 2 < ne else [])
        moved = fence(ins[0], outs[0], *moved)
        in_parts.append(moved[0])
        out_parts.append(moved[1])
        if i + 1 < ne:
            pays[-1] = moved[2]
        if i + 2 < ne:
            grads[-1] = moved[3]

    def start_flow(parts):
        return {"parts": parts, "at": 0, "acc": parts(0).astype(BF)}

    def advance(flow, got):
        flow["at"] += 1
        if flow["at"] == ne - 1:
            flow["got"] = got
        else:
            flow["acc"] = (got.astype(F32) + flow["parts"](flow["at"])).astype(BF)

    def slot(flows, chunks=(), compute=None):
        moved = [ring(f["acc"]) for f in flows] + send_over(chunks)
        done = list(compute()) if compute is not None else []
        moved = joint(moved + done, emit_landed())
        for f, got in zip(flows, moved):
            advance(f, got)
        count = len(flows) + len(chunks)
        finish(chunks, moved[len(flows) : count])
        return moved[count:]

    def token_parts(parts):
        return lambda i: parts[(i + 1) % ne].astype(F32)

    def over_copies(v):
        bit = 2
        while bit < nd:
            low = v.astype(BF)
            v = low.astype(F32) + swap(low, bit).astype(F32)
            bit *= 2
        return v

    shared_shapes = (hbm((d, 2 * ff), BF), hbm((ff, d), BF))
    pair_kinds = [("rows", 0, 0), ("halves", 1)] * 2
    held = {}
    held["shared"] = place_call(
        pair_kinds, [0, 0, ne, ne], idx, [gus[0], dns[0], gu_other, dn_other], shared_shapes, ()
    )

    def shared_pieces(i, into):
        return place_call(
            pair_kinds,
            [i, i, ne + i, ne + i],
            idx,
            [gus[i], dns[i], swap(gus[i], 1), swap(dns[i], 1)],
            shared_shapes,
            into,
        )

    xr, gr, gh, dgu = saved
    flow_in = start_flow(token_parts(in_parts))
    down_shapes = (hbm((n_loc, ff, d), F32),)
    gu_shapes = (hbm((n_loc, d, ff), F32),) * 2
    n_down, n_gu = 4, 8
    crossing = []
    finished = {"down": (), "gu": ()}

    def send_over(chunks):
        return [swap(low, 2) for _, _, low in chunks] if nd > 2 else [low * 0 for _, _, low in chunks]

    landed = []

    def finish(chunks, got):
        landed.extend(zip(chunks, got))

    def emit_landed():
        names = []
        for (name, start, low), more in landed:
            total = low.astype(F32) + more.astype(F32)
            bit = 4
            while bit < nd:
                low = total.astype(BF)
                total = low.astype(F32) + swap(low, bit).astype(F32)
                bit *= 2
            mine = total.astype(BF)
            finished[name] = emit_call(
                start, scal, mine, swap(mine, 1), down_shapes if name == "down" else gu_shapes, finished[name]
            )
            names.append(name)
        landed.clear()
        return names

    def joint(moved, names):
        names = sorted(set(names))
        extra_values = [v for name in names for v in finished[name]]
        out = fence(*moved, *extra_values)
        at = len(moved)
        for name in names:
            count = len(finished[name])
            finished[name] = tuple(out[at : at + count])
            at += count
        return out[: len(moved)]

    def take(count):
        chunks = crossing[:count]
        del crossing[:count]
        return chunks

    def queue(name, low, count):
        height = low.shape[0] // count
        for j in range(count):
            crossing.append((name, j * height, lax.slice_in_dim(low, j * height, (j + 1) * height)))

    def back_slot(i, chunks=(), compute=None):
        held["shared"] = shared_pieces(i, held["shared"])
        sends = [gus[-1], dns[-1]] if len(gus) < ne else []
        moved = [ring(flow_in["acc"])] + [ring(v) for v in sends] + send_over(chunks)
        done = list(compute()) if compute is not None else []
        moved = joint(moved + done + list(held["shared"]), emit_landed())
        held["shared"] = tuple(moved[-2:])
        moved = moved[:-2]
        advance(flow_in, moved[0])
        if sends:
            gus.append(moved[1])
            dns.append(moved[2])
        at = 1 + len(sends)
        finish(chunks, moved[at : at + len(chunks)])
        return moved[at + len(chunks) :]

    (down_t,) = back_slot(1, (), lambda: [dot_tn(gh[0], gr[0]).astype(BF)])
    down_got = swap(down_t, 1)
    (down_m,) = back_slot(2, (), lambda: [dot_tn(gh[1], gr[1]).astype(BF)])
    queue("down", (down_m.astype(F32) + down_got.astype(F32)).astype(BF), n_down)
    (gu_t,) = back_slot(3, take(1), lambda: [dot_tn(xr[0], dgu[0]).astype(BF)])
    gu_got = swap(gu_t, 1)
    (gu_m,) = back_slot(4, take(1), lambda: [dot_tn(xr[1], dgu[1]).astype(BF)])
    queue("gu", (gu_m.astype(F32) + gu_got.astype(F32)).astype(BF), n_gu)
    for i in range(5, ne):
        back_slot(i, take(1))
    rs_in = flow_in["got"]

    base, sback, gum, gut, dnm, dnt = pl.pallas_call(
        shared_expert,
        out_shape=(
            shape((tok, d), F32),
            shape((tok, d), F32),
            hbm((ne, hr, 2 * ff), BF),
            hbm((ne, hr, 2 * ff), BF),
            hbm((ne, hdn, hw), BF),
            hbm((ne, hdn, hw), BF),
        ),
        in_specs=[whole(SMEM)] + [whole()] * 3 + [far()] * 2,
        out_specs=[whole()] * 2 + [far()] * 4,
        scratch_shapes=[
            VMEM((d, 2 * ff), BF),
            VMEM((ff, d), BF),
            VMEM((d, 2 * ff), BF),
            VMEM((ff, d), BF),
            pltpu.SemaphoreType.DMA((2,)),
            pltpu.SemaphoreType.DMA((2, 2 * ne)),
        ],
        compiler_params=params(32),
        cost_estimate=cost(2 * tok * d * ff * 9, 4 * d * 3 * ff),
        name="shared_expert",
    )(gidx, pay, out_grad, res, *held["shared"])

    def dense_parts(mine, theirs):
        others = swap(theirs, 1)
        return lambda i: mine[i].astype(F32) + others[i].astype(F32)

    flow_out = start_flow(token_parts(out_parts))
    flow_gu = start_flow(dense_parts(gum, gut))
    flow_dn = start_flow(dense_parts(dnm, dnt))
    flows = [flow_out, flow_gu, flow_dn]
    rs_in, *firsts = fence(rs_in, *[f["acc"] for f in flows])
    for f, acc in zip(flows, firsts):
        f["acc"] = acc

    def backward():
        return pl.pallas_call(
            functools.partial(attn_backward, n_exp),
            out_shape=(
                shape((tok, d), F32),
                shape((ne, hr, split), BF),
                shape((ne, hr, wide - split), BF),
                shape((ne, hr, split), BF),
                shape((ne, hr, wide - split), BF),
            ),
            in_specs=[whole(SMEM)] + [whole()] * 11 + [far()] * 3,
            out_specs=[whole()] + [far()] * 4,
            scratch_shapes=[
                VMEM((d, wide), BF),
                VMEM((d, wide), BF),
            ]
            + [VMEM((tok, d), BF)] * 8
            + [
                VMEM((extra, d), BF),
                VMEM((tok, d), F32),
                pltpu.SemaphoreType.DMA((8,)),
                pltpu.SemaphoreType.DMA((2, 2 * ne)),
            ],
            compiler_params=params(56),
            cost_estimate=cost(2 * tok * d * d * 8, 2 * d * wide * 2),
            name="attn_backward",
        )(
            gidx, hidden_in, out_grad, seg_col, seg_row, cos, sin, gate, gains, sback, rs_in, in_parts[0],
            store, pay, res,
        )

    input_grad, dml, dmr, dtl, dtr = slot(flows, take(2), backward)

    flow_a = start_flow(dense_parts(dml, dtl))
    flow_b = start_flow(dense_parts(dmr, dtr))
    flows = [flow_a, flow_b] + flows
    for _ in range(ne - 1):
        slot([f for f in flows if f["at"] < ne - 1], take(1))
    for chunk in list(crossing):
        finish([chunk], send_over([chunk]))
    emit_landed()

    output = base + flow_out["got"].astype(F32) + out_parts[0].astype(F32)

    def ring_total(flow):
        return flow["got"].astype(F32) + flow["parts"](ne - 1)

    def dense_join(flow, axis):
        total = over_copies(ring_total(flow)).astype(BF)
        other = swap(total, 1)
        pick = core == 0
        both_halves = [jnp.where(pick, total, other), jnp.where(pick, other, total)]
        return jnp.concatenate(both_halves, axis=axis).astype(F32)

    g_a = dense_join(flow_a, 0)
    g_b = dense_join(flow_b, 0)
    g_gu = dense_join(flow_gu, 0)
    g_dn = dense_join(flow_dn, 1)
    (down_w,) = finished["down"]
    gate_w, up_w = finished["gu"]
    return (
        output,
        input_grad,
        g_b[:, 2 * d + n_exp],
        g_a[:, 0:d],
        g_a[:, d : 2 * d],
        g_b[:, 0:d],
        g_b[:, d : 2 * d],
        g_b[:, 2 * d + n_exp + 1],
        g_b[:, 2 * d : 2 * d + n_exp],
        g_gu[:, 0:ff],
        g_gu[:, ff : 2 * ff],
        g_dn,
        gate_w,
        up_w,
        down_w,
    )


def solution(mesh):
    nd = mesh.shape["dp"]
    ne = mesh.shape["expert"]
    tokens = P(("dp", "expert"), None)
    vector = P("expert")
    matrix = P("expert", None)
    cube = P("expert", None, None)
    return jax.shard_map(
        functools.partial(body, nd, ne),
        mesh=mesh,
        in_specs=(tokens,) * 4
        + (vector, matrix, matrix, matrix, matrix, vector)
        + (matrix,) * 4
        + (cube,) * 3,
        out_specs=(tokens, tokens, vector, matrix, matrix, matrix, matrix, vector)
        + (matrix,) * 4
        + (cube,) * 3,
        check_vma=False,
    )
```

```python
import functools

import jax
import jax.numpy as jnp
import numpy as np
from jax import lax
from jax.experimental import pallas as pl
from jax.experimental.pallas import tpu as pltpu
from jax.sharding import PartitionSpec as P

HD = 128
LANES = 128
EPS = 1e-06
ROPE_BASE = 10000.0
MASKED = -1e30
BF = jnp.bfloat16
F32 = jnp.float32
VMEM = pltpu.VMEM
SMEM = pltpu.SMEM
MIB = 1 << 20


def dot(a, b):
    return jnp.dot(a, b, preferred_element_type=F32)


def dot_nt(a, b):
    return lax.dot_general(a, b, (((1,), (1,)), ((), ())), preferred_element_type=F32)


def dot_tn(a, b):
    return lax.dot_general(a, b, (((0,), (0,)), ((), ())), preferred_element_type=F32)


def sigmoid(v):
    return 1.0 / (1.0 + jnp.exp(-v))


def whole(space=VMEM):
    return pl.BlockSpec(memory_space=space)


def anywhere():
    return pl.BlockSpec(memory_space=pl.ANY)


def far():
    return pl.BlockSpec(memory_space=pltpu.HBM)


def params(mib):
    return pltpu.CompilerParams(vmem_limit_bytes=mib * MIB)


def cost(flops, nbytes):
    return pl.CostEstimate(flops=int(flops), bytes_accessed=int(nbytes), transcendentals=0)


def shape(dims, dtype):
    return jax.ShapeDtypeStruct(dims, dtype)


def hbm(dims, dtype):
    return pltpu.HBM(dims, dtype)


def cycle(n):
    return list(range(0, n, 2)) + list(range(1, n, 2))[::-1]


def ring_perm(nd, ne):
    ring = cycle(ne)
    pos = {e: i for i, e in enumerate(ring)}
    pairs = []
    for d in range(nd):
        for e in range(ne):
            step = 1 if d % 2 == 0 else -1
            pairs.append((d * ne + e, d * ne + ring[(pos[e] + step) % ne]))
    return pairs


def ring_order(ne):
    ring = cycle(ne)
    pos = {e: i for i, e in enumerate(ring)}
    table = np.zeros((2, ne, ne), np.int32)
    for c in range(2):
        step = 1 if c == 0 else -1
        for e in range(ne):
            for s in range(ne):
                table[c, e, s] = ring[(pos[e] - step * s) % ne]
    return table


def place_pieces(kinds, spots, aliased, idx_ref, *refs):
    n = len(kinds)
    pieces = refs[:n]
    outs = refs[n + aliased : -1]
    sems = refs[-1]
    copies = []
    for i, (target, col) in enumerate(kinds):
        height, width = pieces[i].shape
        start = pl.multiple_of(idx_ref[spots[i]] * height, 16)
        dst = outs[target].at[pl.ds(start, height), col : col + width]
        copies.append(pltpu.make_async_copy(pieces[i], dst, sems.at[i]))
    for copy in copies:
        copy.start()
    for copy in copies:
        copy.wait()


def place_call(kinds, spots, idx, pieces, targets, into):
    n = len(kinds)
    return pl.pallas_call(
        functools.partial(place_pieces, kinds, spots, len(into)),
        out_shape=targets,
        in_specs=[whole(SMEM)] + [whole()] * n + [far()] * len(into),
        out_specs=[far()] * len(targets),
        scratch_shapes=[pltpu.SemaphoreType.DMA((n,))],
        input_output_aliases={1 + n + j: j for j in range(len(into))},
        compiler_params=params(8),
        cost_estimate=cost(0, sum(p.size for p in pieces) * 4),
        name="place_pieces",
    )(idx, *pieces, *into)


def emit_rows(start, aliased, scal_ref, mine_ref, other_ref, *refs):
    outs = refs[aliased : -2]
    buf, sems = refs[-2:]
    height = mine_ref.shape[0]
    width = outs[0].shape[2]
    buf[0] = mine_ref[...].astype(F32)
    buf[1] = other_ref[...].astype(F32)
    copies = []
    for side in range(2):
        expert = scal_ref[3 - side]
        for j, out in enumerate(outs):
            copies.append(
                pltpu.make_async_copy(
                    buf.at[side, :, j * width : (j + 1) * width],
                    out.at[expert, pl.ds(start, height), :],
                    sems.at[side, j],
                )
            )
    for copy in copies:
        copy.start()
    for copy in copies:
        copy.wait()


def emit_call(start, scal, mine, other, targets, into):
    return pl.pallas_call(
        functools.partial(emit_rows, start, len(into)),
        out_shape=targets,
        in_specs=[whole(SMEM)] + [whole()] * 2 + [far()] * len(into),
        out_specs=[far()] * len(targets),
        scratch_shapes=[
            VMEM((2,) + mine.shape, F32),
            pltpu.SemaphoreType.DMA((2, len(targets))),
        ],
        input_output_aliases={3 + j: j for j in range(len(into))},
        compiler_params=params(12),
        cost_estimate=cost(0, mine.size * 12),
        name="emit_rows",
    )(scal, mine, other, *into)


def stored_at(i, tok, d):
    row = d + tok * (i // 4)
    col = d * (i % 4)
    return slice(row, row + tok), slice(col, col + d)


def rope(u, cos, sin):
    return u * cos + pltpu.roll(u, HD // 2, 1) * sin


def rope_back(u, cos, sin):
    return u * cos - pltpu.roll(u, HD // 2, 1) * sin


def allowed_mask(seg_col, seg_row):
    n = seg_row.shape[1]
    rows = lax.broadcasted_iota(jnp.int32, (n, n), 0)
    cols = lax.broadcasted_iota(jnp.int32, (n, n), 1)
    return (seg_col == seg_row) & (cols <= rows)


def head_probs(q, k, allowed):
    s = dot_nt(q, k) * (HD ** -0.5)
    s = jnp.where(allowed, s, MASKED)
    e = jnp.exp(s - jnp.max(s, axis=1, keepdims=True))
    return e / jnp.sum(e, axis=1, keepdims=True)


def attn_forward(n_exp, hid_ref, segc_ref, segr_ref, routes_ref, cos_ref, sin_ref, store_in, *rest):
    store, res_hbm, gate_hbm, pay_ref, gains_ref, w_ref, xn_ref, q_ref, k_ref, v_ref, att_ref = rest[:11]
    res_ref, gate_ref, sems, sems_out = rest[11:]
    tok, d = hid_ref.shape
    wide = w_ref.shape[1]
    saves = [
        pltpu.make_async_copy(ref, store.at[stored_at(i, tok, d)], sems_out.at[i])
        for i, ref in enumerate((xn_ref, q_ref, k_ref, v_ref, att_ref))
    ]
    saves.append(pltpu.make_async_copy(res_ref, res_hbm, sems_out.at[5]))
    saves.append(pltpu.make_async_copy(gate_ref, gate_hbm, sems_out.at[6]))
    spans = [(4 * d, wide)] + [(i * d, (i + 1) * d) for i in range(4)]
    loads = [
        pltpu.make_async_copy(store.at[0:d, lo:hi], w_ref.at[:, lo:hi], sems.at[i])
        for i, (lo, hi) in enumerate(spans)
    ]
    for load in loads:
        load.start()
    x = hid_ref[...].astype(F32)
    inv = lax.rsqrt(jnp.mean(x * x, axis=1, keepdims=True) + EPS)
    cos = cos_ref[...]
    sin = sin_ref[...]
    allowed = allowed_mask(segc_ref[...], segr_ref[...])
    loads[0].wait()
    aux = w_ref[:, 4 * d : 4 * d + LANES]
    turned = aux.astype(F32).T
    gains = turned[n_exp : n_exp + 8, :]
    gains_ref[...] = gains
    xn = (x * inv * gains[0:1, :]).astype(BF)
    xn_ref[...] = xn
    saves[0].start()
    for load in loads[1:4]:
        load.wait()
    pair = 2 * HD
    for c in range(0, d, pair):
        qp = dot(xn, w_ref[:, c : c + pair])
        kp = dot(xn, w_ref[:, d + c : d + c + pair])
        vp = dot(xn, w_ref[:, 2 * d + c : 2 * d + c + pair])
        v_ref[:, c : c + pair] = vp.astype(BF)
        for o in range(0, pair, HD):
            q = rope(qp[:, o : o + HD], cos, sin).astype(BF)
            k = rope(kp[:, o : o + HD], cos, sin).astype(BF)
            q_ref[:, c + o : c + o + HD] = q
            k_ref[:, c + o : c + o + HD] = k
            probs = head_probs(q, k, allowed).astype(BF)
            att_ref[:, c + o : c + o + HD] = dot(probs, vp[:, o : o + HD].astype(BF)).astype(BF)
    for save in saves[1:5]:
        save.start()
    loads[4].wait()
    res = x + dot(att_ref[...], w_ref[:, 3 * d : 4 * d])
    res_ref[...] = res
    saves[5].start()
    inv2 = lax.rsqrt(jnp.mean(res * res, axis=1, keepdims=True) + EPS)
    act = (res * inv2 * gains[1:2, :]).astype(BF)
    logits = dot(act, aux)
    lane = lax.broadcasted_iota(jnp.int32, (tok, LANES), 1)
    routes = routes_ref[...]
    chosen = routes[:, 0:1] == lane
    for j in range(1, routes.shape[1]):
        chosen = chosen | (routes[:, j : j + 1] == lane)
    logits = jnp.where(chosen, logits, MASKED)
    e = jnp.where(chosen, jnp.exp(logits - jnp.max(logits, axis=1, keepdims=True)), 0.0)
    gate = e / jnp.sum(e, axis=1, keepdims=True)
    gate_ref[...] = gate
    saves[6].start()
    gate_t = gate.T[0:n_exp, :]
    high = gate_t.astype(BF)
    pay_ref[0:tok, :] = act
    pay_ref[tok : tok + n_exp, :] = jnp.zeros((n_exp, d), BF)
    pay_ref[tok : tok + n_exp, 0:tok] = high
    pay_ref[tok : tok + n_exp, tok : 2 * tok] = (gate_t - high.astype(F32)).astype(BF)
    for save in saves:
        save.wait()


def expert_block(first, nb, cap, n_exp, aliased, scal_ref, *refs):
    pays = refs[:nb]
    grads = refs[nb : 2 * nb]
    wg_hbm, wu_hbm, wd_hbm, sgu_ref, sdn_ref = refs[2 * nb : 2 * nb + 5]
    outs = refs[2 * nb + 5 + aliased :]
    saved = outs[:6]
    in_refs = outs[6 : 6 + nb]
    out_refs = outs[6 + nb : 6 + 2 * nb]
    wgu_ref, wd_ref, xr_ref, gr_ref, gh_ref, dgu_ref, agu_ref, adn_ref, sems_w, sems, sems_a = outs[6 + 2 * nb :]
    n_loc, _, ff2 = wgu_ref.shape
    ff = ff2 // 2
    tok, d = grads[0].shape
    loads = []
    for e in range(n_loc):
        three = (
            pltpu.make_async_copy(wg_hbm.at[scal_ref[n_loc + e]], wgu_ref.at[e, :, 0:ff], sems_w.at[e, 0]),
            pltpu.make_async_copy(wu_hbm.at[scal_ref[n_loc + e]], wgu_ref.at[e, :, ff:ff2], sems_w.at[e, 1]),
            pltpu.make_async_copy(wd_hbm.at[scal_ref[n_loc + e]], wd_ref.at[e], sems_w.at[e, 2]),
        )
        for copy in three:
            copy.start()
        loads.append(three)
    sums = []
    if aliased:
        sums.append(pltpu.make_async_copy(saved[4], agu_ref, sems_a.at[0]))
        sums.append(pltpu.make_async_copy(saved[5], adn_ref, sems_a.at[1]))
    for copy in sums:
        copy.start()
    rowid = lax.broadcasted_iota(jnp.int32, (n_exp, tok), 0)
    tri = (
        lax.broadcasted_iota(jnp.int32, (tok, tok), 0)
        < lax.broadcasted_iota(jnp.int32, (tok, tok), 1)
    )
    tri = jnp.where(tri, 1.0, 0.0).astype(BF)
    slots = lax.broadcasted_iota(jnp.int32, (cap, tok), 0)
    gates = []
    for b in range(nb):
        gt = pays[b][tok : tok + n_exp, 0:tok].astype(F32)
        gt = gt + pays[b][tok : tok + n_exp, tok : 2 * tok].astype(F32)
        for e in range(n_loc):
            gates.append(jnp.sum(jnp.where(rowid == scal_ref[e], gt, 0.0), axis=0, keepdims=True))
    used = len(gates)
    stack = jnp.concatenate(gates + [jnp.zeros((-used % 8, tok), F32)] * (used % 8 > 0), axis=0)
    ranks = dot(jnp.where(stack > 0.0, 1.0, 0.0).astype(BF), tri)
    masks, picks, gs = {}, {}, {}
    for b in range(nb):
        for e in range(n_loc):
            at = b * n_loc + e
            g = gates[at]
            slot = jnp.where(g > 0.0, ranks[at : at + 1, :], -1.0).astype(jnp.int32)
            mask = slots == slot
            pick = jnp.where(mask, 1.0, 0.0).astype(BF)
            masks[b, e] = mask
            picks[b, e] = pick
            gs[b, e] = jnp.sum(jnp.where(mask, g, 0.0), axis=1, keepdims=True)
            rows = slice(b * cap, (b + 1) * cap)
            xr_ref[e, rows, :] = dot(pick, pays[b][0:tok, :]).astype(BF)
            gr_ref[e, rows, :] = dot(pick, grads[b][...]).astype(BF)
    copies = []

    def save(j, e, ref):
        copy = pltpu.make_async_copy(
            ref.at[e], saved[j].at[e, pl.ds(first * cap, nb * cap), :], sems.at[j, e]
        )
        copy.start()
        copies.append(copy)

    for copy in sums:
        copy.wait()
    wide_f = sdn_ref.shape[0]
    s_in, s_out = [], []
    for b in range(nb):
        act_b = pays[b][0:tok, :]
        grad_b = grads[b][...]
        sgu = dot(act_b, sgu_ref[...])
        shu = dot_nt(grad_b, sdn_ref[...])
        sg = sgu[:, 0:wide_f]
        su = sgu[:, wide_f : 2 * wide_f]
        sig = sigmoid(sg)
        sact = sg * sig
        sh = (sact * su).astype(BF)
        sd = jnp.concatenate([shu * su * (sig + sact * (1.0 - sig)), shu * sact], axis=1).astype(BF)
        s_out.append(dot(sh, sdn_ref[...]))
        s_in.append(dot_nt(sd, sgu_ref[...]))
        dgu_b = dot_tn(act_b, sd)
        ddn_b = dot_tn(sh, grad_b)
        if aliased or b > 0:
            agu_ref[...] += dgu_b
            adn_ref[...] += ddn_b
        else:
            agu_ref[...] = dgu_b
            adn_ref[...] = ddn_b
    stores = [
        pltpu.make_async_copy(agu_ref, saved[4], sems_a.at[0]),
        pltpu.make_async_copy(adn_ref, saved[5], sems_a.at[1]),
    ]
    for copy in stores:
        copy.start()
        copies.append(copy)
    ggm = [jnp.zeros((n_exp, tok), F32) for _ in range(nb)]
    xis, yos = [], []
    for e in range(n_loc):
        save(0, e, xr_ref)
        save(1, e, gr_ref)
        loads[e][0].wait()
        loads[e][1].wait()
        egu = dot(xr_ref[e], wgu_ref[e])
        loads[e][2].wait()
        hu = dot_nt(gr_ref[e], wd_ref[e])
        gate = jnp.concatenate([gs[b, e] for b in range(nb)], axis=0)
        eg = egu[:, 0:ff]
        eu = egu[:, ff:ff2]
        sig = sigmoid(eg)
        act = eg * sig
        h = act * eu
        gg = jnp.sum(h.astype(BF).astype(F32) * hu, axis=1, keepdims=True)
        gh_ref[e] = (gate * h).astype(BF)
        save(2, e, gh_ref)
        hg = gate * hu
        dgu_ref[e, :, 0:ff] = (hg * eu * (sig + act * (1.0 - sig))).astype(BF)
        dgu_ref[e, :, ff:ff2] = (hg * act).astype(BF)
        save(3, e, dgu_ref)
        yos.append(dot(gh_ref[e], wd_ref[e]).astype(BF))
        xis.append(dot_nt(dgu_ref[e], wgu_ref[e]).astype(BF))
        for b in range(nb):
            row = jnp.sum(jnp.where(masks[b, e], gg[b * cap : (b + 1) * cap], 0.0), axis=0, keepdims=True)
            ggm[b] = ggm[b] + jnp.where(rowid == scal_ref[e], row, 0.0)
    for b in range(nb):
        rows = slice(b * cap, (b + 1) * cap)
        pick = jnp.concatenate([picks[b, e] for e in range(n_loc)], axis=0)
        in_rows = dot_tn(pick, jnp.concatenate([v[rows] for v in xis], axis=0))
        out_rows = dot_tn(pick, jnp.concatenate([v[rows] for v in yos], axis=0))
        in_refs[b][0:tok, :] = (in_rows + s_in[b]).astype(BF)
        out_refs[b][...] = (out_rows + s_out[b]).astype(BF)
        high = ggm[b].astype(BF)
        in_refs[b][tok : tok + n_exp, :] = jnp.zeros((n_exp, d), BF)
        in_refs[b][tok : tok + n_exp, 0:tok] = high
        in_refs[b][tok : tok + n_exp, tok : 2 * tok] = (ggm[b] - high.astype(F32)).astype(BF)
    for copy in copies:
        copy.wait()


def expert_call(first, nb, cap, n_exp, scal, pays, grads, weights, saved):
    extra, d = pays[0].shape
    tok = grads[0].shape[0]
    n_loc, _, ff = weights[0].shape
    wide_f = weights[4].shape[0]
    rows = cap * (extra - tok) // n_loc
    saved_shapes = (
        hbm((n_loc, rows, d), BF),
        hbm((n_loc, rows, d), BF),
        hbm((n_loc, rows, ff), BF),
        hbm((n_loc, rows, 2 * ff), BF),
        hbm((d, 2 * wide_f), F32),
        hbm((wide_f, d), F32),
    )
    outs = pl.pallas_call(
        functools.partial(expert_block, first, nb, cap, n_exp, len(saved)),
        out_shape=saved_shapes + (shape((extra, d), BF),) * nb + (shape((tok, d), BF),) * nb,
        in_specs=[whole(SMEM)]
        + [whole()] * (2 * nb)
        + [far()] * 3
        + [whole()] * 2
        + [far()] * len(saved),
        out_specs=[far()] * 6 + [whole()] * (2 * nb),
        scratch_shapes=[
            VMEM((n_loc, d, 2 * ff), BF),
            VMEM((n_loc, ff, d), BF),
            VMEM((n_loc, nb * cap, d), BF),
            VMEM((n_loc, nb * cap, d), BF),
            VMEM((n_loc, nb * cap, ff), BF),
            VMEM((n_loc, nb * cap, 2 * ff), BF),
            VMEM((d, 2 * wide_f), F32),
            VMEM((wide_f, d), F32),
            pltpu.SemaphoreType.DMA((n_loc, 3)),
            pltpu.SemaphoreType.DMA((4, n_loc)),
            pltpu.SemaphoreType.DMA((2,)),
        ],
        input_output_aliases={1 + 2 * nb + 5 + j: j for j in range(len(saved))},
        compiler_params=params(40),
        cost_estimate=cost(nb * cap * n_loc * d * ff * 12, 3 * n_loc * d * ff * 2),
        name="expert_block",
    )(scal, *pays, *grads, *weights, *saved)
    return outs[:6], list(outs[6 : 6 + nb]), list(outs[6 + nb :])


def attn_backward(
    n_exp, gidx_ref, hid_ref, grad_ref, segc_ref, segr_ref, cos_ref, sin_ref, gate_ref, gains_ref,
    rs_ref, own_ref, *rest
):
    n = gidx_ref.shape[0]
    store, pay_hbm, res_hbm = rest[:3]
    ig_ref, mine_ref, first_ref, theirs_ref, w_ref, dw_ref, dq_ref, dk_ref, dv_ref = rest[3:12]
    xn_ref, q_ref, k_ref, v_ref, att_ref, pay_ref, res_ref, sems_in, sems_out = rest[12:]
    height = mine_ref.shape[1]
    tok, d = hid_ref.shape
    sources = [store.at[stored_at(i, tok, d)] for i in range(5)] + [pay_hbm, res_hbm]
    sources.append(store.at[0:d, :])
    loads = [
        pltpu.make_async_copy(src, ref, sems_in.at[i])
        for i, (src, ref) in enumerate(
            zip(sources, (xn_ref, q_ref, k_ref, v_ref, att_ref, pay_ref, res_ref, w_ref))
        )
    ]
    for i in (5, 6, 7, 4, 1, 2, 3, 0):
        loads[i].start()
    loads[5].wait()
    gains = gains_ref[...]
    gain1 = gains[0:1, :]
    gain2 = gains[1:2, :]
    rows = rs_ref[...].astype(F32) + own_ref[...].astype(F32)
    tail = rows[tok : tok + n_exp, :]
    ggt = tail[:, 0:tok] + tail[:, tok : 2 * tok]
    ggt = jnp.concatenate([ggt, jnp.zeros((LANES - n_exp, tok), F32)], axis=0)
    gg = ggt.T
    gate = gate_ref[...]
    picked = gate * (gg - jnp.sum(gate * gg, axis=1, keepdims=True))
    logit_grad = picked.astype(BF)
    act_t = pay_ref[0:tok, :].T
    aux_grad = dot(act_t, logit_grad)
    grad = grad_ref[...].astype(F32)
    loads[6].wait()
    res = res_ref[...]
    inv2 = lax.rsqrt(jnp.mean(res * res, axis=1, keepdims=True) + EPS)
    loads[7].wait()
    moe_in = rows[0:tok, :] + dot_nt(logit_grad, w_ref[:, 4 * d : 4 * d + LANES])
    weighted = moe_in * gain2
    gg2 = jnp.sum(moe_in * res * inv2, axis=0, keepdims=True)
    inner = jnp.mean(weighted * res, axis=1, keepdims=True)
    rgrad = grad + inv2 * weighted - res * (inv2 * inv2 * inv2 * inner)
    low = rgrad.astype(BF)
    for i in (4, 1, 2, 3, 0):
        loads[i].wait()
    dw_ref[:, 3 * d : 4 * d] = dot(att_ref[...].T, low).astype(BF)
    allowed = allowed_mask(segc_ref[...], segr_ref[...])
    cos = cos_ref[...]
    sin = sin_ref[...]
    scale = HD ** -0.5
    pair = 2 * HD
    for c in range(0, d, pair):
        agp = dot_nt(low, w_ref[c : c + pair, 3 * d : 4 * d]).astype(BF)
        for o in range(0, pair, HD):
            cols = slice(c + o, c + o + HD)
            q = q_ref[:, cols]
            k = k_ref[:, cols]
            ag = agp[:, o : o + HD]
            probs = head_probs(q, k, allowed)
            dv_ref[:, cols] = dot_tn(probs.astype(BF), ag).astype(BF)
            dp = dot_nt(ag, v_ref[:, cols])
            ds = (probs * (dp - jnp.sum(probs * dp, axis=1, keepdims=True))).astype(BF)
            dq = dot(ds, k) * scale
            dk = dot_tn(ds, q) * scale
            dq_ref[:, cols] = rope_back(dq, cos, sin).astype(BF)
            dk_ref[:, cols] = rope_back(dk, cos, sin).astype(BF)
    back = dot_nt(dq_ref[...], w_ref[:, 0:d])
    back += dot_nt(dk_ref[...], w_ref[:, d : 2 * d])
    back += dot_nt(dv_ref[...], w_ref[:, 2 * d : 3 * d])
    x = hid_ref[...].astype(F32)
    inv = lax.rsqrt(jnp.mean(x * x, axis=1, keepdims=True) + EPS)
    weighted = back * gain1
    gg1 = jnp.sum(back * x * inv, axis=0, keepdims=True)
    inner = jnp.mean(weighted * x, axis=1, keepdims=True)
    ig_ref[...] = rgrad + inv * weighted - x * (inv * inv * inv * inner)
    rowid = lax.broadcasted_iota(jnp.int32, (LANES, d), 0)
    gain_rows = jnp.where(rowid == n_exp, gg1, 0.0) + jnp.where(rowid == n_exp + 1, gg2, 0.0)
    dw_ref[:, 4 * d : 4 * d + LANES] = (aux_grad + gain_rows.T).astype(BF)
    xn_t = xn_ref[...].T
    dw_ref[:, 0:d] = dot(xn_t, dq_ref[...]).astype(BF)
    dw_ref[:, d : 2 * d] = dot(xn_t, dk_ref[...]).astype(BF)
    dw_ref[:, 2 * d : 3 * d] = dot(xn_t, dv_ref[...]).astype(BF)
    half = n // 2
    outs = []
    for i in range(n):
        start = pl.multiple_of(gidx_ref[i] * height, 16)
        out = mine_ref.at[i] if i < half else first_ref if i == half else theirs_ref.at[i - half - 1]
        copy = pltpu.make_async_copy(dw_ref.at[pl.ds(start, height), :], out, sems_out.at[i])
        copy.start()
        outs.append(copy)
    for copy in outs:
        copy.wait()


def body(
    nd,
    ne,
    hidden_in,
    out_grad,
    segment_ids,
    routes,
    attn_gain,
    w_query,
    w_key,
    w_value,
    w_out,
    moe_gain,
    w_router,
    shared_gate,
    shared_up,
    shared_down,
    expert_gate,
    expert_up,
    expert_down,
):
    tok, d = hidden_in.shape
    n_exp = w_router.shape[1]
    n_loc = expert_gate.shape[0]
    ff = expert_gate.shape[2]
    top_k = routes.shape[1]
    cap = min(tok, 8 * ((10 * tok * top_k + 56 * n_exp - 1) // (56 * n_exp)))
    extra = tok + n_exp
    hr = d // ne // 2
    hdn = shared_down.shape[0]
    wide = 4 * d + LANES

    me = lax.axis_index("expert")
    core = lax.axis_index("dp") % 2
    perm = ring_perm(nd, ne)
    both = ("dp", "expert")

    def ring(v):
        return lax.ppermute(v, both, perm)

    def after(v, *others):
        return lax.optimization_barrier((v,) + others)[0]

    def swap(v, bit):
        return lax.ppermute(v, "dp", [(i, i ^ bit) for i in range(nd)])

    table = jnp.asarray(ring_order(ne))
    mine_order = lax.dynamic_slice(table, (core, me, 0), (1, 1, ne)).reshape(ne)
    other_order = lax.dynamic_slice(table, (1 - core, me, 0), (1, 1, ne)).reshape(ne)
    idx = jnp.concatenate([mine_order * 2 + core, other_order * 2 + 1 - core])
    gidx = jnp.concatenate(
        [jnp.roll(mine_order, -1) * 2 + core, jnp.roll(other_order, -1) * 2 + 1 - core]
    )
    scal = jnp.stack([me * n_loc + 1 - core, me * n_loc + core, 1 - core, core]).astype(jnp.int32)

    def fence(*vs):
        return list(lax.optimization_barrier(tuple(vs)))

    def halves(v):
        v = v.reshape(2, v.shape[0] // 2, v.shape[1])
        return (
            lax.dynamic_index_in_dim(v, core, 0, False),
            lax.dynamic_index_in_dim(v, 1 - core, 0, False),
        )

    units = ff // ne
    wide_f = -(-units // LANES) * LANES

    def spread(v):
        v = v.reshape(v.shape[0], ne, units).transpose(1, 0, 2)
        return jnp.pad(v, ((0, 0), (0, 0), (0, wide_f - units)))

    def exchange(v):
        return lax.all_to_all(v, "expert", split_axis=0, concat_axis=0, tiled=True)

    sgu = jnp.concatenate([spread(halves(shared_gate)[0]), spread(halves(shared_up)[0])], axis=2)
    sdn = jnp.pad(shared_down, ((0, wide_f - units), (0, 0)))

    split = 2 * d
    aux = jnp.concatenate(
        [
            w_router,
            attn_gain[:, None],
            moe_gain[:, None],
            jnp.zeros((w_router.shape[0], LANES - n_exp - 2), BF),
        ],
        axis=1,
    )
    left, left_other = halves(jnp.concatenate([w_query, w_key], axis=1))
    right, right_other = halves(jnp.concatenate([w_value, w_out, aux], axis=1))
    store_shape = (hbm((d + 2 * tok, wide), BF),)
    kinds = [(0, 0), (0, split)] * 2
    store = place_call(
        kinds, [0, 0, ne, ne], idx, [left, right, left_other, right_other], store_shape, ()
    )
    for i in range(1, ne):
        left = ring(left)
        right = ring(right)
        if i == 2:
            left, sgu = fence(left, sgu)
            sgu = exchange(sgu)
        if i == 4:
            left, sgu = fence(left, sgu)
            sgu = jnp.stack([sgu, swap(sgu, 1)])
            sgu = jnp.where(core == 0, sgu, sgu[::-1]).transpose(1, 0, 2, 3).reshape(d, 2 * wide_f)
        if i == 6:
            left, sgu = fence(left, sgu)
        if i + 1 < ne:
            placed = place_call(
                kinds, [i, i, ne + i, ne + i], idx, [left, right, swap(left, 1), swap(right, 1)], store_shape, store
            )
            left = fence(left, *store)[0]
            right = fence(right, *store)[0]
        else:
            left, right, *store = fence(left, right, *store)
            placed = place_call(
                kinds, [i, i, ne + i, ne + i], idx, [left, right, swap(left, 1), swap(right, 1)], store_shape, store
            )
        store = placed

    half = HD // 2
    freq = ROPE_BASE ** (-2.0 * np.arange(half) / HD)
    ang = np.arange(tok)[:, None] * freq[None, :]
    cos = jnp.asarray(np.concatenate([np.cos(ang), np.cos(ang)], 1).astype(np.float32))
    sin = jnp.asarray(np.concatenate([-np.sin(ang), np.sin(ang)], 1).astype(np.float32))
    seg_row = segment_ids
    seg_col = segment_ids.reshape(tok, 1)

    g0, left, right = fence(out_grad, left, right)
    grads = [g0, ring(g0)]
    store, res, gate, pay, gains = pl.pallas_call(
        functools.partial(attn_forward, n_exp),
        out_shape=store_shape
        + (
            hbm((tok, d), F32),
            hbm((tok, LANES), F32),
            shape((extra, d), BF),
            shape((8, d), F32),
        ),
        in_specs=[whole()] * 6 + [far()],
        out_specs=[far()] * 3 + [whole()] * 2,
        scratch_shapes=[VMEM((d, wide), BF)]
        + [VMEM((tok, d), BF)] * 5
        + [
            VMEM((tok, d), F32),
            VMEM((tok, LANES), F32),
            pltpu.SemaphoreType.DMA((5,)),
            pltpu.SemaphoreType.DMA((7,)),
        ],
        input_output_aliases={6: 0},
        compiler_params=params(36),
        cost_estimate=cost(2 * tok * d * d * 4, d * wide * 2),
        name="attn_forward",
    )(hidden_in, seg_col, seg_row, routes, cos, sin, *store)
    pay, grads[1] = fence(pay, grads[1])

    def start_flow(parts):
        return {"parts": parts, "at": 0, "acc": parts(0).astype(BF)}

    def advance(flow, got):
        flow["at"] += 1
        if flow["at"] == ne - 1:
            flow["got"] = got
        else:
            flow["acc"] = (got.astype(F32) + flow["parts"](flow["at"])).astype(BF)

    def ring_total(flow):
        return flow["got"].astype(F32) + flow["parts"](ne - 1)

    def token_parts(parts):
        return lambda i: parts[(i + 1) % ne].astype(F32)

    def dense_parts(mine, first, rest):
        return lambda i: mine[i].astype(F32) + (first if i == 0 else rest[i - 1]).astype(F32)

    down_shapes = (hbm((n_loc, ff, d), F32),)
    gu_shapes = (hbm((n_loc, d, ff), F32),) * 2
    n_down, n_gu = 4, 8
    waiting, landed, shared_out = [], [], []
    finished = {"down": (), "gu": ()}

    def queue(name, low, count):
        height = low.shape[0] // count
        for j in range(count):
            waiting.append((name, j * height, lax.slice_in_dim(low, j * height, (j + 1) * height)))

    def across(low):
        return swap(low, 2) if nd > 2 else low * 0

    def summed(low, more):
        total = low.astype(F32) + more.astype(F32)
        bit = 4
        while bit < nd:
            low = total.astype(BF)
            total = low.astype(F32) + swap(low, bit).astype(F32)
            bit *= 2
        return total.astype(BF)

    def emit():
        names = set()
        for name, start, mine, other in shared_out:
            if name not in finished:
                held[name] = (start, mine, other)
                continue
            shapes = down_shapes if name == "down" else gu_shapes
            finished[name] = emit_call(start, scal, mine, other, shapes, finished[name])
            names.add(name)
        shared_out.clear()
        return sorted(names)

    held = {}

    def slot(flows=(), sends=(), swaps=(), cross=0, compute=None, keep=(), ready=None, write=True):
        chunks = waiting[:cross]
        del waiting[:cross]
        summing = [(name, start, summed(low, more)) for (name, start, low), more in landed]
        landed.clear()
        moved = [ring(f["acc"]) for f in flows] + [ring(v) for v in sends]
        moved += [across(low) for _, _, low in chunks]
        moved += [swap(v, 1) for v in swaps]
        moved += [swap(mine, 1) for _, _, mine in summing]
        names = emit() if write else []
        done = list(compute()) if compute is not None else []
        late = [v for name in names for v in finished[name]]
        out = fence(*moved, *done, *keep, *late)

        def pop(count):
            first = out[:count]
            del out[:count]
            return first

        arrived = pop(len(flows))
        sent = pop(len(sends))
        landed.extend(zip(chunks, pop(len(chunks))))
        swapped = pop(len(swaps))
        if ready is not None:
            ready(swapped)
        for f, got in zip(flows, arrived):
            advance(f, got)
        for (name, start, mine), other in zip(summing, pop(len(summing))):
            shared_out.append((name, start, mine, other))
        done = pop(len(done))
        kept = pop(len(keep))
        for name in names:
            finished[name] = tuple(pop(len(finished[name])))
        return sent, swapped, done, kept

    pays = [pay]
    saved = ()
    in_parts, out_parts = [], []
    flow_in = None
    for i in range(ne):
        sends = []
        if i + 1 < ne:
            sends.append(pays[i])
        if i + 2 < ne:
            sends.append(grads[i + 1])
        if i == ne - 2:
            flow_in = start_flow(token_parts(in_parts))

        def block(i=i):
            new, ins, outs = expert_call(
                i, 1, cap, n_exp, scal, pays[i : i + 1], grads[i : i + 1],
                (expert_gate, expert_up, expert_down, sgu, sdn), saved,
            )
            held["saved"] = new
            return [ins[0], outs[0]]

        sent, _, done, _ = slot([flow_in] if flow_in else [], sends, compute=block)
        saved = held["saved"]
        in_parts.append(done[0])
        out_parts.append(done[1])
        if i + 1 < ne:
            pays.append(sent[0])
        if i + 2 < ne:
            grads.append(sent[-1])

    xr, gr, gh, dgu, sum_gu, sum_dn = saved
    hw = d // 2
    gu_halves = sum_gu.astype(BF).reshape(ne, 2, hr, 2 * wide_f).transpose(1, 0, 2, 3)
    dn_halves = sum_dn[0:units].astype(BF).reshape(units, 2, hw).transpose(1, 0, 2)

    def of_side(v, side):
        return lax.dynamic_index_in_dim(v, side, 0, False)

    _, (gu_more, dn_more), (down_t,), _ = slot(
        [flow_in],
        swaps=[of_side(gu_halves, 1 - core), of_side(dn_halves, 1 - core)],
        compute=lambda: [dot_tn(gh[0], gr[0]).astype(BF)],
    )

    def add(left, right):
        return (left.astype(F32) + right.astype(F32)).astype(BF)

    _, (down_got,), (down_m,), _ = slot(
        [flow_in], swaps=[down_t], compute=lambda: [dot_tn(gh[1], gr[1]).astype(BF)]
    )
    queue("down", add(down_m, down_got), n_down)
    _, _, (gu_t,), _ = slot([flow_in], cross=1, compute=lambda: [dot_tn(xr[0], dgu[0]).astype(BF)])
    _, _, (gu_m,), _ = slot([flow_in], cross=1, compute=lambda: [dot_tn(xr[1], dgu[1]).astype(BF)])
    _, (gu_got,), _, _ = slot([flow_in], swaps=[gu_t], cross=1)
    while flow_in["at"] < ne - 1:
        slot([flow_in])
    height = d // n_gu
    for j in range(n_gu):
        cut_rows = slice(j * height, (j + 1) * height)
        waiting.append(("gu", j * height, add(gu_m[cut_rows], gu_got[cut_rows])))
    waiting.insert(2, ("sgu", 0, add(of_side(gu_halves, core), gu_more)))
    waiting.insert(3, ("sdn", 0, add(of_side(dn_halves, core), dn_more)))
    rs_in = flow_in["got"]
    flow_out = start_flow(token_parts(out_parts))

    def backward():
        return pl.pallas_call(
            functools.partial(attn_backward, n_exp),
            out_shape=(
                shape((tok, d), F32),
                hbm((ne, hr, wide), BF),
                hbm((hr, wide), BF),
                hbm((ne - 1, hr, wide), BF),
            ),
            in_specs=[whole(SMEM)] + [whole()] * 10 + [far()] * 3,
            out_specs=[whole()] + [far()] * 3,
            scratch_shapes=[
                VMEM((d, wide), BF),
                VMEM((d, wide), BF),
            ]
            + [VMEM((tok, d), BF)] * 8
            + [
                VMEM((extra, d), BF),
                VMEM((tok, d), F32),
                pltpu.SemaphoreType.DMA((8,)),
                pltpu.SemaphoreType.DMA((2 * ne,)),
            ],
            compiler_params=params(56),
            cost_estimate=cost(2 * tok * d * d * 8, 2 * d * wide * 2),
            name="attn_backward",
        )(
            gidx, hidden_in, out_grad, seg_col, seg_row, cos, sin, gate, gains, rs_in, in_parts[0],
            store, pay, res,
        )

    _, _, (input_grad, d_mine, d_first, d_rest), _ = slot([flow_out], cross=2, compute=backward, write=False)
    flow_d = start_flow(dense_parts(d_mine, swap(d_first, 1), None))

    def rest_of_d(swapped):
        flow_d["parts"] = dense_parts(d_mine, None, swapped[0])

    slot([flow_d, flow_out], swaps=[d_rest], cross=2, ready=rest_of_d)

    def shared_exchange():
        if "sgu" in held and "sgu_sent" not in held:
            _, mine, _ = held["sgu"]
            held["sgu_sent"] = True
            return [exchange(mine)]
        return []

    while flow_d["at"] < ne - 1:
        flows = [flow_d]
        if flow_out["at"] < ne - 3:
            flows.append(flow_out)
        _, _, got, _ = slot(flows, cross=1, compute=shared_exchange)
        if got:
            held["spread"] = got[0]
    queue("dense", ring_total(flow_d).astype(BF), 1)
    spread_other = []
    while waiting or landed or shared_out or flow_out["at"] < ne - 1:
        swaps = [held["spread"]] if not spread_other else []
        _, swapped, _, _ = slot(
            [flow_out] if flow_out["at"] < ne - 1 else [], swaps=swaps, cross=len(waiting)
        )
        spread_other += swapped

    output = res + flow_out["got"].astype(F32) + out_parts[0].astype(F32)
    pick = core == 0

    def sides(name):
        _, mine, other = held[name]
        mine = mine.astype(F32)
        other = other.astype(F32)
        return jnp.where(pick, mine, other), jnp.where(pick, other, mine)

    g_d = jnp.concatenate(sides("dense"), axis=0)
    held["rows"] = (0, held["spread"], spread_other[0])
    both_rows = jnp.concatenate(sides("rows"), axis=1)
    g_gate = both_rows[:, :, 0:units].transpose(1, 0, 2).reshape(2 * hr, ff)
    g_up = both_rows[:, :, wide_f : wide_f + units].transpose(1, 0, 2).reshape(2 * hr, ff)
    g_dn = jnp.concatenate(sides("sdn"), axis=1)
    (down_w,) = finished["down"]
    gate_w, up_w = finished["gu"]
    return (
        output,
        input_grad,
        g_d[:, 4 * d + n_exp],
        g_d[:, 0:d],
        g_d[:, d : 2 * d],
        g_d[:, 2 * d : 3 * d],
        g_d[:, 3 * d : 4 * d],
        g_d[:, 4 * d + n_exp + 1],
        g_d[:, 4 * d : 4 * d + n_exp],
        g_gate,
        g_up,
        g_dn,
        gate_w,
        up_w,
        down_w,
    )


def solution(mesh):
    nd = mesh.shape["dp"]
    ne = mesh.shape["expert"]
    tokens = P(("dp", "expert"), None)
    vector = P("expert")
    matrix = P("expert", None)
    cube = P("expert", None, None)
    return jax.shard_map(
        functools.partial(body, nd, ne),
        mesh=mesh,
        in_specs=(tokens,) * 4
        + (vector, matrix, matrix, matrix, matrix, vector)
        + (matrix,) * 4
        + (cube,) * 3,
        out_specs=(tokens, tokens, vector, matrix, matrix, matrix, matrix, vector)
        + (matrix,) * 4
        + (cube,) * 3,
        check_vma=False,
    )
```

```python
import functools

import jax
import jax.numpy as jnp
import numpy as np
from jax import lax
from jax.experimental import pallas as pl
from jax.experimental.pallas import tpu as pltpu
from jax.sharding import PartitionSpec as P

HD = 128
LANES = 128
EPS = 1e-06
ROPE_BASE = 10000.0
MASKED = -1e30
BF = jnp.bfloat16
F32 = jnp.float32
VMEM = pltpu.VMEM
SMEM = pltpu.SMEM
MIB = 1 << 20


def dot(a, b):
    return jnp.dot(a, b, preferred_element_type=F32)


def dot_nt(a, b):
    return lax.dot_general(a, b, (((1,), (1,)), ((), ())), preferred_element_type=F32)


def dot_tn(a, b):
    return lax.dot_general(a, b, (((0,), (0,)), ((), ())), preferred_element_type=F32)


def sigmoid(v):
    return 1.0 / (1.0 + jnp.exp(-v))


def whole(space=VMEM):
    return pl.BlockSpec(memory_space=space)


def anywhere():
    return pl.BlockSpec(memory_space=pl.ANY)


def far():
    return pl.BlockSpec(memory_space=pltpu.HBM)


def params(mib):
    return pltpu.CompilerParams(vmem_limit_bytes=mib * MIB)


def cost(flops, nbytes):
    return pl.CostEstimate(flops=int(flops), bytes_accessed=int(nbytes), transcendentals=0)


def shape(dims, dtype):
    return jax.ShapeDtypeStruct(dims, dtype)


def hbm(dims, dtype):
    return pltpu.HBM(dims, dtype)


def cycle(n):
    return list(range(0, n, 2)) + list(range(1, n, 2))[::-1]


def ring_perm(nd, ne):
    ring = cycle(ne)
    pos = {e: i for i, e in enumerate(ring)}
    pairs = []
    for d in range(nd):
        for e in range(ne):
            step = 1 if d % 2 == 0 else -1
            pairs.append((d * ne + e, d * ne + ring[(pos[e] + step) % ne]))
    return pairs


def ring_order(ne):
    ring = cycle(ne)
    pos = {e: i for i, e in enumerate(ring)}
    table = np.zeros((2, ne, ne), np.int32)
    for c in range(2):
        step = 1 if c == 0 else -1
        for e in range(ne):
            for s in range(ne):
                table[c, e, s] = ring[(pos[e] - step * s) % ne]
    return table


def place_pieces(kinds, spots, aliased, idx_ref, *refs):
    n = len(kinds)
    pieces = refs[:n]
    outs = refs[n + aliased : -1]
    sems = refs[-1]
    copies = []
    for i, (target, col) in enumerate(kinds):
        height, width = pieces[i].shape
        start = pl.multiple_of(idx_ref[spots[i]] * height, 16)
        dst = outs[target].at[pl.ds(start, height), col : col + width]
        copies.append(pltpu.make_async_copy(pieces[i], dst, sems.at[i]))
    for copy in copies:
        copy.start()
    for copy in copies:
        copy.wait()


def place_call(kinds, spots, idx, pieces, targets, into):
    n = len(kinds)
    return pl.pallas_call(
        functools.partial(place_pieces, kinds, spots, len(into)),
        out_shape=targets,
        in_specs=[whole(SMEM)] + [whole()] * n + [far()] * len(into),
        out_specs=[far()] * len(targets),
        scratch_shapes=[pltpu.SemaphoreType.DMA((n,))],
        input_output_aliases={1 + n + j: j for j in range(len(into))},
        compiler_params=params(8),
        cost_estimate=cost(0, sum(p.size for p in pieces) * 4),
        name="place_pieces",
    )(idx, *pieces, *into)


def emit_rows(start, aliased, scal_ref, mine_ref, other_ref, *refs):
    outs = refs[aliased : -2]
    buf, sems = refs[-2:]
    height = mine_ref.shape[0]
    width = outs[0].shape[2]
    buf[0] = mine_ref[...].astype(F32)
    buf[1] = other_ref[...].astype(F32)
    copies = []
    for side in range(2):
        expert = scal_ref[3 - side]
        for j, out in enumerate(outs):
            copies.append(
                pltpu.make_async_copy(
                    buf.at[side, :, j * width : (j + 1) * width],
                    out.at[expert, pl.ds(start, height), :],
                    sems.at[side, j],
                )
            )
    for copy in copies:
        copy.start()
    for copy in copies:
        copy.wait()


def emit_call(start, scal, mine, other, targets, into):
    return pl.pallas_call(
        functools.partial(emit_rows, start, len(into)),
        out_shape=targets,
        in_specs=[whole(SMEM)] + [whole()] * 2 + [far()] * len(into),
        out_specs=[far()] * len(targets),
        scratch_shapes=[
            VMEM((2,) + mine.shape, F32),
            pltpu.SemaphoreType.DMA((2, len(targets))),
        ],
        input_output_aliases={3 + j: j for j in range(len(into))},
        compiler_params=params(12),
        cost_estimate=cost(0, mine.size * 12),
        name="emit_rows",
    )(scal, mine, other, *into)


def stored_at(i, tok, d):
    row = d + tok * (i // 4)
    col = d * (i % 4)
    return slice(row, row + tok), slice(col, col + d)


def rope(u, cos, sin):
    return u * cos + pltpu.roll(u, HD // 2, 1) * sin


def rope_back(u, cos, sin):
    return u * cos - pltpu.roll(u, HD // 2, 1) * sin


def allowed_mask(seg_col, seg_row):
    n = seg_row.shape[1]
    rows = lax.broadcasted_iota(jnp.int32, (n, n), 0)
    cols = lax.broadcasted_iota(jnp.int32, (n, n), 1)
    return (seg_col == seg_row) & (cols <= rows)


def head_probs(q, k, allowed):
    s = dot_nt(q, k) * (HD ** -0.5)
    s = jnp.where(allowed, s, MASKED)
    e = jnp.exp(s - jnp.max(s, axis=1, keepdims=True))
    return e / jnp.sum(e, axis=1, keepdims=True)


def attn_forward(n_exp, hid_ref, segc_ref, segr_ref, routes_ref, cos_ref, sin_ref, store_in, *rest):
    store, res_hbm, gate_hbm, pay_ref, gains_ref, w_ref, xn_ref, q_ref, k_ref, v_ref, att_ref = rest[:11]
    res_ref, gate_ref, sems, sems_out = rest[11:]
    tok, d = hid_ref.shape
    wide = w_ref.shape[1]
    saves = [
        pltpu.make_async_copy(ref, store.at[stored_at(i, tok, d)], sems_out.at[i])
        for i, ref in enumerate((xn_ref, q_ref, k_ref, v_ref, att_ref))
    ]
    saves.append(pltpu.make_async_copy(res_ref, res_hbm, sems_out.at[5]))
    saves.append(pltpu.make_async_copy(gate_ref, gate_hbm, sems_out.at[6]))
    spans = [(4 * d, wide)] + [(i * d, (i + 1) * d) for i in range(4)]
    loads = [
        pltpu.make_async_copy(store.at[0:d, lo:hi], w_ref.at[:, lo:hi], sems.at[i])
        for i, (lo, hi) in enumerate(spans)
    ]
    for load in loads:
        load.start()
    x = hid_ref[...].astype(F32)
    inv = lax.rsqrt(jnp.mean(x * x, axis=1, keepdims=True) + EPS)
    cos = cos_ref[...]
    sin = sin_ref[...]
    allowed = allowed_mask(segc_ref[...], segr_ref[...])
    loads[0].wait()
    aux = w_ref[:, 4 * d : 4 * d + LANES]
    turned = aux.astype(F32).T
    gains = turned[n_exp : n_exp + 8, :]
    gains_ref[...] = gains
    xn = (x * inv * gains[0:1, :]).astype(BF)
    xn_ref[...] = xn
    saves[0].start()
    pair = 2 * HD
    for j, ref in ((0, q_ref), (1, k_ref)):
        loads[1 + j].wait()
        for c in range(0, d, pair):
            pre = dot(xn, w_ref[:, j * d + c : j * d + c + pair])
            for o in range(0, pair, HD):
                ref[:, c + o : c + o + HD] = rope(pre[:, o : o + HD], cos, sin).astype(BF)
    loads[3].wait()
    for c in range(0, d, pair):
        vp = dot(xn, w_ref[:, 2 * d + c : 2 * d + c + pair]).astype(BF)
        v_ref[:, c : c + pair] = vp
        for o in range(0, pair, HD):
            cols = slice(c + o, c + o + HD)
            probs = head_probs(q_ref[:, cols], k_ref[:, cols], allowed).astype(BF)
            att_ref[:, cols] = dot(probs, vp[:, o : o + HD]).astype(BF)
    for save in saves[1:5]:
        save.start()
    loads[4].wait()
    res = x + dot(att_ref[...], w_ref[:, 3 * d : 4 * d])
    res_ref[...] = res
    saves[5].start()
    inv2 = lax.rsqrt(jnp.mean(res * res, axis=1, keepdims=True) + EPS)
    act = (res * inv2 * gains[1:2, :]).astype(BF)
    logits = dot(act, aux)
    lane = lax.broadcasted_iota(jnp.int32, (tok, LANES), 1)
    routes = routes_ref[...]
    chosen = routes[:, 0:1] == lane
    for j in range(1, routes.shape[1]):
        chosen = chosen | (routes[:, j : j + 1] == lane)
    logits = jnp.where(chosen, logits, MASKED)
    e = jnp.where(chosen, jnp.exp(logits - jnp.max(logits, axis=1, keepdims=True)), 0.0)
    gate = e / jnp.sum(e, axis=1, keepdims=True)
    gate_ref[...] = gate
    saves[6].start()
    gate_t = gate.T[0:n_exp, :]
    high = gate_t.astype(BF)
    pay_ref[0:tok, :] = act
    pay_ref[tok : tok + n_exp, :] = jnp.zeros((n_exp, d), BF)
    pay_ref[tok : tok + n_exp, 0:tok] = high
    pay_ref[tok : tok + n_exp, tok : 2 * tok] = (gate_t - high.astype(F32)).astype(BF)
    for save in saves:
        save.wait()


def expert_block(first, nb, cap, n_exp, aliased, scal_ref, *refs):
    pays = refs[:nb]
    grads = refs[nb : 2 * nb]
    wg_hbm, wu_hbm, wd_hbm, sgu_ref, sdn_ref = refs[2 * nb : 2 * nb + 5]
    outs = refs[2 * nb + 5 + aliased :]
    saved = outs[:6]
    in_refs = outs[6 : 6 + nb]
    out_refs = outs[6 + nb : 6 + 2 * nb]
    wgu_ref, wd_ref, xr_ref, gr_ref, gh_ref, dgu_ref, agu_ref, adn_ref, sems_w, sems, sems_a = outs[6 + 2 * nb :]
    n_loc, _, ff2 = wgu_ref.shape
    ff = ff2 // 2
    tok, d = grads[0].shape
    loads = []
    for e in range(n_loc):
        three = (
            pltpu.make_async_copy(wg_hbm.at[scal_ref[n_loc + e]], wgu_ref.at[e, :, 0:ff], sems_w.at[e, 0]),
            pltpu.make_async_copy(wu_hbm.at[scal_ref[n_loc + e]], wgu_ref.at[e, :, ff:ff2], sems_w.at[e, 1]),
            pltpu.make_async_copy(wd_hbm.at[scal_ref[n_loc + e]], wd_ref.at[e], sems_w.at[e, 2]),
        )
        for copy in three:
            copy.start()
        loads.append(three)
    sums = []
    if aliased:
        sums.append(pltpu.make_async_copy(saved[4], agu_ref, sems_a.at[0]))
        sums.append(pltpu.make_async_copy(saved[5], adn_ref, sems_a.at[1]))
    for copy in sums:
        copy.start()
    rowid = lax.broadcasted_iota(jnp.int32, (n_exp, tok), 0)
    tri = (
        lax.broadcasted_iota(jnp.int32, (tok, tok), 0)
        < lax.broadcasted_iota(jnp.int32, (tok, tok), 1)
    )
    tri = jnp.where(tri, 1.0, 0.0).astype(BF)
    slots = lax.broadcasted_iota(jnp.int32, (cap, tok), 0)
    gates = []
    for b in range(nb):
        gt = pays[b][tok : tok + n_exp, 0:tok].astype(F32)
        gt = gt + pays[b][tok : tok + n_exp, tok : 2 * tok].astype(F32)
        for e in range(n_loc):
            gates.append(jnp.sum(jnp.where(rowid == scal_ref[e], gt, 0.0), axis=0, keepdims=True))
    used = len(gates)
    stack = jnp.concatenate(gates + [jnp.zeros((-used % 8, tok), F32)] * (used % 8 > 0), axis=0)
    ranks = dot(jnp.where(stack > 0.0, 1.0, 0.0).astype(BF), tri)
    masks, picks, gs = {}, {}, {}
    for b in range(nb):
        for e in range(n_loc):
            at = b * n_loc + e
            g = gates[at]
            slot = jnp.where(g > 0.0, ranks[at : at + 1, :], -1.0).astype(jnp.int32)
            mask = slots == slot
            pick = jnp.where(mask, 1.0, 0.0).astype(BF)
            masks[b, e] = mask
            picks[b, e] = pick
            gs[b, e] = jnp.sum(jnp.where(mask, g, 0.0), axis=1, keepdims=True)
            rows = slice(b * cap, (b + 1) * cap)
            xr_ref[e, rows, :] = dot(pick, pays[b][0:tok, :]).astype(BF)
            gr_ref[e, rows, :] = dot(pick, grads[b][...]).astype(BF)
    copies = []

    def save(j, e, ref):
        copy = pltpu.make_async_copy(
            ref.at[e], saved[j].at[e, pl.ds(first * cap, nb * cap), :], sems.at[j, e]
        )
        copy.start()
        copies.append(copy)

    for copy in sums:
        copy.wait()
    wide_f = sdn_ref.shape[0]
    s_in, s_out = [], []
    for b in range(nb):
        act_b = pays[b][0:tok, :]
        grad_b = grads[b][...]
        sgu = dot(act_b, sgu_ref[...])
        shu = dot_nt(grad_b, sdn_ref[...])
        sg = sgu[:, 0:wide_f]
        su = sgu[:, wide_f : 2 * wide_f]
        sig = sigmoid(sg)
        sact = sg * sig
        sh = (sact * su).astype(BF)
        sd = jnp.concatenate([shu * su * (sig + sact * (1.0 - sig)), shu * sact], axis=1).astype(BF)
        s_out.append(dot(sh, sdn_ref[...]))
        s_in.append(dot_nt(sd, sgu_ref[...]))
        dgu_b = dot_tn(act_b, sd)
        ddn_b = dot_tn(sh, grad_b)
        if aliased or b > 0:
            agu_ref[...] += dgu_b
            adn_ref[...] += ddn_b
        else:
            agu_ref[...] = dgu_b
            adn_ref[...] = ddn_b
    stores = [
        pltpu.make_async_copy(agu_ref, saved[4], sems_a.at[0]),
        pltpu.make_async_copy(adn_ref, saved[5], sems_a.at[1]),
    ]
    for copy in stores:
        copy.start()
        copies.append(copy)
    ggm = [jnp.zeros((n_exp, tok), F32) for _ in range(nb)]
    xis, yos = [], []
    for e in range(n_loc):
        save(0, e, xr_ref)
        save(1, e, gr_ref)
        loads[e][0].wait()
        loads[e][1].wait()
        egu = dot(xr_ref[e], wgu_ref[e])
        loads[e][2].wait()
        hu = dot_nt(gr_ref[e], wd_ref[e])
        gate = jnp.concatenate([gs[b, e] for b in range(nb)], axis=0)
        eg = egu[:, 0:ff]
        eu = egu[:, ff:ff2]
        sig = sigmoid(eg)
        act = eg * sig
        h = act * eu
        gg = jnp.sum(h.astype(BF).astype(F32) * hu, axis=1, keepdims=True)
        gh_ref[e] = (gate * h).astype(BF)
        save(2, e, gh_ref)
        hg = gate * hu
        dgu_ref[e, :, 0:ff] = (hg * eu * (sig + act * (1.0 - sig))).astype(BF)
        dgu_ref[e, :, ff:ff2] = (hg * act).astype(BF)
        save(3, e, dgu_ref)
        yos.append(dot(gh_ref[e], wd_ref[e]).astype(BF))
        xis.append(dot_nt(dgu_ref[e], wgu_ref[e]).astype(BF))
        for b in range(nb):
            row = jnp.sum(jnp.where(masks[b, e], gg[b * cap : (b + 1) * cap], 0.0), axis=0, keepdims=True)
            ggm[b] = ggm[b] + jnp.where(rowid == scal_ref[e], row, 0.0)
    for b in range(nb):
        rows = slice(b * cap, (b + 1) * cap)
        pick = jnp.concatenate([picks[b, e] for e in range(n_loc)], axis=0)
        in_rows = dot_tn(pick, jnp.concatenate([v[rows] for v in xis], axis=0))
        out_rows = dot_tn(pick, jnp.concatenate([v[rows] for v in yos], axis=0))
        in_refs[b][0:tok, :] = (in_rows + s_in[b]).astype(BF)
        out_refs[b][...] = (out_rows + s_out[b]).astype(BF)
        high = ggm[b].astype(BF)
        in_refs[b][tok : tok + n_exp, :] = jnp.zeros((n_exp, d), BF)
        in_refs[b][tok : tok + n_exp, 0:tok] = high
        in_refs[b][tok : tok + n_exp, tok : 2 * tok] = (ggm[b] - high.astype(F32)).astype(BF)
    for copy in copies:
        copy.wait()


def expert_call(first, nb, cap, n_exp, scal, pays, grads, weights, saved):
    extra, d = pays[0].shape
    tok = grads[0].shape[0]
    n_loc, _, ff = weights[0].shape
    wide_f = weights[4].shape[0]
    rows = cap * (extra - tok) // n_loc
    saved_shapes = (
        hbm((n_loc, rows, d), BF),
        hbm((n_loc, rows, d), BF),
        hbm((n_loc, rows, ff), BF),
        hbm((n_loc, rows, 2 * ff), BF),
        hbm((d, 2 * wide_f), F32),
        hbm((wide_f, d), F32),
    )
    outs = pl.pallas_call(
        functools.partial(expert_block, first, nb, cap, n_exp, len(saved)),
        out_shape=saved_shapes + (shape((extra, d), BF),) * nb + (shape((tok, d), BF),) * nb,
        in_specs=[whole(SMEM)]
        + [whole()] * (2 * nb)
        + [far()] * 3
        + [whole()] * 2
        + [far()] * len(saved),
        out_specs=[far()] * 6 + [whole()] * (2 * nb),
        scratch_shapes=[
            VMEM((n_loc, d, 2 * ff), BF),
            VMEM((n_loc, ff, d), BF),
            VMEM((n_loc, nb * cap, d), BF),
            VMEM((n_loc, nb * cap, d), BF),
            VMEM((n_loc, nb * cap, ff), BF),
            VMEM((n_loc, nb * cap, 2 * ff), BF),
            VMEM((d, 2 * wide_f), F32),
            VMEM((wide_f, d), F32),
            pltpu.SemaphoreType.DMA((n_loc, 3)),
            pltpu.SemaphoreType.DMA((4, n_loc)),
            pltpu.SemaphoreType.DMA((2,)),
        ],
        input_output_aliases={1 + 2 * nb + 5 + j: j for j in range(len(saved))},
        compiler_params=params(40),
        cost_estimate=cost(nb * cap * n_loc * d * ff * 12, 3 * n_loc * d * ff * 2),
        name="expert_block",
    )(scal, *pays, *grads, *weights, *saved)
    return outs[:6], list(outs[6 : 6 + nb]), list(outs[6 + nb :])


def attn_backward(
    n_exp, gidx_ref, hid_ref, grad_ref, segc_ref, segr_ref, cos_ref, sin_ref, gate_ref, gains_ref,
    rs_ref, own_ref, *rest
):
    n = gidx_ref.shape[0]
    store, pay_hbm, res_hbm = rest[:3]
    ig_ref, mine_ref, first_ref, soon_ref, later_ref, w_ref, dw_ref, dq_ref, dk_ref, dv_ref = rest[3:13]
    xn_ref, q_ref, k_ref, v_ref, att_ref, pay_ref, res_ref, sems_in, sems_out = rest[13:]
    height = mine_ref.shape[1]
    tok, d = hid_ref.shape
    sources = [store.at[stored_at(i, tok, d)] for i in range(5)] + [pay_hbm, res_hbm]
    targets = [xn_ref, q_ref, k_ref, v_ref, att_ref, pay_ref, res_ref]
    for lo, hi in ((3 * d, w_ref.shape[1]), (0, 3 * d)):
        sources.append(store.at[0:d, lo:hi])
        targets.append(w_ref.at[:, lo:hi])
    loads = [
        pltpu.make_async_copy(src, ref, sems_in.at[i])
        for i, (src, ref) in enumerate(zip(sources, targets))
    ]
    for i in (5, 6, 7, 4, 1, 2, 3):
        loads[i].start()
    loads[5].wait()
    gains = gains_ref[...]
    gain1 = gains[0:1, :]
    gain2 = gains[1:2, :]
    rows = rs_ref[...].astype(F32) + own_ref[...].astype(F32)
    tail = rows[tok : tok + n_exp, :]
    ggt = tail[:, 0:tok] + tail[:, tok : 2 * tok]
    ggt = jnp.concatenate([ggt, jnp.zeros((LANES - n_exp, tok), F32)], axis=0)
    gg = ggt.T
    gate = gate_ref[...]
    picked = gate * (gg - jnp.sum(gate * gg, axis=1, keepdims=True))
    logit_grad = picked.astype(BF)
    act_t = pay_ref[0:tok, :].T
    aux_grad = dot(act_t, logit_grad)
    grad = grad_ref[...].astype(F32)
    loads[6].wait()
    res = res_ref[...]
    inv2 = lax.rsqrt(jnp.mean(res * res, axis=1, keepdims=True) + EPS)
    loads[7].wait()
    loads[0].start()
    loads[8].start()
    moe_in = rows[0:tok, :] + dot_nt(logit_grad, w_ref[:, 4 * d : 4 * d + LANES])
    weighted = moe_in * gain2
    gg2 = jnp.sum(moe_in * res * inv2, axis=0, keepdims=True)
    inner = jnp.mean(weighted * res, axis=1, keepdims=True)
    rgrad = grad + inv2 * weighted - res * (inv2 * inv2 * inv2 * inner)
    low = rgrad.astype(BF)
    for i in (4, 1, 2, 3):
        loads[i].wait()
    dw_ref[:, 3 * d : 4 * d] = dot(att_ref[...].T, low).astype(BF)
    allowed = allowed_mask(segc_ref[...], segr_ref[...])
    cos = cos_ref[...]
    sin = sin_ref[...]
    scale = HD ** -0.5
    pair = 2 * HD
    for c in range(0, d, pair):
        agp = dot_nt(low, w_ref[c : c + pair, 3 * d : 4 * d]).astype(BF)
        for o in range(0, pair, HD):
            cols = slice(c + o, c + o + HD)
            q = q_ref[:, cols]
            k = k_ref[:, cols]
            ag = agp[:, o : o + HD]
            probs = head_probs(q, k, allowed)
            dv_ref[:, cols] = dot_tn(probs.astype(BF), ag).astype(BF)
            dp = dot_nt(ag, v_ref[:, cols])
            ds = (probs * (dp - jnp.sum(probs * dp, axis=1, keepdims=True))).astype(BF)
            dq = dot(ds, k) * scale
            dk = dot_tn(ds, q) * scale
            dq_ref[:, cols] = rope_back(dq, cos, sin).astype(BF)
            dk_ref[:, cols] = rope_back(dk, cos, sin).astype(BF)
    loads[8].wait()
    loads[0].wait()
    back = dot_nt(dq_ref[...], w_ref[:, 0:d])
    back += dot_nt(dk_ref[...], w_ref[:, d : 2 * d])
    back += dot_nt(dv_ref[...], w_ref[:, 2 * d : 3 * d])
    x = hid_ref[...].astype(F32)
    inv = lax.rsqrt(jnp.mean(x * x, axis=1, keepdims=True) + EPS)
    weighted = back * gain1
    gg1 = jnp.sum(back * x * inv, axis=0, keepdims=True)
    inner = jnp.mean(weighted * x, axis=1, keepdims=True)
    ig_ref[...] = rgrad + inv * weighted - x * (inv * inv * inv * inner)
    rowid = lax.broadcasted_iota(jnp.int32, (LANES, d), 0)
    gain_rows = jnp.where(rowid == n_exp, gg1, 0.0) + jnp.where(rowid == n_exp + 1, gg2, 0.0)
    dw_ref[:, 4 * d : 4 * d + LANES] = (aux_grad + gain_rows.T).astype(BF)
    xn_t = xn_ref[...].T
    dw_ref[:, 0:d] = dot(xn_t, dq_ref[...]).astype(BF)
    dw_ref[:, d : 2 * d] = dot(xn_t, dk_ref[...]).astype(BF)
    dw_ref[:, 2 * d : 3 * d] = dot(xn_t, dv_ref[...]).astype(BF)
    half = n // 2
    outs = []
    for i in range(n):
        start = pl.multiple_of(gidx_ref[i] * height, 16)
        out = mine_ref.at[i] if i < half else first_ref
        if i > half:
            at = i - half - 1
            soon = soon_ref.shape[0]
            out = soon_ref.at[at] if at < soon else later_ref.at[at - soon]
        copy = pltpu.make_async_copy(dw_ref.at[pl.ds(start, height), :], out, sems_out.at[i])
        copy.start()
        outs.append(copy)
    for copy in outs:
        copy.wait()


def body(
    nd,
    ne,
    hidden_in,
    out_grad,
    segment_ids,
    routes,
    attn_gain,
    w_query,
    w_key,
    w_value,
    w_out,
    moe_gain,
    w_router,
    shared_gate,
    shared_up,
    shared_down,
    expert_gate,
    expert_up,
    expert_down,
):
    tok, d = hidden_in.shape
    n_exp = w_router.shape[1]
    n_loc = expert_gate.shape[0]
    ff = expert_gate.shape[2]
    top_k = routes.shape[1]
    cap = min(tok, 8 * ((10 * tok * top_k + 56 * n_exp - 1) // (56 * n_exp)))
    extra = tok + n_exp
    hr = d // ne // 2
    hdn = shared_down.shape[0]
    wide = 4 * d + LANES

    me = lax.axis_index("expert")
    core = lax.axis_index("dp") % 2
    perm = ring_perm(nd, ne)
    both = ("dp", "expert")

    def ring(v):
        return lax.ppermute(v, both, perm)

    def after(v, *others):
        return lax.optimization_barrier((v,) + others)[0]

    def swap(v, bit):
        return lax.ppermute(v, "dp", [(i, i ^ bit) for i in range(nd)])

    table = jnp.asarray(ring_order(ne))
    mine_order = lax.dynamic_slice(table, (core, me, 0), (1, 1, ne)).reshape(ne)
    other_order = lax.dynamic_slice(table, (1 - core, me, 0), (1, 1, ne)).reshape(ne)
    idx = jnp.concatenate([mine_order * 2 + core, other_order * 2 + 1 - core])
    gidx = jnp.concatenate(
        [jnp.roll(mine_order, -1) * 2 + core, jnp.roll(other_order, -1) * 2 + 1 - core]
    )
    scal = jnp.stack([me * n_loc + 1 - core, me * n_loc + core, 1 - core, core]).astype(jnp.int32)

    def fence(*vs):
        return list(lax.optimization_barrier(tuple(vs)))

    def halves(v):
        v = v.reshape(2, v.shape[0] // 2, v.shape[1])
        return (
            lax.dynamic_index_in_dim(v, core, 0, False),
            lax.dynamic_index_in_dim(v, 1 - core, 0, False),
        )

    units = ff // ne
    wide_f = -(-units // LANES) * LANES

    def spread(v):
        v = v.reshape(v.shape[0], ne, units).transpose(1, 0, 2)
        return jnp.pad(v, ((0, 0), (0, 0), (0, wide_f - units)))

    def exchange(v):
        return lax.all_to_all(v, "expert", split_axis=0, concat_axis=0, tiled=True)

    expert_gate, expert_up, expert_down = (
        pltpu.with_memory_space_constraint(v, pltpu.HBM) for v in (expert_gate, expert_up, expert_down)
    )
    sgu = jnp.concatenate([spread(halves(shared_gate)[0]), spread(halves(shared_up)[0])], axis=2)
    sdn = jnp.pad(shared_down, ((0, wide_f - units), (0, 0)))

    split = 2 * d
    aux = jnp.concatenate(
        [
            w_router,
            attn_gain[:, None],
            moe_gain[:, None],
            jnp.zeros((w_router.shape[0], LANES - n_exp - 2), BF),
        ],
        axis=1,
    )
    left, left_other = (jnp.concatenate(v, axis=1) for v in zip(halves(w_query), halves(w_key)))
    right, right_other = (
        jnp.concatenate(v, axis=1) for v in zip(halves(w_value), halves(w_out), halves(aux))
    )
    store_shape = (hbm((d + 2 * tok, wide), BF),)
    kinds = [(0, 0), (0, split)] * 2
    store = place_call(
        kinds, [0, 0, ne, ne], idx, [left, right, left_other, right_other], store_shape, ()
    )
    for i in range(1, ne):
        left = ring(left)
        right = ring(right)
        if i == 2:
            left, sgu = fence(left, sgu)
            sgu = exchange(sgu)
        if i == 4:
            left, sgu, sdn = fence(left, sgu, sdn)
            sgu = jnp.stack([sgu, swap(sgu, 1)])
            sgu = jnp.where(core == 0, sgu, sgu[::-1]).transpose(1, 0, 2, 3).reshape(d, 2 * wide_f)
        if i == 6:
            left, sgu = fence(left, sgu)
        if i + 1 < ne:
            placed = place_call(
                kinds, [i, i, ne + i, ne + i], idx, [left, right, swap(left, 1), swap(right, 1)], store_shape, store
            )
            left = fence(left, *store)[0]
            right = fence(right, *store)[0]
        else:
            left, right, *store = fence(left, right, *store)
            placed = place_call(
                kinds, [i, i, ne + i, ne + i], idx, [left, right, swap(left, 1), swap(right, 1)], store_shape, store
            )
        store = placed

    half = HD // 2
    freq = ROPE_BASE ** (-2.0 * np.arange(half) / HD)
    ang = np.arange(tok)[:, None] * freq[None, :]
    cos = jnp.asarray(np.concatenate([np.cos(ang), np.cos(ang)], 1).astype(np.float32))
    sin = jnp.asarray(np.concatenate([-np.sin(ang), np.sin(ang)], 1).astype(np.float32))
    seg_row = segment_ids
    seg_col = segment_ids.reshape(tok, 1)

    g0, left, right = fence(out_grad, left, right)
    grads = [g0, ring(g0)]
    store, res, gate, pay, gains = pl.pallas_call(
        functools.partial(attn_forward, n_exp),
        out_shape=store_shape
        + (
            hbm((tok, d), F32),
            hbm((tok, LANES), F32),
            shape((extra, d), BF),
            shape((8, d), F32),
        ),
        in_specs=[whole()] * 6 + [far()],
        out_specs=[far()] * 3 + [whole()] * 2,
        scratch_shapes=[VMEM((d, wide), BF)]
        + [VMEM((tok, d), BF)] * 5
        + [
            VMEM((tok, d), F32),
            VMEM((tok, LANES), F32),
            pltpu.SemaphoreType.DMA((5,)),
            pltpu.SemaphoreType.DMA((7,)),
        ],
        input_output_aliases={6: 0},
        compiler_params=params(36),
        cost_estimate=cost(2 * tok * d * d * 4, d * wide * 2),
        name="attn_forward",
    )(hidden_in, seg_col, seg_row, routes, cos, sin, *store)
    pay, grads[1] = fence(pay, grads[1])

    def start_flow(parts):
        return {"parts": parts, "at": 0, "acc": parts(0).astype(BF)}

    def advance(flow, got):
        flow["at"] += 1
        if flow["at"] == ne - 1:
            flow["got"] = got
        else:
            flow["acc"] = (got.astype(F32) + flow["parts"](flow["at"])).astype(BF)

    def ring_total(flow):
        return flow["got"].astype(F32) + flow["parts"](ne - 1)

    def token_parts(parts):
        return lambda i: parts[(i + 1) % ne].astype(F32)

    def dense_parts(mine, others):
        def part(i):
            at = i
            for group in others:
                if at < group.shape[0]:
                    return mine[i].astype(F32) + group[at].astype(F32)
                at -= group.shape[0]

        return part

    down_shapes = (hbm((n_loc, ff, d), F32),)
    gu_shapes = (hbm((n_loc, d, ff), F32),) * 2
    n_down, n_gu = 4, 8
    waiting, landed, shared_out = [], [], []
    finished = {"down": (), "gu": ()}

    def queue(name, low, count):
        height = low.shape[0] // count
        for j in range(count):
            waiting.append((name, j * height, lax.slice_in_dim(low, j * height, (j + 1) * height)))

    def across(low):
        return swap(low, 2) if nd > 2 else low * 0

    def summed(low, more):
        total = low.astype(F32) + more.astype(F32)
        bit = 4
        while bit < nd:
            low = total.astype(BF)
            total = low.astype(F32) + swap(low, bit).astype(F32)
            bit *= 2
        return total.astype(BF)

    def emit():
        names = set()
        for name, start, mine, other in shared_out:
            if name not in finished:
                held[name] = (start, mine, other)
                continue
            shapes = down_shapes if name == "down" else gu_shapes
            finished[name] = emit_call(start, scal, mine, other, shapes, finished[name])
            names.add(name)
        shared_out.clear()
        return sorted(names)

    held = {}

    def slot(flows=(), sends=(), swaps=(), cross=0, compute=None, keep=(), ready=None, write=True, joint=True):
        chunks = waiting[:cross]
        del waiting[:cross]
        summing = [(name, start, summed(low, more)) for (name, start, low), more in landed]
        landed.clear()
        moved = [ring(f["acc"]) for f in flows] + [ring(v) for v in sends]
        moved += [across(low) for _, _, low in chunks]
        moved += [swap(v, 1) for v in swaps]
        moved += [swap(mine, 1) for _, _, mine in summing]
        names = emit() if write else []
        done = list(compute()) if compute is not None else []
        late = [v for name in names for v in finished[name]]
        if joint:
            out = fence(*moved, *done, *keep, *late)
        else:
            done = fence(*done)
            out = [fence(v, done[0])[0] for v in moved] + done

        def pop(count):
            first = out[:count]
            del out[:count]
            return first

        arrived = pop(len(flows))
        sent = pop(len(sends))
        landed.extend(zip(chunks, pop(len(chunks))))
        swapped = pop(len(swaps))
        if ready is not None:
            ready(swapped)
        for f, got in zip(flows, arrived):
            advance(f, got)
        for (name, start, mine), other in zip(summing, pop(len(summing))):
            shared_out.append((name, start, mine, other))
        done = pop(len(done))
        kept = pop(len(keep))
        for name in names:
            finished[name] = tuple(pop(len(finished[name])))
        return sent, swapped, done, kept

    pays = [pay]
    saved = ()
    in_parts, out_parts = [], []
    flow_in = None
    for i in range(ne):
        sends = []
        if i + 1 < ne:
            sends.append(pays[i])
        if i + 2 < ne:
            sends.append(grads[i + 1])
        if i == ne - 2:
            flow_in = start_flow(token_parts(in_parts))

        def block(i=i):
            new, ins, outs = expert_call(
                i, 1, cap, n_exp, scal, pays[i : i + 1], grads[i : i + 1],
                (expert_gate, expert_up, expert_down, sgu, sdn), saved,
            )
            held["saved"] = new
            return [ins[0], outs[0]]

        sent, _, done, _ = slot([flow_in] if flow_in else [], sends, compute=block, joint=False)
        saved = held["saved"]
        in_parts.append(done[0])
        out_parts.append(done[1])
        if i + 1 < ne:
            pays.append(sent[0])
        if i + 2 < ne:
            grads.append(sent[-1])

    xr, gr, gh, dgu, sum_gu, sum_dn = saved
    hw = d // 2
    gu_halves = sum_gu.astype(BF).reshape(ne, 2, hr, 2 * wide_f).transpose(1, 0, 2, 3)
    dn_halves = sum_dn[0:units].astype(BF).reshape(units, 2, hw).transpose(1, 0, 2)

    def of_side(v, side):
        return lax.dynamic_index_in_dim(v, side, 0, False)

    flow_out = start_flow(token_parts(out_parts))
    _, (gu_more, dn_more), (down_t,), _ = slot(
        [flow_in, flow_out],
        swaps=[of_side(gu_halves, 1 - core), of_side(dn_halves, 1 - core)],
        compute=lambda: [dot_tn(gh[0], gr[0]).astype(BF)],
    )

    def add(left, right):
        return (left.astype(F32) + right.astype(F32)).astype(BF)

    _, (down_got,), (down_m,), _ = slot(
        [flow_in, flow_out], swaps=[down_t], compute=lambda: [dot_tn(gh[1], gr[1]).astype(BF)]
    )
    queue("down", add(down_m, down_got), n_down)
    _, _, (gu_t,), _ = slot(
        [flow_in, flow_out], cross=1, compute=lambda: [dot_tn(xr[0], dgu[0]).astype(BF)]
    )
    _, _, (gu_m,), _ = slot(
        [flow_in, flow_out], cross=1, compute=lambda: [dot_tn(xr[1], dgu[1]).astype(BF)]
    )
    _, (gu_got,), _, _ = slot([flow_in], swaps=[gu_t], cross=1)
    while flow_in["at"] < ne - 1:
        slot([flow_in])
    height = d // n_gu
    for j in range(n_gu):
        cut_rows = slice(j * height, (j + 1) * height)
        waiting.append(("gu", j * height, add(gu_m[cut_rows], gu_got[cut_rows])))
    waiting.insert(2, ("sgu", 0, add(of_side(gu_halves, core), gu_more)))
    waiting.insert(3, ("sdn", 0, add(of_side(dn_halves, core), dn_more)))
    rs_in = flow_in["got"]

    soon = 3

    def backward():
        return pl.pallas_call(
            functools.partial(attn_backward, n_exp),
            out_shape=(
                shape((tok, d), F32),
                hbm((ne, hr, wide), BF),
                hbm((hr, wide), BF),
                hbm((soon, hr, wide), BF),
                hbm((ne - 1 - soon, hr, wide), BF),
            ),
            in_specs=[whole(SMEM)] + [whole()] * 10 + [far()] * 3,
            out_specs=[whole()] + [far()] * 4,
            scratch_shapes=[
                VMEM((d, wide), BF),
                VMEM((d, wide), BF),
            ]
            + [VMEM((tok, d), BF)] * 8
            + [
                VMEM((extra, d), BF),
                VMEM((tok, d), F32),
                pltpu.SemaphoreType.DMA((9,)),
                pltpu.SemaphoreType.DMA((2 * ne,)),
            ],
            compiler_params=params(56),
            cost_estimate=cost(2 * tok * d * d * 8, 2 * d * wide * 2),
            name="attn_backward",
        )(
            gidx, hidden_in, out_grad, seg_col, seg_row, cos, sin, gate, gains, rs_in, in_parts[0],
            store, pay, res,
        )

    _, _, (input_grad, d_mine, d_first, d_soon, d_later), _ = slot(
        [flow_out], cross=2, compute=backward, write=False
    )
    others = [swap(d_first, 1)[None]]
    flow_d = start_flow(dense_parts(d_mine, others))
    slot([flow_d], swaps=[d_soon], cross=2, ready=others.extend)
    slot([flow_d], swaps=[d_later], cross=1, ready=others.extend)

    def shared_exchange():
        if "sgu" in held and "sgu_sent" not in held:
            _, mine, _ = held["sgu"]
            held["sgu_sent"] = True
            return [exchange(mine)]
        return []

    pick = core == 0

    def sides(name):
        _, mine, other = held[name]
        mine = mine.astype(F32)
        other = other.astype(F32)
        return jnp.where(pick, mine, other), jnp.where(pick, other, mine)

    def row_halves():
        held["rows"] = (0, held["spread"], held["spread_other"])
        both_rows = jnp.concatenate(sides("rows"), axis=1)
        g_gate = both_rows[:, :, 0:units].transpose(1, 0, 2).reshape(2 * hr, ff)
        g_up = both_rows[:, :, wide_f : wide_f + units].transpose(1, 0, 2).reshape(2 * hr, ff)
        return [g_gate, g_up]

    while flow_d["at"] < ne - 1:
        ready_rows = "spread_other" in held and "gate_up" not in held
        swaps = [held["spread"]] if "spread" in held and "spread_other" not in held else []
        _, swapped, got, _ = slot(
            [flow_d], swaps=swaps, cross=1, compute=row_halves if ready_rows else shared_exchange
        )
        if ready_rows:
            held["gate_up"] = got
        elif got:
            held["spread"] = got[0]
        if swapped:
            held["spread_other"] = swapped[0]
    low = ring_total(flow_d).astype(BF)
    first_rows = -(-hr // 32) * 16
    waiting.append(("dense0", 0, low[0:first_rows]))
    waiting.append(("dense1", 0, low[first_rows:hr]))
    while waiting or landed or flow_out["at"] < ne - 1:
        slot([flow_out] if flow_out["at"] < ne - 1 else [], cross=1)
    emit()

    output = res + flow_out["got"].astype(F32) + out_parts[0].astype(F32)
    upper, lower = sides("dense0"), sides("dense1")
    g_d = jnp.concatenate([upper[0], lower[0], upper[1], lower[1]], axis=0)
    g_gate, g_up = held["gate_up"]
    g_dn = jnp.concatenate(sides("sdn"), axis=1)
    (down_w,) = finished["down"]
    gate_w, up_w = finished["gu"]
    return (
        output,
        input_grad,
        g_d[:, 4 * d + n_exp],
        g_d[:, 0:d],
        g_d[:, d : 2 * d],
        g_d[:, 2 * d : 3 * d],
        g_d[:, 3 * d : 4 * d],
        g_d[:, 4 * d + n_exp + 1],
        g_d[:, 4 * d : 4 * d + n_exp],
        g_gate,
        g_up,
        g_dn,
        gate_w,
        up_w,
        down_w,
    )


def solution(mesh):
    nd = mesh.shape["dp"]
    ne = mesh.shape["expert"]
    tokens = P(("dp", "expert"), None)
    vector = P("expert")
    matrix = P("expert", None)
    cube = P("expert", None, None)
    return jax.shard_map(
        functools.partial(body, nd, ne),
        mesh=mesh,
        in_specs=(tokens,) * 4
        + (vector, matrix, matrix, matrix, matrix, vector)
        + (matrix,) * 4
        + (cube,) * 3,
        out_specs=(tokens, tokens, vector, matrix, matrix, matrix, matrix, vector)
        + (matrix,) * 4
        + (cube,) * 3,
        check_vma=False,
    )
```

```python
import functools

import jax
import jax.numpy as jnp
import numpy as np
from jax import lax
from jax.experimental import pallas as pl
from jax.experimental.pallas import tpu as pltpu
from jax.sharding import PartitionSpec as P

HD = 128
LANES = 128
EPS = 1e-06
ROPE_BASE = 10000.0
MASKED = -1e30
BF = jnp.bfloat16
F32 = jnp.float32
VMEM = pltpu.VMEM
SMEM = pltpu.SMEM
MIB = 1 << 20


def dot(a, b):
    return jnp.dot(a, b, preferred_element_type=F32)


def dot_nt(a, b):
    return lax.dot_general(a, b, (((1,), (1,)), ((), ())), preferred_element_type=F32)


def dot_tn(a, b):
    return lax.dot_general(a, b, (((0,), (0,)), ((), ())), preferred_element_type=F32)


def sigmoid(v):
    return 1.0 / (1.0 + jnp.exp(-v))


def whole(space=VMEM):
    return pl.BlockSpec(memory_space=space)


def anywhere():
    return pl.BlockSpec(memory_space=pl.ANY)


def far():
    return pl.BlockSpec(memory_space=pltpu.HBM)


def params(mib):
    return pltpu.CompilerParams(vmem_limit_bytes=mib * MIB)


def cost(flops, nbytes):
    return pl.CostEstimate(flops=int(flops), bytes_accessed=int(nbytes), transcendentals=0)


def shape(dims, dtype):
    return jax.ShapeDtypeStruct(dims, dtype)


def hbm(dims, dtype):
    return pltpu.HBM(dims, dtype)


def cycle(n):
    return list(range(0, n, 2)) + list(range(1, n, 2))[::-1]


def ring_perm(nd, ne, planes=False):
    ring = cycle(ne)
    pos = {e: i for i, e in enumerate(ring)}
    pairs = []
    for d in range(nd):
        for e in range(ne):
            step = 1 if (d + (d // 2 if planes else 0)) % 2 == 0 else -1
            pairs.append((d * ne + e, d * ne + ring[(pos[e] + step) % ne]))
    return pairs


def ring_order(ne):
    ring = cycle(ne)
    pos = {e: i for i, e in enumerate(ring)}
    table = np.zeros((2, ne, ne), np.int32)
    for c in range(2):
        step = 1 if c == 0 else -1
        for e in range(ne):
            for s in range(ne):
                table[c, e, s] = ring[(pos[e] - step * s) % ne]
    return table


def place_pieces(kinds, spots, aliased, idx_ref, *refs):
    n = len(kinds)
    pieces = refs[:n]
    outs = refs[n + aliased : -1]
    sems = refs[-1]
    copies = []
    for i, (target, col) in enumerate(kinds):
        height, width = pieces[i].shape
        start = pl.multiple_of(idx_ref[spots[i]] * height, 16)
        dst = outs[target].at[pl.ds(start, height), col : col + width]
        copies.append(pltpu.make_async_copy(pieces[i], dst, sems.at[i]))
    for copy in copies:
        copy.start()
    for copy in copies:
        copy.wait()


def place_call(kinds, spots, idx, pieces, targets, into):
    n = len(kinds)
    return pl.pallas_call(
        functools.partial(place_pieces, kinds, spots, len(into)),
        out_shape=targets,
        in_specs=[whole(SMEM)] + [whole()] * n + [far()] * len(into),
        out_specs=[far()] * len(targets),
        scratch_shapes=[pltpu.SemaphoreType.DMA((n,))],
        input_output_aliases={1 + n + j: j for j in range(len(into))},
        compiler_params=params(8),
        cost_estimate=cost(0, sum(p.size for p in pieces) * 4),
        name="place_pieces",
    )(idx, *pieces, *into)


def emit_rows(start, aliased, scal_ref, mine_ref, other_ref, *refs):
    outs = refs[aliased : -2]
    buf, sems = refs[-2:]
    height = mine_ref.shape[0]
    width = outs[0].shape[2]
    buf[0] = mine_ref[...].astype(F32)
    buf[1] = other_ref[...].astype(F32)
    copies = []
    for side in range(2):
        expert = scal_ref[3 - side]
        for j, out in enumerate(outs):
            copies.append(
                pltpu.make_async_copy(
                    buf.at[side, :, j * width : (j + 1) * width],
                    out.at[expert, pl.ds(start, height), :],
                    sems.at[side, j],
                )
            )
    for copy in copies:
        copy.start()
    for copy in copies:
        copy.wait()


def emit_call(start, scal, mine, other, targets, into):
    return pl.pallas_call(
        functools.partial(emit_rows, start, len(into)),
        out_shape=targets,
        in_specs=[whole(SMEM)] + [whole()] * 2 + [far()] * len(into),
        out_specs=[far()] * len(targets),
        scratch_shapes=[
            VMEM((2,) + mine.shape, F32),
            pltpu.SemaphoreType.DMA((2, len(targets))),
        ],
        input_output_aliases={3 + j: j for j in range(len(into))},
        compiler_params=params(12),
        cost_estimate=cost(0, mine.size * 12),
        name="emit_rows",
    )(scal, mine, other, *into)


def stored_at(i, tok, d):
    row = d + tok * (i // 4)
    col = d * (i % 4)
    return slice(row, row + tok), slice(col, col + d)


def rope(u, cos, sin):
    return u * cos + pltpu.roll(u, HD // 2, 1) * sin


def rope_back(u, cos, sin):
    return u * cos - pltpu.roll(u, HD // 2, 1) * sin


def allowed_mask(seg_col, seg_row):
    n = seg_row.shape[1]
    rows = lax.broadcasted_iota(jnp.int32, (n, n), 0)
    cols = lax.broadcasted_iota(jnp.int32, (n, n), 1)
    return (seg_col == seg_row) & (cols <= rows)


def head_probs(q, k, allowed):
    s = dot_nt(q, k) * (HD ** -0.5)
    s = jnp.where(allowed, s, MASKED)
    e = jnp.exp(s - jnp.max(s, axis=1, keepdims=True))
    return e / jnp.sum(e, axis=1, keepdims=True)


def attn_forward(n_exp, hid_ref, segc_ref, segr_ref, routes_ref, cos_ref, sin_ref, store_in, *rest):
    store, res_hbm, gate_hbm, pay_ref, gains_ref, w_ref, xn_ref, q_ref, k_ref, v_ref, att_ref = rest[:11]
    res_ref, gate_ref, sems, sems_out = rest[11:]
    tok, d = hid_ref.shape
    wide = w_ref.shape[1]
    saves = [
        pltpu.make_async_copy(ref, store.at[stored_at(i, tok, d)], sems_out.at[i])
        for i, ref in enumerate((xn_ref, q_ref, k_ref, v_ref, att_ref))
    ]
    saves.append(pltpu.make_async_copy(res_ref, res_hbm, sems_out.at[5]))
    saves.append(pltpu.make_async_copy(gate_ref, gate_hbm, sems_out.at[6]))
    spans = [(4 * d, wide)] + [(i * d, (i + 1) * d) for i in range(4)]
    loads = [
        pltpu.make_async_copy(store.at[0:d, lo:hi], w_ref.at[:, lo:hi], sems.at[i])
        for i, (lo, hi) in enumerate(spans)
    ]
    for load in loads:
        load.start()
    x = hid_ref[...].astype(F32)
    inv = lax.rsqrt(jnp.mean(x * x, axis=1, keepdims=True) + EPS)
    cos = cos_ref[...]
    sin = sin_ref[...]
    allowed = allowed_mask(segc_ref[...], segr_ref[...])
    loads[0].wait()
    aux = w_ref[:, 4 * d : 4 * d + LANES]
    turned = aux.astype(F32).T
    gains = turned[n_exp : n_exp + 8, :]
    gains_ref[...] = gains
    xn = (x * inv * gains[0:1, :]).astype(BF)
    xn_ref[...] = xn
    saves[0].start()
    pair = 2 * HD
    for j, ref in ((0, q_ref), (1, k_ref)):
        loads[1 + j].wait()
        for c in range(0, d, pair):
            pre = dot(xn, w_ref[:, j * d + c : j * d + c + pair])
            for o in range(0, pair, HD):
                ref[:, c + o : c + o + HD] = rope(pre[:, o : o + HD], cos, sin).astype(BF)
    loads[3].wait()
    for c in range(0, d, pair):
        vp = dot(xn, w_ref[:, 2 * d + c : 2 * d + c + pair]).astype(BF)
        v_ref[:, c : c + pair] = vp
        for o in range(0, pair, HD):
            cols = slice(c + o, c + o + HD)
            probs = head_probs(q_ref[:, cols], k_ref[:, cols], allowed).astype(BF)
            att_ref[:, cols] = dot(probs, vp[:, o : o + HD]).astype(BF)
    for save in saves[1:5]:
        save.start()
    loads[4].wait()
    res = x + dot(att_ref[...], w_ref[:, 3 * d : 4 * d])
    res_ref[...] = res
    saves[5].start()
    inv2 = lax.rsqrt(jnp.mean(res * res, axis=1, keepdims=True) + EPS)
    act = (res * inv2 * gains[1:2, :]).astype(BF)
    logits = dot(act, aux)
    lane = lax.broadcasted_iota(jnp.int32, (tok, LANES), 1)
    routes = routes_ref[...]
    chosen = routes[:, 0:1] == lane
    for j in range(1, routes.shape[1]):
        chosen = chosen | (routes[:, j : j + 1] == lane)
    logits = jnp.where(chosen, logits, MASKED)
    e = jnp.where(chosen, jnp.exp(logits - jnp.max(logits, axis=1, keepdims=True)), 0.0)
    gate = e / jnp.sum(e, axis=1, keepdims=True)
    gate_ref[...] = gate
    saves[6].start()
    gate_t = gate.T[0:n_exp, :]
    high = gate_t.astype(BF)
    pay_ref[0:tok, :] = act
    pay_ref[tok : tok + n_exp, :] = jnp.zeros((n_exp, d), BF)
    pay_ref[tok : tok + n_exp, 0:tok] = high
    pay_ref[tok : tok + n_exp, tok : 2 * tok] = (gate_t - high.astype(F32)).astype(BF)
    for save in saves:
        save.wait()


def expert_block(first, nb, cap, n_exp, aliased, scal_ref, *refs):
    pays = refs[:nb]
    grads = refs[nb : 2 * nb]
    wg_hbm, wu_hbm, wd_hbm, sgu_ref, sdn_ref = refs[2 * nb : 2 * nb + 5]
    outs = refs[2 * nb + 5 + aliased :]
    saved = outs[:6]
    in_refs = outs[6 : 6 + nb]
    out_refs = outs[6 + nb : 6 + 2 * nb]
    wgu_ref, wd_ref, xr_ref, gr_ref, gh_ref, dgu_ref, agu_ref, adn_ref, sems_w, sems, sems_a = outs[6 + 2 * nb :]
    n_loc, _, ff2 = wgu_ref.shape
    ff = ff2 // 2
    tok, d = grads[0].shape
    loads = []
    for e in range(n_loc):
        three = (
            pltpu.make_async_copy(wg_hbm.at[scal_ref[n_loc + e]], wgu_ref.at[e, :, 0:ff], sems_w.at[e, 0]),
            pltpu.make_async_copy(wu_hbm.at[scal_ref[n_loc + e]], wgu_ref.at[e, :, ff:ff2], sems_w.at[e, 1]),
            pltpu.make_async_copy(wd_hbm.at[scal_ref[n_loc + e]], wd_ref.at[e], sems_w.at[e, 2]),
        )
        for copy in three:
            copy.start()
        loads.append(three)
    sums = []
    if aliased:
        sums.append(pltpu.make_async_copy(saved[4], agu_ref, sems_a.at[0]))
        sums.append(pltpu.make_async_copy(saved[5], adn_ref, sems_a.at[1]))
    for copy in sums:
        copy.start()
    rowid = lax.broadcasted_iota(jnp.int32, (n_exp, tok), 0)
    tri = (
        lax.broadcasted_iota(jnp.int32, (tok, tok), 0)
        < lax.broadcasted_iota(jnp.int32, (tok, tok), 1)
    )
    tri = jnp.where(tri, 1.0, 0.0).astype(BF)
    slots = lax.broadcasted_iota(jnp.int32, (cap, tok), 0)
    gates = []
    for b in range(nb):
        gt = pays[b][tok : tok + n_exp, 0:tok].astype(F32)
        gt = gt + pays[b][tok : tok + n_exp, tok : 2 * tok].astype(F32)
        for e in range(n_loc):
            gates.append(jnp.sum(jnp.where(rowid == scal_ref[e], gt, 0.0), axis=0, keepdims=True))
    used = len(gates)
    stack = jnp.concatenate(gates + [jnp.zeros((-used % 8, tok), F32)] * (used % 8 > 0), axis=0)
    ranks = dot(jnp.where(stack > 0.0, 1.0, 0.0).astype(BF), tri)
    masks, picks, gs = {}, {}, {}
    for b in range(nb):
        for e in range(n_loc):
            at = b * n_loc + e
            g = gates[at]
            slot = jnp.where(g > 0.0, ranks[at : at + 1, :], -1.0).astype(jnp.int32)
            mask = slots == slot
            pick = jnp.where(mask, 1.0, 0.0).astype(BF)
            masks[b, e] = mask
            picks[b, e] = pick
            gs[b, e] = jnp.sum(jnp.where(mask, g, 0.0), axis=1, keepdims=True)
            rows = slice(b * cap, (b + 1) * cap)
            xr_ref[e, rows, :] = dot(pick, pays[b][0:tok, :]).astype(BF)
            gr_ref[e, rows, :] = dot(pick, grads[b][...]).astype(BF)
    copies = []

    def save(j, e, ref):
        copy = pltpu.make_async_copy(
            ref.at[e], saved[j].at[e, pl.ds(first * cap, nb * cap), :], sems.at[j, e]
        )
        copy.start()
        copies.append(copy)

    for copy in sums:
        copy.wait()
    wide_f = sdn_ref.shape[0]
    s_in, s_out = [], []
    for b in range(nb):
        act_b = pays[b][0:tok, :]
        grad_b = grads[b][...]
        sgu = dot(act_b, sgu_ref[...])
        shu = dot_nt(grad_b, sdn_ref[...])
        sg = sgu[:, 0:wide_f]
        su = sgu[:, wide_f : 2 * wide_f]
        sig = sigmoid(sg)
        sact = sg * sig
        sh = (sact * su).astype(BF)
        sd = jnp.concatenate([shu * su * (sig + sact * (1.0 - sig)), shu * sact], axis=1).astype(BF)
        s_out.append(dot(sh, sdn_ref[...]))
        s_in.append(dot_nt(sd, sgu_ref[...]))
        dgu_b = dot_tn(act_b, sd)
        ddn_b = dot_tn(sh, grad_b)
        if aliased or b > 0:
            agu_ref[...] += dgu_b
            adn_ref[...] += ddn_b
        else:
            agu_ref[...] = dgu_b
            adn_ref[...] = ddn_b
    stores = [
        pltpu.make_async_copy(agu_ref, saved[4], sems_a.at[0]),
        pltpu.make_async_copy(adn_ref, saved[5], sems_a.at[1]),
    ]
    for copy in stores:
        copy.start()
        copies.append(copy)
    ggm = [jnp.zeros((n_exp, tok), F32) for _ in range(nb)]
    xis, yos = [], []
    for e in range(n_loc):
        save(0, e, xr_ref)
        save(1, e, gr_ref)
        loads[e][0].wait()
        loads[e][1].wait()
        egu = dot(xr_ref[e], wgu_ref[e])
        loads[e][2].wait()
        hu = dot_nt(gr_ref[e], wd_ref[e])
        gate = jnp.concatenate([gs[b, e] for b in range(nb)], axis=0)
        eg = egu[:, 0:ff]
        eu = egu[:, ff:ff2]
        sig = sigmoid(eg)
        act = eg * sig
        h = act * eu
        gg = jnp.sum(h.astype(BF).astype(F32) * hu, axis=1, keepdims=True)
        gh_ref[e] = (gate * h).astype(BF)
        save(2, e, gh_ref)
        hg = gate * hu
        dgu_ref[e, :, 0:ff] = (hg * eu * (sig + act * (1.0 - sig))).astype(BF)
        dgu_ref[e, :, ff:ff2] = (hg * act).astype(BF)
        save(3, e, dgu_ref)
        yos.append(dot(gh_ref[e], wd_ref[e]).astype(BF))
        xis.append(dot_nt(dgu_ref[e], wgu_ref[e]).astype(BF))
        for b in range(nb):
            row = jnp.sum(jnp.where(masks[b, e], gg[b * cap : (b + 1) * cap], 0.0), axis=0, keepdims=True)
            ggm[b] = ggm[b] + jnp.where(rowid == scal_ref[e], row, 0.0)
    for b in range(nb):
        rows = slice(b * cap, (b + 1) * cap)
        pick = jnp.concatenate([picks[b, e] for e in range(n_loc)], axis=0)
        in_rows = dot_tn(pick, jnp.concatenate([v[rows] for v in xis], axis=0))
        out_rows = dot_tn(pick, jnp.concatenate([v[rows] for v in yos], axis=0))
        in_refs[b][0:tok, :] = (in_rows + s_in[b]).astype(BF)
        out_refs[b][...] = (out_rows + s_out[b]).astype(BF)
        high = ggm[b].astype(BF)
        in_refs[b][tok : tok + n_exp, :] = jnp.zeros((n_exp, d), BF)
        in_refs[b][tok : tok + n_exp, 0:tok] = high
        in_refs[b][tok : tok + n_exp, tok : 2 * tok] = (ggm[b] - high.astype(F32)).astype(BF)
    for copy in copies:
        copy.wait()


def expert_call(first, nb, cap, n_exp, scal, pays, grads, weights, saved):
    extra, d = pays[0].shape
    tok = grads[0].shape[0]
    n_loc, _, ff = weights[0].shape
    wide_f = weights[4].shape[0]
    rows = cap * (extra - tok) // n_loc
    saved_shapes = (
        hbm((n_loc, rows, d), BF),
        hbm((n_loc, rows, d), BF),
        hbm((n_loc, rows, ff), BF),
        hbm((n_loc, rows, 2 * ff), BF),
        hbm((d, 2 * wide_f), F32),
        hbm((wide_f, d), F32),
    )
    outs = pl.pallas_call(
        functools.partial(expert_block, first, nb, cap, n_exp, len(saved)),
        out_shape=saved_shapes + (shape((extra, d), BF),) * nb + (shape((tok, d), BF),) * nb,
        in_specs=[whole(SMEM)]
        + [whole()] * (2 * nb)
        + [far()] * 3
        + [whole()] * 2
        + [far()] * len(saved),
        out_specs=[far()] * 6 + [whole()] * (2 * nb),
        scratch_shapes=[
            VMEM((n_loc, d, 2 * ff), BF),
            VMEM((n_loc, ff, d), BF),
            VMEM((n_loc, nb * cap, d), BF),
            VMEM((n_loc, nb * cap, d), BF),
            VMEM((n_loc, nb * cap, ff), BF),
            VMEM((n_loc, nb * cap, 2 * ff), BF),
            VMEM((d, 2 * wide_f), F32),
            VMEM((wide_f, d), F32),
            pltpu.SemaphoreType.DMA((n_loc, 3)),
            pltpu.SemaphoreType.DMA((4, n_loc)),
            pltpu.SemaphoreType.DMA((2,)),
        ],
        input_output_aliases={1 + 2 * nb + 5 + j: j for j in range(len(saved))},
        compiler_params=params(40),
        cost_estimate=cost(nb * cap * n_loc * d * ff * 12, 3 * n_loc * d * ff * 2),
        name="expert_block",
    )(scal, *pays, *grads, *weights, *saved)
    return outs[:6], list(outs[6 : 6 + nb]), list(outs[6 + nb :])


def attn_backward(
    n_exp, gidx_ref, hid_ref, grad_ref, segc_ref, segr_ref, cos_ref, sin_ref, gate_ref, gains_ref,
    rs_ref, own_ref, *rest
):
    n = gidx_ref.shape[0]
    store, pay_hbm, res_hbm = rest[:3]
    ig_ref, mine_ref, first_ref, soon_ref, later_ref, w_ref, dw_ref, dq_ref, dk_ref, dv_ref = rest[3:13]
    xn_ref, q_ref, k_ref, v_ref, att_ref, pay_ref, res_ref, sems_in, sems_out = rest[13:]
    height = mine_ref.shape[1]
    tok, d = hid_ref.shape
    sources = [store.at[stored_at(i, tok, d)] for i in range(5)] + [pay_hbm, res_hbm]
    targets = [xn_ref, q_ref, k_ref, v_ref, att_ref, pay_ref, res_ref]
    for lo, hi in ((3 * d, w_ref.shape[1]), (0, 3 * d)):
        sources.append(store.at[0:d, lo:hi])
        targets.append(w_ref.at[:, lo:hi])
    loads = [
        pltpu.make_async_copy(src, ref, sems_in.at[i])
        for i, (src, ref) in enumerate(zip(sources, targets))
    ]
    for i in (5, 6, 7, 4, 1, 2, 3):
        loads[i].start()
    loads[5].wait()
    gains = gains_ref[...]
    gain1 = gains[0:1, :]
    gain2 = gains[1:2, :]
    rows = rs_ref[...].astype(F32) + own_ref[...].astype(F32)
    tail = rows[tok : tok + n_exp, :]
    ggt = tail[:, 0:tok] + tail[:, tok : 2 * tok]
    ggt = jnp.concatenate([ggt, jnp.zeros((LANES - n_exp, tok), F32)], axis=0)
    gg = ggt.T
    gate = gate_ref[...]
    picked = gate * (gg - jnp.sum(gate * gg, axis=1, keepdims=True))
    logit_grad = picked.astype(BF)
    act_t = pay_ref[0:tok, :].T
    aux_grad = dot(act_t, logit_grad)
    grad = grad_ref[...].astype(F32)
    loads[6].wait()
    res = res_ref[...]
    inv2 = lax.rsqrt(jnp.mean(res * res, axis=1, keepdims=True) + EPS)
    loads[7].wait()
    loads[0].start()
    loads[8].start()
    moe_in = rows[0:tok, :] + dot_nt(logit_grad, w_ref[:, 4 * d : 4 * d + LANES])
    weighted = moe_in * gain2
    gg2 = jnp.sum(moe_in * res * inv2, axis=0, keepdims=True)
    inner = jnp.mean(weighted * res, axis=1, keepdims=True)
    rgrad = grad + inv2 * weighted - res * (inv2 * inv2 * inv2 * inner)
    low = rgrad.astype(BF)
    for i in (4, 1, 2, 3):
        loads[i].wait()
    dw_ref[:, 3 * d : 4 * d] = dot(att_ref[...].T, low).astype(BF)
    allowed = allowed_mask(segc_ref[...], segr_ref[...])
    cos = cos_ref[...]
    sin = sin_ref[...]
    scale = HD ** -0.5
    pair = 2 * HD
    for c in range(0, d, pair):
        agp = dot_nt(low, w_ref[c : c + pair, 3 * d : 4 * d]).astype(BF)
        for o in range(0, pair, HD):
            cols = slice(c + o, c + o + HD)
            q = q_ref[:, cols]
            k = k_ref[:, cols]
            ag = agp[:, o : o + HD]
            probs = head_probs(q, k, allowed)
            dv_ref[:, cols] = dot_tn(probs.astype(BF), ag).astype(BF)
            dp = dot_nt(ag, v_ref[:, cols])
            ds = (probs * (dp - jnp.sum(probs * dp, axis=1, keepdims=True))).astype(BF)
            dq = dot(ds, k) * scale
            dk = dot_tn(ds, q) * scale
            dq_ref[:, cols] = rope_back(dq, cos, sin).astype(BF)
            dk_ref[:, cols] = rope_back(dk, cos, sin).astype(BF)
    loads[8].wait()
    loads[0].wait()
    back = dot_nt(dq_ref[...], w_ref[:, 0:d])
    back += dot_nt(dk_ref[...], w_ref[:, d : 2 * d])
    back += dot_nt(dv_ref[...], w_ref[:, 2 * d : 3 * d])
    x = hid_ref[...].astype(F32)
    inv = lax.rsqrt(jnp.mean(x * x, axis=1, keepdims=True) + EPS)
    weighted = back * gain1
    gg1 = jnp.sum(back * x * inv, axis=0, keepdims=True)
    inner = jnp.mean(weighted * x, axis=1, keepdims=True)
    ig_ref[...] = rgrad + inv * weighted - x * (inv * inv * inv * inner)
    rowid = lax.broadcasted_iota(jnp.int32, (LANES, d), 0)
    gain_rows = jnp.where(rowid == n_exp, gg1, 0.0) + jnp.where(rowid == n_exp + 1, gg2, 0.0)
    dw_ref[:, 4 * d : 4 * d + LANES] = (aux_grad + gain_rows.T).astype(BF)
    xn_t = xn_ref[...].T
    dw_ref[:, 0:d] = dot(xn_t, dq_ref[...]).astype(BF)
    dw_ref[:, d : 2 * d] = dot(xn_t, dk_ref[...]).astype(BF)
    dw_ref[:, 2 * d : 3 * d] = dot(xn_t, dv_ref[...]).astype(BF)
    half = n // 2
    outs = []
    for i in range(n):
        start = pl.multiple_of(gidx_ref[i] * height, 16)
        out = mine_ref.at[i] if i < half else first_ref
        if i > half:
            at = i - half - 1
            soon = soon_ref.shape[0]
            out = soon_ref.at[at] if at < soon else later_ref.at[at - soon]
        copy = pltpu.make_async_copy(dw_ref.at[pl.ds(start, height), :], out, sems_out.at[i])
        copy.start()
        outs.append(copy)
    for copy in outs:
        copy.wait()


def body(
    nd,
    ne,
    hidden_in,
    out_grad,
    segment_ids,
    routes,
    attn_gain,
    w_query,
    w_key,
    w_value,
    w_out,
    moe_gain,
    w_router,
    shared_gate,
    shared_up,
    shared_down,
    expert_gate,
    expert_up,
    expert_down,
):
    tok, d = hidden_in.shape
    n_exp = w_router.shape[1]
    n_loc = expert_gate.shape[0]
    ff = expert_gate.shape[2]
    top_k = routes.shape[1]
    cap = min(tok, 8 * ((10 * tok * top_k + 56 * n_exp - 1) // (56 * n_exp)))
    extra = tok + n_exp
    hr = d // ne // 2
    hdn = shared_down.shape[0]
    wide = 4 * d + LANES

    me = lax.axis_index("expert")
    core = lax.axis_index("dp") % 2
    perm = ring_perm(nd, ne)
    both = ("dp", "expert")

    def ring(v):
        return lax.ppermute(v, both, perm)

    def swap(v, bit):
        return lax.ppermute(v, "dp", [(i, i ^ bit) for i in range(nd)])

    table = jnp.asarray(ring_order(ne))
    mine_order = lax.dynamic_slice(table, (core, me, 0), (1, 1, ne)).reshape(ne)
    other_order = lax.dynamic_slice(table, (1 - core, me, 0), (1, 1, ne)).reshape(ne)
    gidx = jnp.concatenate(
        [jnp.roll(mine_order, -1) * 2 + core, jnp.roll(other_order, -1) * 2 + 1 - core]
    )
    scal = jnp.stack([me * n_loc + 1 - core, me * n_loc + core, 1 - core, core]).astype(jnp.int32)

    def fence(*vs):
        return list(lax.optimization_barrier(tuple(vs)))

    def halves(v):
        v = v.reshape(2, v.shape[0] // 2, v.shape[1])
        return (
            lax.dynamic_index_in_dim(v, core, 0, False),
            lax.dynamic_index_in_dim(v, 1 - core, 0, False),
        )

    units = ff // ne
    wide_f = -(-units // LANES) * LANES

    def spread(v):
        v = v.reshape(v.shape[0], ne, units).transpose(1, 0, 2)
        return jnp.pad(v, ((0, 0), (0, 0), (0, wide_f - units)))

    def exchange(v):
        return lax.all_to_all(v, "expert", split_axis=0, concat_axis=0, tiled=True)

    expert_gate, expert_up, expert_down = (
        pltpu.with_memory_space_constraint(v, pltpu.HBM) for v in (expert_gate, expert_up, expert_down)
    )
    sgu = jnp.concatenate([spread(halves(shared_gate)[0]), spread(halves(shared_up)[0])], axis=2)
    sdn = jnp.pad(shared_down, ((0, wide_f - units), (0, 0)))

    split = 2 * d
    aux = jnp.concatenate(
        [
            w_router,
            attn_gain[:, None],
            moe_gain[:, None],
            jnp.zeros((w_router.shape[0], LANES - n_exp - 2), BF),
        ],
        axis=1,
    )
    left, left_other = (jnp.concatenate(v, axis=1) for v in zip(halves(w_query), halves(w_key)))
    right, right_other = (
        jnp.concatenate(v, axis=1) for v in zip(halves(w_value), halves(w_out), halves(aux))
    )
    store_shape = (hbm((d + 2 * tok, wide), BF),)
    planes = ring_perm(nd, ne, True)
    way = (core + lax.axis_index("dp") // 2) % 2
    same = lax.dynamic_slice(table, (way, me, 0), (1, 1, ne)).reshape(ne)
    back = lax.dynamic_slice(table, (1 - way, me, 0), (1, 1, ne)).reshape(ne)
    idx = jnp.concatenate([same * 2 + core, back * 2 + 1 - core, back * 2 + core, same * 2 + 1 - core])
    kinds = [(0, 0), (0, split)] * 2
    store = place_call(
        kinds, [0, 0, ne, ne], idx, [left, right, left_other, right_other], store_shape, ()
    )
    crossed = 2 if nd > 2 else 0

    def place(groups, into):
        spots, pieces = [], []
        for near, far_side, two in groups:
            spots += [near, near, far_side, far_side]
            pieces += [*two, *[swap(v, 1) for v in two]]
        return place_call(kinds * len(groups), spots, idx, pieces, store_shape, into)

    over = {}
    last = ne - 1 - crossed
    for i in range(1, last + 1):
        left = lax.ppermute(left, both, planes)
        right = lax.ppermute(right, both, planes)
        if i <= crossed:
            over[i] = (swap(left, 2), swap(right, 2))
        if i == 2:
            left, sgu = fence(left, sgu)
            sgu = exchange(sgu)
        if i == 4:
            left, sgu, sdn = fence(left, sgu, sdn)
            sgu = jnp.stack([sgu, swap(sgu, 1)])
            sgu = jnp.where(core == 0, sgu, sgu[::-1]).transpose(1, 0, 2, 3).reshape(d, 2 * wide_f)
        if i == 5:
            left, sgu = fence(left, sgu)
        if i - 2 in over:
            xl, xr = over[i - 2]
            left, xl = fence(left, xl)
            if i < last:
                over[i - 2] = (xl, xr)
        if i - 3 in over:
            xl, xr = over[i - 3]
            right, xr = fence(right, xr)
            over[i - 3] = (xl, xr)
        if i < last:
            groups = [(i, ne + i, (left, right))]
            if i == 4 and 1 in over:
                groups.append((2 * ne + 1, 3 * ne + 1, over.pop(1)))
            placed = place(groups, store)
            left = fence(left, *store)[0]
            right = fence(right, *store)[0]
        else:
            left, right, *store = fence(left, right, *store)
            groups = [(i, ne + i, (left, right))]
            groups += [(2 * ne + k, 3 * ne + k, over[k]) for k in sorted(over)]
            placed = place(groups, store)
        store = placed

    half = HD // 2
    freq = ROPE_BASE ** (-2.0 * np.arange(half) / HD)
    ang = np.arange(tok)[:, None] * freq[None, :]
    cos = jnp.asarray(np.concatenate([np.cos(ang), np.cos(ang)], 1).astype(np.float32))
    sin = jnp.asarray(np.concatenate([-np.sin(ang), np.sin(ang)], 1).astype(np.float32))
    seg_row = segment_ids
    seg_col = segment_ids.reshape(tok, 1)

    g0, left, right = fence(out_grad, left, right)
    grads = [g0, ring(g0)]
    store, res, gate, pay, gains = pl.pallas_call(
        functools.partial(attn_forward, n_exp),
        out_shape=store_shape
        + (
            hbm((tok, d), F32),
            hbm((tok, LANES), F32),
            shape((extra, d), BF),
            shape((8, d), F32),
        ),
        in_specs=[whole()] * 6 + [far()],
        out_specs=[far()] * 3 + [whole()] * 2,
        scratch_shapes=[VMEM((d, wide), BF)]
        + [VMEM((tok, d), BF)] * 5
        + [
            VMEM((tok, d), F32),
            VMEM((tok, LANES), F32),
            pltpu.SemaphoreType.DMA((5,)),
            pltpu.SemaphoreType.DMA((7,)),
        ],
        input_output_aliases={6: 0},
        compiler_params=params(36),
        cost_estimate=cost(2 * tok * d * d * 4, d * wide * 2),
        name="attn_forward",
    )(hidden_in, seg_col, seg_row, routes, cos, sin, *store)
    pay, grads[1] = fence(pay, grads[1])

    def start_flow(parts):
        return {"parts": parts, "at": 0, "acc": parts(0).astype(BF)}

    def advance(flow, got):
        flow["at"] += 1
        if flow["at"] == ne - 1:
            flow["got"] = got
        else:
            flow["acc"] = (got.astype(F32) + flow["parts"](flow["at"])).astype(BF)

    def ring_total(flow):
        return flow["got"].astype(F32) + flow["parts"](ne - 1)

    def token_parts(parts):
        return lambda i: parts[(i + 1) % ne].astype(F32)

    def dense_parts(mine, others):
        def part(i):
            at = i
            for group in others:
                if at < group.shape[0]:
                    return mine[i].astype(F32) + group[at].astype(F32)
                at -= group.shape[0]

        return part

    down_shapes = (hbm((n_loc, ff, d), F32),)
    gu_shapes = (hbm((n_loc, d, ff), F32),) * 2
    n_down, n_gu = 4, 8
    waiting, landed, shared_out = [], [], []
    finished = {"down": (), "gu": ()}

    def queue(name, low, count):
        height = low.shape[0] // count
        for j in range(count):
            waiting.append((name, j * height, lax.slice_in_dim(low, j * height, (j + 1) * height)))

    def across(low):
        return swap(low, 2) if nd > 2 else low * 0

    def summed(low, more):
        total = low.astype(F32) + more.astype(F32)
        bit = 4
        while bit < nd:
            low = total.astype(BF)
            total = low.astype(F32) + swap(low, bit).astype(F32)
            bit *= 2
        return total.astype(BF)

    def emit():
        names = set()
        for name, start, mine, other in shared_out:
            if name not in finished:
                held[name] = (start, mine, other)
                continue
            shapes = down_shapes if name == "down" else gu_shapes
            finished[name] = emit_call(start, scal, mine, other, shapes, finished[name])
            names.add(name)
        shared_out.clear()
        return sorted(names)

    held = {}

    def slot(flows=(), sends=(), swaps=(), cross=0, compute=None, keep=(), ready=None, write=True, joint=True):
        chunks = waiting[:cross]
        del waiting[:cross]
        summing = [(name, start, summed(low, more)) for (name, start, low), more in landed]
        landed.clear()
        moved = [ring(f["acc"]) for f in flows] + [ring(v) for v in sends]
        moved += [across(low) for _, _, low in chunks]
        moved += [swap(v, 1) for v in swaps]
        moved += [swap(mine, 1) for _, _, mine in summing]
        names = emit() if write else []
        done = list(compute()) if compute is not None else []
        late = [v for name in names for v in finished[name]]
        if joint:
            out = fence(*moved, *done, *keep, *late)
        else:
            done = fence(*done)
            out = [fence(v, done[0])[0] for v in moved] + done

        def pop(count):
            first = out[:count]
            del out[:count]
            return first

        arrived = pop(len(flows))
        sent = pop(len(sends))
        landed.extend(zip(chunks, pop(len(chunks))))
        swapped = pop(len(swaps))
        if ready is not None:
            ready(swapped)
        for f, got in zip(flows, arrived):
            advance(f, got)
        for (name, start, mine), other in zip(summing, pop(len(summing))):
            shared_out.append((name, start, mine, other))
        done = pop(len(done))
        kept = pop(len(keep))
        for name in names:
            finished[name] = tuple(pop(len(finished[name])))
        return sent, swapped, done, kept

    pays = [pay]
    saved = ()
    in_parts, out_parts = [], []
    flow_in = None
    for i in range(ne):
        sends = []
        if i + 1 < ne:
            sends.append(pays[i])
        if i + 2 < ne:
            sends.append(grads[i + 1])
        if i == ne - 2:
            flow_in = start_flow(token_parts(in_parts))

        def block(i=i):
            new, ins, outs = expert_call(
                i, 1, cap, n_exp, scal, pays[i : i + 1], grads[i : i + 1],
                (expert_gate, expert_up, expert_down, sgu, sdn), saved,
            )
            held["saved"] = new
            return [ins[0], outs[0]]

        sent, _, done, _ = slot([flow_in] if flow_in else [], sends, compute=block, joint=False)
        saved = held["saved"]
        in_parts.append(done[0])
        out_parts.append(done[1])
        if i + 1 < ne:
            pays.append(sent[0])
        if i + 2 < ne:
            grads.append(sent[-1])

    xr, gr, gh, dgu, sum_gu, sum_dn = saved
    hw = d // 2
    gu_halves = sum_gu.astype(BF).reshape(ne, 2, hr, 2 * wide_f).transpose(1, 0, 2, 3)
    dn_halves = sum_dn[0:units].astype(BF).reshape(units, 2, hw).transpose(1, 0, 2)

    def of_side(v, side):
        return lax.dynamic_index_in_dim(v, side, 0, False)

    flow_out = start_flow(token_parts(out_parts))
    _, (gu_more, dn_more), (down_t,), _ = slot(
        [flow_in, flow_out],
        swaps=[of_side(gu_halves, 1 - core), of_side(dn_halves, 1 - core)],
        compute=lambda: [dot_tn(gh[0], gr[0]).astype(BF)],
    )

    def add(left, right):
        return (left.astype(F32) + right.astype(F32)).astype(BF)

    _, (down_got,), (down_m,), _ = slot(
        [flow_in, flow_out], swaps=[down_t], compute=lambda: [dot_tn(gh[1], gr[1]).astype(BF)]
    )
    queue("down", add(down_m, down_got), n_down)
    _, _, (gu_t,), _ = slot(
        [flow_in, flow_out], cross=1, compute=lambda: [dot_tn(xr[0], dgu[0]).astype(BF)]
    )
    _, _, (gu_m,), _ = slot(
        [flow_in, flow_out], cross=1, compute=lambda: [dot_tn(xr[1], dgu[1]).astype(BF)]
    )
    _, (gu_got,), _, _ = slot([flow_in], swaps=[gu_t], cross=1)
    while flow_in["at"] < ne - 1:
        slot([flow_in])
    height = d // n_gu
    for j in range(n_gu):
        cut_rows = slice(j * height, (j + 1) * height)
        waiting.append(("gu", j * height, add(gu_m[cut_rows], gu_got[cut_rows])))
    waiting.insert(2, ("sgu", 0, add(of_side(gu_halves, core), gu_more)))
    waiting.insert(3, ("sdn", 0, add(of_side(dn_halves, core), dn_more)))
    rs_in = flow_in["got"]

    soon = 3

    def backward():
        return pl.pallas_call(
            functools.partial(attn_backward, n_exp),
            out_shape=(
                shape((tok, d), F32),
                hbm((ne, hr, wide), BF),
                hbm((hr, wide), BF),
                hbm((soon, hr, wide), BF),
                hbm((ne - 1 - soon, hr, wide), BF),
            ),
            in_specs=[whole(SMEM)] + [whole()] * 10 + [far()] * 3,
            out_specs=[whole()] + [far()] * 4,
            scratch_shapes=[
                VMEM((d, wide), BF),
                VMEM((d, wide), BF),
            ]
            + [VMEM((tok, d), BF)] * 8
            + [
                VMEM((extra, d), BF),
                VMEM((tok, d), F32),
                pltpu.SemaphoreType.DMA((9,)),
                pltpu.SemaphoreType.DMA((2 * ne,)),
            ],
            compiler_params=params(56),
            cost_estimate=cost(2 * tok * d * d * 8, 2 * d * wide * 2),
            name="attn_backward",
        )(
            gidx, hidden_in, out_grad, seg_col, seg_row, cos, sin, gate, gains, rs_in, in_parts[0],
            store, pay, res,
        )

    _, _, (input_grad, d_mine, d_first, d_soon, d_later), _ = slot(
        [flow_out], cross=2, compute=backward, write=False
    )
    others = [swap(d_first, 1)[None]]
    flow_d = start_flow(dense_parts(d_mine, others))
    slot([flow_d], swaps=[d_soon], cross=2, ready=others.extend)
    slot([flow_d], swaps=[d_later], cross=1, ready=others.extend)

    def shared_exchange():
        if "sgu" in held and "sgu_sent" not in held:
            _, mine, _ = held["sgu"]
            held["sgu_sent"] = True
            return [exchange(mine)]
        return []

    pick = core == 0

    def sides(name):
        _, mine, other = held[name]
        mine = mine.astype(F32)
        other = other.astype(F32)
        return jnp.where(pick, mine, other), jnp.where(pick, other, mine)

    def row_halves():
        held["rows"] = (0, held["spread"], held["spread_other"])
        both_rows = jnp.concatenate(sides("rows"), axis=1)
        g_gate = both_rows[:, :, 0:units].transpose(1, 0, 2).reshape(2 * hr, ff)
        g_up = both_rows[:, :, wide_f : wide_f + units].transpose(1, 0, 2).reshape(2 * hr, ff)
        return [g_gate, g_up]

    while flow_d["at"] < ne - 1:
        ready_rows = "spread_other" in held and "gate_up" not in held
        swaps = [held["spread"]] if "spread" in held and "spread_other" not in held else []
        _, swapped, got, _ = slot(
            [flow_d], swaps=swaps, cross=1, compute=row_halves if ready_rows else shared_exchange
        )
        if ready_rows:
            held["gate_up"] = got
        elif got:
            held["spread"] = got[0]
        if swapped:
            held["spread_other"] = swapped[0]
    low = ring_total(flow_d).astype(BF)
    first_rows = -(-hr // 32) * 16
    waiting.append(("dense0", 0, low[0:first_rows]))
    waiting.append(("dense1", 0, low[first_rows:hr]))
    while waiting or landed or flow_out["at"] < ne - 1:
        slot([flow_out] if flow_out["at"] < ne - 1 else [], cross=1)
    emit()

    output = res + flow_out["got"].astype(F32) + out_parts[0].astype(F32)
    upper, lower = sides("dense0"), sides("dense1")
    g_d = jnp.concatenate([upper[0], lower[0], upper[1], lower[1]], axis=0)
    g_gate, g_up = held["gate_up"]
    g_dn = jnp.concatenate(sides("sdn"), axis=1)
    (down_w,) = finished["down"]
    gate_w, up_w = finished["gu"]
    return (
        output,
        input_grad,
        g_d[:, 4 * d + n_exp],
        g_d[:, 0:d],
        g_d[:, d : 2 * d],
        g_d[:, 2 * d : 3 * d],
        g_d[:, 3 * d : 4 * d],
        g_d[:, 4 * d + n_exp + 1],
        g_d[:, 4 * d : 4 * d + n_exp],
        g_gate,
        g_up,
        g_dn,
        gate_w,
        up_w,
        down_w,
    )


def solution(mesh):
    nd = mesh.shape["dp"]
    ne = mesh.shape["expert"]
    tokens = P(("dp", "expert"), None)
    vector = P("expert")
    matrix = P("expert", None)
    cube = P("expert", None, None)
    return jax.shard_map(
        functools.partial(body, nd, ne),
        mesh=mesh,
        in_specs=(tokens,) * 4
        + (vector, matrix, matrix, matrix, matrix, vector)
        + (matrix,) * 4
        + (cube,) * 3,
        out_specs=(tokens, tokens, vector, matrix, matrix, matrix, matrix, vector)
        + (matrix,) * 4
        + (cube,) * 3,
        check_vma=False,
    )
```

```python
import functools

import jax
import jax.numpy as jnp
import numpy as np
from jax import lax
from jax.experimental import pallas as pl
from jax.experimental.pallas import tpu as pltpu
from jax.sharding import PartitionSpec as P

HD = 128
LANES = 128
EPS = 1e-06
ROPE_BASE = 10000.0
MASKED = -1e30
BF = jnp.bfloat16
F32 = jnp.float32
VMEM = pltpu.VMEM
SMEM = pltpu.SMEM
MIB = 1 << 20


def dot(a, b):
    return jnp.dot(a, b, preferred_element_type=F32)


def dot_nt(a, b):
    return lax.dot_general(a, b, (((1,), (1,)), ((), ())), preferred_element_type=F32)


def dot_tn(a, b):
    return lax.dot_general(a, b, (((0,), (0,)), ((), ())), preferred_element_type=F32)


def sigmoid(v):
    return 1.0 / (1.0 + jnp.exp(-v))


def whole(space=VMEM):
    return pl.BlockSpec(memory_space=space)


def anywhere():
    return pl.BlockSpec(memory_space=pl.ANY)


def far():
    return pl.BlockSpec(memory_space=pltpu.HBM)


def params(mib):
    return pltpu.CompilerParams(vmem_limit_bytes=mib * MIB)


def cost(flops, nbytes):
    return pl.CostEstimate(flops=int(flops), bytes_accessed=int(nbytes), transcendentals=0)


def shape(dims, dtype):
    return jax.ShapeDtypeStruct(dims, dtype)


def hbm(dims, dtype):
    return pltpu.HBM(dims, dtype)


def cycle(n):
    return list(range(0, n, 2)) + list(range(1, n, 2))[::-1]


def ring_perm(nd, ne, planes=False):
    ring = cycle(ne)
    pos = {e: i for i, e in enumerate(ring)}
    pairs = []
    for d in range(nd):
        for e in range(ne):
            step = 1 if (d + (d // 2 if planes else 0)) % 2 == 0 else -1
            pairs.append((d * ne + e, d * ne + ring[(pos[e] + step) % ne]))
    return pairs


def ring_order(ne):
    ring = cycle(ne)
    pos = {e: i for i, e in enumerate(ring)}
    table = np.zeros((2, ne, ne), np.int32)
    for c in range(2):
        step = 1 if c == 0 else -1
        for e in range(ne):
            for s in range(ne):
                table[c, e, s] = ring[(pos[e] - step * s) % ne]
    return table


def place_pieces(kinds, spots, aliased, idx_ref, *refs):
    n = len(kinds)
    pieces = refs[:n]
    outs = refs[n + aliased : -1]
    sems = refs[-1]
    copies = []
    for i, (target, col) in enumerate(kinds):
        height, width = pieces[i].shape
        start = pl.multiple_of(idx_ref[spots[i]] * height, 16)
        dst = outs[target].at[pl.ds(start, height), col : col + width]
        copies.append(pltpu.make_async_copy(pieces[i], dst, sems.at[i]))
    for copy in copies:
        copy.start()
    for copy in copies:
        copy.wait()


def place_call(kinds, spots, idx, pieces, targets, into):
    n = len(kinds)
    return pl.pallas_call(
        functools.partial(place_pieces, kinds, spots, len(into)),
        out_shape=targets,
        in_specs=[whole(SMEM)] + [whole()] * n + [far()] * len(into),
        out_specs=[far()] * len(targets),
        scratch_shapes=[pltpu.SemaphoreType.DMA((n,))],
        input_output_aliases={1 + n + j: j for j in range(len(into))},
        compiler_params=params(8),
        cost_estimate=cost(0, sum(p.size for p in pieces) * 4),
        name="place_pieces",
    )(idx, *pieces, *into)


def emit_rows(start, aliased, scal_ref, mine_ref, other_ref, *refs):
    outs = refs[aliased : -2]
    buf, sems = refs[-2:]
    height = mine_ref.shape[0]
    width = outs[0].shape[2]
    buf[0] = mine_ref[...].astype(F32)
    buf[1] = other_ref[...].astype(F32)
    copies = []
    for side in range(2):
        expert = scal_ref[3 - side]
        for j, out in enumerate(outs):
            copies.append(
                pltpu.make_async_copy(
                    buf.at[side, :, j * width : (j + 1) * width],
                    out.at[expert, pl.ds(start, height), :],
                    sems.at[side, j],
                )
            )
    for copy in copies:
        copy.start()
    for copy in copies:
        copy.wait()


def emit_call(start, scal, mine, other, targets, into):
    return pl.pallas_call(
        functools.partial(emit_rows, start, len(into)),
        out_shape=targets,
        in_specs=[whole(SMEM)] + [whole()] * 2 + [far()] * len(into),
        out_specs=[far()] * len(targets),
        scratch_shapes=[
            VMEM((2,) + mine.shape, F32),
            pltpu.SemaphoreType.DMA((2, len(targets))),
        ],
        input_output_aliases={3 + j: j for j in range(len(into))},
        compiler_params=params(12),
        cost_estimate=cost(0, mine.size * 12),
        name="emit_rows",
    )(scal, mine, other, *into)


def stored_at(i, tok, d):
    row = d + tok * (i // 4)
    col = d * (i % 4)
    return slice(row, row + tok), slice(col, col + d)


def rope(u, cos, sin):
    return u * cos + pltpu.roll(u, HD // 2, 1) * sin


def rope_back(u, cos, sin):
    return u * cos - pltpu.roll(u, HD // 2, 1) * sin


def allowed_mask(seg_col, seg_row):
    n = seg_row.shape[1]
    rows = lax.broadcasted_iota(jnp.int32, (n, n), 0)
    cols = lax.broadcasted_iota(jnp.int32, (n, n), 1)
    return (seg_col == seg_row) & (cols <= rows)


def head_probs(q, k, allowed):
    s = dot_nt(q, k) * (HD ** -0.5)
    s = jnp.where(allowed, s, MASKED)
    e = jnp.exp(s - jnp.max(s, axis=1, keepdims=True))
    return e / jnp.sum(e, axis=1, keepdims=True)


def attn_forward(n_exp, hid_ref, segc_ref, segr_ref, routes_ref, cos_ref, sin_ref, store_in, *rest):
    store, res_hbm, gate_hbm, pay_ref, gains_ref, w_ref, xn_ref, q_ref, k_ref, v_ref, att_ref = rest[:11]
    res_ref, gate_ref, sems, sems_out = rest[11:]
    tok, d = hid_ref.shape
    wide = w_ref.shape[1]
    saves = [
        pltpu.make_async_copy(ref, store.at[stored_at(i, tok, d)], sems_out.at[i])
        for i, ref in enumerate((xn_ref, q_ref, k_ref, v_ref, att_ref))
    ]
    saves.append(pltpu.make_async_copy(res_ref, res_hbm, sems_out.at[5]))
    saves.append(pltpu.make_async_copy(gate_ref, gate_hbm, sems_out.at[6]))
    spans = [(4 * d, wide)] + [(i * d, (i + 1) * d) for i in range(4)]
    loads = [
        pltpu.make_async_copy(store.at[0:d, lo:hi], w_ref.at[:, lo:hi], sems.at[i])
        for i, (lo, hi) in enumerate(spans)
    ]
    for load in loads:
        load.start()
    x = hid_ref[...].astype(F32)
    inv = lax.rsqrt(jnp.mean(x * x, axis=1, keepdims=True) + EPS)
    cos = cos_ref[...]
    sin = sin_ref[...]
    allowed = allowed_mask(segc_ref[...], segr_ref[...])
    loads[0].wait()
    aux = w_ref[:, 4 * d : 4 * d + LANES]
    turned = aux.astype(F32).T
    gains = turned[n_exp : n_exp + 8, :]
    gains_ref[...] = gains
    xn = (x * inv * gains[0:1, :]).astype(BF)
    xn_ref[...] = xn
    saves[0].start()
    pair = 2 * HD
    for j, ref in ((0, q_ref), (1, k_ref)):
        loads[1 + j].wait()
        for c in range(0, d, pair):
            pre = dot(xn, w_ref[:, j * d + c : j * d + c + pair])
            for o in range(0, pair, HD):
                ref[:, c + o : c + o + HD] = rope(pre[:, o : o + HD], cos, sin).astype(BF)
    loads[3].wait()
    for c in range(0, d, pair):
        vp = dot(xn, w_ref[:, 2 * d + c : 2 * d + c + pair]).astype(BF)
        v_ref[:, c : c + pair] = vp
        for o in range(0, pair, HD):
            cols = slice(c + o, c + o + HD)
            probs = head_probs(q_ref[:, cols], k_ref[:, cols], allowed).astype(BF)
            att_ref[:, cols] = dot(probs, vp[:, o : o + HD]).astype(BF)
    for save in saves[1:5]:
        save.start()
    loads[4].wait()
    res = x + dot(att_ref[...], w_ref[:, 3 * d : 4 * d])
    res_ref[...] = res
    saves[5].start()
    inv2 = lax.rsqrt(jnp.mean(res * res, axis=1, keepdims=True) + EPS)
    act = (res * inv2 * gains[1:2, :]).astype(BF)
    logits = dot(act, aux)
    lane = lax.broadcasted_iota(jnp.int32, (tok, LANES), 1)
    routes = routes_ref[...]
    chosen = routes[:, 0:1] == lane
    for j in range(1, routes.shape[1]):
        chosen = chosen | (routes[:, j : j + 1] == lane)
    logits = jnp.where(chosen, logits, MASKED)
    e = jnp.where(chosen, jnp.exp(logits - jnp.max(logits, axis=1, keepdims=True)), 0.0)
    gate = e / jnp.sum(e, axis=1, keepdims=True)
    gate_ref[...] = gate
    saves[6].start()
    gate_t = gate.T[0:n_exp, :]
    high = gate_t.astype(BF)
    pay_ref[0:tok, :] = act
    pay_ref[tok : tok + n_exp, :] = jnp.zeros((n_exp, d), BF)
    pay_ref[tok : tok + n_exp, 0:tok] = high
    pay_ref[tok : tok + n_exp, tok : 2 * tok] = (gate_t - high.astype(F32)).astype(BF)
    for save in saves:
        save.wait()


def expert_block(first, nb, cap, n_exp, aliased, scal_ref, *refs):
    pays = refs[:nb]
    grads = refs[nb : 2 * nb]
    wg_hbm, wu_hbm, wd_hbm, sgu_ref, sdn_ref = refs[2 * nb : 2 * nb + 5]
    outs = refs[2 * nb + 5 + aliased :]
    saved = outs[:6]
    in_refs = outs[6 : 6 + nb]
    out_refs = outs[6 + nb : 6 + 2 * nb]
    wgu_ref, wd_ref, xr_ref, gr_ref, gh_ref, dgu_ref, agu_ref, adn_ref, sems_w, sems, sems_a = outs[6 + 2 * nb :]
    n_loc, _, ff2 = wgu_ref.shape
    ff = ff2 // 2
    tok, d = grads[0].shape
    loads = []
    for e in range(n_loc):
        three = (
            pltpu.make_async_copy(wg_hbm.at[scal_ref[n_loc + e]], wgu_ref.at[e, :, 0:ff], sems_w.at[e, 0]),
            pltpu.make_async_copy(wu_hbm.at[scal_ref[n_loc + e]], wgu_ref.at[e, :, ff:ff2], sems_w.at[e, 1]),
            pltpu.make_async_copy(wd_hbm.at[scal_ref[n_loc + e]], wd_ref.at[e], sems_w.at[e, 2]),
        )
        for copy in three:
            copy.start()
        loads.append(three)
    sums = []
    if aliased:
        sums.append(pltpu.make_async_copy(saved[4], agu_ref, sems_a.at[0]))
        sums.append(pltpu.make_async_copy(saved[5], adn_ref, sems_a.at[1]))
    for copy in sums:
        copy.start()
    rowid = lax.broadcasted_iota(jnp.int32, (n_exp, tok), 0)
    tri = (
        lax.broadcasted_iota(jnp.int32, (tok, tok), 0)
        < lax.broadcasted_iota(jnp.int32, (tok, tok), 1)
    )
    tri = jnp.where(tri, 1.0, 0.0).astype(BF)
    slots = lax.broadcasted_iota(jnp.int32, (cap, tok), 0)
    gates = []
    for b in range(nb):
        gt = pays[b][tok : tok + n_exp, 0:tok].astype(F32)
        gt = gt + pays[b][tok : tok + n_exp, tok : 2 * tok].astype(F32)
        for e in range(n_loc):
            gates.append(jnp.sum(jnp.where(rowid == scal_ref[e], gt, 0.0), axis=0, keepdims=True))
    used = len(gates)
    stack = jnp.concatenate(gates + [jnp.zeros((-used % 8, tok), F32)] * (used % 8 > 0), axis=0)
    ranks = dot(jnp.where(stack > 0.0, 1.0, 0.0).astype(BF), tri)
    masks, picks, gs = {}, {}, {}
    for b in range(nb):
        for e in range(n_loc):
            at = b * n_loc + e
            g = gates[at]
            slot = jnp.where(g > 0.0, ranks[at : at + 1, :], -1.0).astype(jnp.int32)
            mask = slots == slot
            pick = jnp.where(mask, 1.0, 0.0).astype(BF)
            masks[b, e] = mask
            picks[b, e] = pick
            gs[b, e] = jnp.sum(jnp.where(mask, g, 0.0), axis=1, keepdims=True)
            rows = slice(b * cap, (b + 1) * cap)
            xr_ref[e, rows, :] = dot(pick, pays[b][0:tok, :]).astype(BF)
            gr_ref[e, rows, :] = dot(pick, grads[b][...]).astype(BF)
    copies = []

    def save(j, e, ref):
        copy = pltpu.make_async_copy(
            ref.at[e], saved[j].at[e, pl.ds(first * cap, nb * cap), :], sems.at[j, e]
        )
        copy.start()
        copies.append(copy)

    for copy in sums:
        copy.wait()
    wide_f = sdn_ref.shape[0]
    s_in, s_out = [], []
    for b in range(nb):
        act_b = pays[b][0:tok, :]
        grad_b = grads[b][...]
        sgu = dot(act_b, sgu_ref[...])
        shu = dot_nt(grad_b, sdn_ref[...])
        sg = sgu[:, 0:wide_f]
        su = sgu[:, wide_f : 2 * wide_f]
        sig = sigmoid(sg)
        sact = sg * sig
        sh = (sact * su).astype(BF)
        sd = jnp.concatenate([shu * su * (sig + sact * (1.0 - sig)), shu * sact], axis=1).astype(BF)
        s_out.append(dot(sh, sdn_ref[...]))
        s_in.append(dot_nt(sd, sgu_ref[...]))
        dgu_b = dot_tn(act_b, sd)
        ddn_b = dot_tn(sh, grad_b)
        if aliased or b > 0:
            agu_ref[...] += dgu_b
            adn_ref[...] += ddn_b
        else:
            agu_ref[...] = dgu_b
            adn_ref[...] = ddn_b
    stores = [
        pltpu.make_async_copy(agu_ref, saved[4], sems_a.at[0]),
        pltpu.make_async_copy(adn_ref, saved[5], sems_a.at[1]),
    ]
    for copy in stores:
        copy.start()
        copies.append(copy)
    ggm = [jnp.zeros((n_exp, tok), F32) for _ in range(nb)]
    xis, yos = [], []
    for e in range(n_loc):
        save(0, e, xr_ref)
        save(1, e, gr_ref)
        loads[e][0].wait()
        loads[e][1].wait()
        egu = dot(xr_ref[e], wgu_ref[e])
        loads[e][2].wait()
        hu = dot_nt(gr_ref[e], wd_ref[e])
        gate = jnp.concatenate([gs[b, e] for b in range(nb)], axis=0)
        eg = egu[:, 0:ff]
        eu = egu[:, ff:ff2]
        sig = sigmoid(eg)
        act = eg * sig
        h = act * eu
        gg = jnp.sum(h.astype(BF).astype(F32) * hu, axis=1, keepdims=True)
        gh_ref[e] = (gate * h).astype(BF)
        save(2, e, gh_ref)
        hg = gate * hu
        dgu_ref[e, :, 0:ff] = (hg * eu * (sig + act * (1.0 - sig))).astype(BF)
        dgu_ref[e, :, ff:ff2] = (hg * act).astype(BF)
        save(3, e, dgu_ref)
        yos.append(dot(gh_ref[e], wd_ref[e]).astype(BF))
        xis.append(dot_nt(dgu_ref[e], wgu_ref[e]).astype(BF))
        for b in range(nb):
            row = jnp.sum(jnp.where(masks[b, e], gg[b * cap : (b + 1) * cap], 0.0), axis=0, keepdims=True)
            ggm[b] = ggm[b] + jnp.where(rowid == scal_ref[e], row, 0.0)
    for b in range(nb):
        rows = slice(b * cap, (b + 1) * cap)
        pick = jnp.concatenate([picks[b, e] for e in range(n_loc)], axis=0)
        in_rows = dot_tn(pick, jnp.concatenate([v[rows] for v in xis], axis=0))
        out_rows = dot_tn(pick, jnp.concatenate([v[rows] for v in yos], axis=0))
        in_refs[b][0:tok, :] = (in_rows + s_in[b]).astype(BF)
        out_refs[b][...] = (out_rows + s_out[b]).astype(BF)
        high = ggm[b].astype(BF)
        in_refs[b][tok : tok + n_exp, :] = jnp.zeros((n_exp, d), BF)
        in_refs[b][tok : tok + n_exp, 0:tok] = high
        in_refs[b][tok : tok + n_exp, tok : 2 * tok] = (ggm[b] - high.astype(F32)).astype(BF)
    for copy in copies:
        copy.wait()


def expert_call(first, nb, cap, n_exp, scal, pays, grads, weights, saved):
    extra, d = pays[0].shape
    tok = grads[0].shape[0]
    n_loc, _, ff = weights[0].shape
    wide_f = weights[4].shape[0]
    rows = cap * (extra - tok) // n_loc
    saved_shapes = (
        hbm((n_loc, rows, d), BF),
        hbm((n_loc, rows, d), BF),
        hbm((n_loc, rows, ff), BF),
        hbm((n_loc, rows, 2 * ff), BF),
        hbm((d, 2 * wide_f), F32),
        hbm((wide_f, d), F32),
    )
    outs = pl.pallas_call(
        functools.partial(expert_block, first, nb, cap, n_exp, len(saved)),
        out_shape=saved_shapes + (shape((extra, d), BF),) * nb + (shape((tok, d), BF),) * nb,
        in_specs=[whole(SMEM)]
        + [whole()] * (2 * nb)
        + [far()] * 3
        + [whole()] * 2
        + [far()] * len(saved),
        out_specs=[far()] * 6 + [whole()] * (2 * nb),
        scratch_shapes=[
            VMEM((n_loc, d, 2 * ff), BF),
            VMEM((n_loc, ff, d), BF),
            VMEM((n_loc, nb * cap, d), BF),
            VMEM((n_loc, nb * cap, d), BF),
            VMEM((n_loc, nb * cap, ff), BF),
            VMEM((n_loc, nb * cap, 2 * ff), BF),
            VMEM((d, 2 * wide_f), F32),
            VMEM((wide_f, d), F32),
            pltpu.SemaphoreType.DMA((n_loc, 3)),
            pltpu.SemaphoreType.DMA((4, n_loc)),
            pltpu.SemaphoreType.DMA((2,)),
        ],
        input_output_aliases={1 + 2 * nb + 5 + j: j for j in range(len(saved))},
        compiler_params=params(40),
        cost_estimate=cost(nb * cap * n_loc * d * ff * 12, 3 * n_loc * d * ff * 2),
        name="expert_block",
    )(scal, *pays, *grads, *weights, *saved)
    return outs[:6], list(outs[6 : 6 + nb]), list(outs[6 + nb :])


def attn_backward(
    n_exp, gidx_ref, hid_ref, grad_ref, segc_ref, segr_ref, cos_ref, sin_ref, gate_ref, gains_ref,
    rs_ref, own_ref, *rest
):
    n = gidx_ref.shape[0]
    store, pay_hbm, res_hbm = rest[:3]
    ig_ref, mine_ref, first_ref, soon_ref, later_ref, w_ref, dw_ref, dq_ref, dk_ref, dv_ref = rest[3:13]
    xn_ref, q_ref, k_ref, v_ref, att_ref, pay_ref, res_ref, sems_in, sems_out = rest[13:]
    height = mine_ref.shape[1]
    tok, d = hid_ref.shape
    sources = [store.at[stored_at(i, tok, d)] for i in range(5)] + [pay_hbm, res_hbm]
    targets = [xn_ref, q_ref, k_ref, v_ref, att_ref, pay_ref, res_ref]
    for lo, hi in ((3 * d, w_ref.shape[1]), (0, 3 * d)):
        sources.append(store.at[0:d, lo:hi])
        targets.append(w_ref.at[:, lo:hi])
    loads = [
        pltpu.make_async_copy(src, ref, sems_in.at[i])
        for i, (src, ref) in enumerate(zip(sources, targets))
    ]
    for i in (5, 6, 7, 4, 1, 2, 3):
        loads[i].start()
    loads[5].wait()
    gains = gains_ref[...]
    gain1 = gains[0:1, :]
    gain2 = gains[1:2, :]
    rows = rs_ref[...].astype(F32) + own_ref[...].astype(F32)
    tail = rows[tok : tok + n_exp, :]
    ggt = tail[:, 0:tok] + tail[:, tok : 2 * tok]
    ggt = jnp.concatenate([ggt, jnp.zeros((LANES - n_exp, tok), F32)], axis=0)
    gg = ggt.T
    gate = gate_ref[...]
    picked = gate * (gg - jnp.sum(gate * gg, axis=1, keepdims=True))
    logit_grad = picked.astype(BF)
    act_t = pay_ref[0:tok, :].T
    aux_grad = dot(act_t, logit_grad)
    grad = grad_ref[...].astype(F32)
    loads[6].wait()
    res = res_ref[...]
    inv2 = lax.rsqrt(jnp.mean(res * res, axis=1, keepdims=True) + EPS)
    loads[7].wait()
    loads[0].start()
    loads[8].start()
    moe_in = rows[0:tok, :] + dot_nt(logit_grad, w_ref[:, 4 * d : 4 * d + LANES])
    weighted = moe_in * gain2
    gg2 = jnp.sum(moe_in * res * inv2, axis=0, keepdims=True)
    inner = jnp.mean(weighted * res, axis=1, keepdims=True)
    rgrad = grad + inv2 * weighted - res * (inv2 * inv2 * inv2 * inner)
    low = rgrad.astype(BF)
    for i in (4, 1, 2, 3):
        loads[i].wait()
    dw_ref[:, 3 * d : 4 * d] = dot(att_ref[...].T, low).astype(BF)
    allowed = allowed_mask(segc_ref[...], segr_ref[...])
    cos = cos_ref[...]
    sin = sin_ref[...]
    scale = HD ** -0.5
    pair = 2 * HD
    for c in range(0, d, pair):
        agp = dot_nt(low, w_ref[c : c + pair, 3 * d : 4 * d]).astype(BF)
        for o in range(0, pair, HD):
            cols = slice(c + o, c + o + HD)
            q = q_ref[:, cols]
            k = k_ref[:, cols]
            ag = agp[:, o : o + HD]
            probs = head_probs(q, k, allowed)
            dv_ref[:, cols] = dot_tn(probs.astype(BF), ag).astype(BF)
            dp = dot_nt(ag, v_ref[:, cols])
            ds = (probs * (dp - jnp.sum(probs * dp, axis=1, keepdims=True))).astype(BF)
            dq = dot(ds, k) * scale
            dk = dot_tn(ds, q) * scale
            dq_ref[:, cols] = rope_back(dq, cos, sin).astype(BF)
            dk_ref[:, cols] = rope_back(dk, cos, sin).astype(BF)
    loads[8].wait()
    loads[0].wait()
    back = dot_nt(dq_ref[...], w_ref[:, 0:d])
    back += dot_nt(dk_ref[...], w_ref[:, d : 2 * d])
    back += dot_nt(dv_ref[...], w_ref[:, 2 * d : 3 * d])
    x = hid_ref[...].astype(F32)
    inv = lax.rsqrt(jnp.mean(x * x, axis=1, keepdims=True) + EPS)
    weighted = back * gain1
    gg1 = jnp.sum(back * x * inv, axis=0, keepdims=True)
    inner = jnp.mean(weighted * x, axis=1, keepdims=True)
    ig_ref[...] = rgrad + inv * weighted - x * (inv * inv * inv * inner)
    rowid = lax.broadcasted_iota(jnp.int32, (LANES, d), 0)
    gain_rows = jnp.where(rowid == n_exp, gg1, 0.0) + jnp.where(rowid == n_exp + 1, gg2, 0.0)
    dw_ref[:, 4 * d : 4 * d + LANES] = (aux_grad + gain_rows.T).astype(BF)
    xn_t = xn_ref[...].T
    dw_ref[:, 0:d] = dot(xn_t, dq_ref[...]).astype(BF)
    dw_ref[:, d : 2 * d] = dot(xn_t, dk_ref[...]).astype(BF)
    dw_ref[:, 2 * d : 3 * d] = dot(xn_t, dv_ref[...]).astype(BF)
    half = n // 2
    outs = []
    for i in range(n):
        start = pl.multiple_of(gidx_ref[i] * height, 16)
        out = mine_ref.at[i] if i < half else first_ref
        if i > half:
            at = i - half - 1
            soon = soon_ref.shape[0]
            out = soon_ref.at[at] if at < soon else later_ref.at[at - soon]
        copy = pltpu.make_async_copy(dw_ref.at[pl.ds(start, height), :], out, sems_out.at[i])
        copy.start()
        outs.append(copy)
    for copy in outs:
        copy.wait()


def body(
    nd,
    ne,
    hidden_in,
    out_grad,
    segment_ids,
    routes,
    attn_gain,
    w_query,
    w_key,
    w_value,
    w_out,
    moe_gain,
    w_router,
    shared_gate,
    shared_up,
    shared_down,
    expert_gate,
    expert_up,
    expert_down,
):
    tok, d = hidden_in.shape
    n_exp = w_router.shape[1]
    n_loc = expert_gate.shape[0]
    ff = expert_gate.shape[2]
    top_k = routes.shape[1]
    cap = min(tok, 8 * ((10 * tok * top_k + 56 * n_exp - 1) // (56 * n_exp)))
    extra = tok + n_exp
    hr = d // ne // 2
    hdn = shared_down.shape[0]
    wide = 4 * d + LANES

    me = lax.axis_index("expert")
    core = lax.axis_index("dp") % 2
    perm = ring_perm(nd, ne)
    both = ("dp", "expert")

    def ring(v):
        return lax.ppermute(v, both, perm)

    def swap(v, bit):
        return lax.ppermute(v, "dp", [(i, i ^ bit) for i in range(nd)])

    table = jnp.asarray(ring_order(ne))
    mine_order = lax.dynamic_slice(table, (core, me, 0), (1, 1, ne)).reshape(ne)
    other_order = lax.dynamic_slice(table, (1 - core, me, 0), (1, 1, ne)).reshape(ne)
    gidx = jnp.concatenate(
        [jnp.roll(mine_order, -1) * 2 + core, jnp.roll(other_order, -1) * 2 + 1 - core]
    )
    scal = jnp.stack([me * n_loc + 1 - core, me * n_loc + core, 1 - core, core]).astype(jnp.int32)

    def fence(*vs):
        return list(lax.optimization_barrier(tuple(vs)))

    def halves(v):
        v = v.reshape(2, v.shape[0] // 2, v.shape[1])
        return (
            lax.dynamic_index_in_dim(v, core, 0, False),
            lax.dynamic_index_in_dim(v, 1 - core, 0, False),
        )

    units = ff // ne
    wide_f = -(-units // LANES) * LANES

    def spread(v):
        v = v.reshape(v.shape[0], ne, units).transpose(1, 0, 2)
        return jnp.pad(v, ((0, 0), (0, 0), (0, wide_f - units)))

    def exchange(v):
        return lax.all_to_all(v, "expert", split_axis=0, concat_axis=0, tiled=True)

    expert_gate, expert_up, expert_down = (
        pltpu.with_memory_space_constraint(v, pltpu.HBM) for v in (expert_gate, expert_up, expert_down)
    )
    sgu = jnp.concatenate([spread(halves(shared_gate)[0]), spread(halves(shared_up)[0])], axis=2)
    sdn = jnp.pad(shared_down, ((0, wide_f - units), (0, 0)))

    split = 2 * d
    aux = jnp.concatenate(
        [
            w_router,
            attn_gain[:, None],
            moe_gain[:, None],
            jnp.zeros((w_router.shape[0], LANES - n_exp - 2), BF),
        ],
        axis=1,
    )
    left, left_other = (jnp.concatenate(v, axis=1) for v in zip(halves(w_query), halves(w_key)))
    right, right_other = (
        jnp.concatenate(v, axis=1) for v in zip(halves(w_value), halves(w_out), halves(aux))
    )
    store_shape = (hbm((d + 2 * tok, wide), BF),)
    planes = ring_perm(nd, ne, True)
    way = (core + lax.axis_index("dp") // 2) % 2
    same = lax.dynamic_slice(table, (way, me, 0), (1, 1, ne)).reshape(ne)
    back = lax.dynamic_slice(table, (1 - way, me, 0), (1, 1, ne)).reshape(ne)
    idx = jnp.concatenate([same * 2 + core, back * 2 + 1 - core, back * 2 + core, same * 2 + 1 - core])
    kinds = [(0, 0), (0, split)] * 2
    store = place_call(
        kinds, [0, 0, ne, ne], idx, [left, right, left_other, right_other], store_shape, ()
    )
    crossed = 2 if nd > 2 else 0

    def place(groups, into):
        spots, pieces = [], []
        for near, far_side, two in groups:
            spots += [near, near, far_side, far_side]
            pieces += [*two, *[swap(v, 1) for v in two]]
        return place_call(kinds * len(groups), spots, idx, pieces, store_shape, into)

    over = {}
    last = ne - 1 - crossed
    for i in range(1, last + 1):
        left = lax.ppermute(left, both, planes)
        right = lax.ppermute(right, both, planes)
        if i <= crossed:
            over[i] = (swap(left, 2), swap(right, 2))
        if i == 2:
            left, sgu = fence(left, sgu)
            sgu = exchange(sgu)
        if i == 4:
            left, sgu, sdn = fence(left, sgu, sdn)
            sgu = jnp.stack([sgu, swap(sgu, 1)])
            sgu = jnp.where(core == 0, sgu, sgu[::-1]).transpose(1, 0, 2, 3).reshape(d, 2 * wide_f)
        if i == 5:
            left, sgu = fence(left, sgu)
        if i - 2 in over:
            xl, xr = over[i - 2]
            left, xl = fence(left, xl)
            if i < last:
                over[i - 2] = (xl, xr)
        if i - 3 in over:
            xl, xr = over[i - 3]
            right, xr = fence(right, xr)
            over[i - 3] = (xl, xr)
        if i < last:
            groups = [(i, ne + i, (left, right))]
            if i == 4 and 1 in over:
                groups.append((2 * ne + 1, 3 * ne + 1, over.pop(1)))
            placed = place(groups, store)
            left = fence(left, *store)[0]
            right = fence(right, *store)[0]
        else:
            left, right, *store = fence(left, right, *store)
            groups = [(i, ne + i, (left, right))]
            groups += [(2 * ne + k, 3 * ne + k, over[k]) for k in sorted(over)]
            placed = place(groups, store)
        store = placed

    half = HD // 2
    freq = ROPE_BASE ** (-2.0 * np.arange(half) / HD)
    ang = np.arange(tok)[:, None] * freq[None, :]
    cos = jnp.asarray(np.concatenate([np.cos(ang), np.cos(ang)], 1).astype(np.float32))
    sin = jnp.asarray(np.concatenate([-np.sin(ang), np.sin(ang)], 1).astype(np.float32))
    seg_row = segment_ids
    seg_col = segment_ids.reshape(tok, 1)

    g0, left, right = fence(out_grad, left, right)
    grads = [g0, ring(g0)]
    store, res, gate, pay, gains = pl.pallas_call(
        functools.partial(attn_forward, n_exp),
        out_shape=store_shape
        + (
            hbm((tok, d), F32),
            hbm((tok, LANES), F32),
            shape((extra, d), BF),
            shape((8, d), F32),
        ),
        in_specs=[whole()] * 6 + [far()],
        out_specs=[far()] * 3 + [whole()] * 2,
        scratch_shapes=[VMEM((d, wide), BF)]
        + [VMEM((tok, d), BF)] * 5
        + [
            VMEM((tok, d), F32),
            VMEM((tok, LANES), F32),
            pltpu.SemaphoreType.DMA((5,)),
            pltpu.SemaphoreType.DMA((7,)),
        ],
        input_output_aliases={6: 0},
        compiler_params=params(36),
        cost_estimate=cost(2 * tok * d * d * 4, d * wide * 2),
        name="attn_forward",
    )(hidden_in, seg_col, seg_row, routes, cos, sin, *store)
    pay, grads[1] = fence(pay, grads[1])

    def start_flow(parts):
        return {"parts": parts, "at": 0, "acc": parts(0).astype(BF)}

    def advance(flow, got):
        flow["at"] += 1
        if flow["at"] == ne - 1:
            flow["got"] = got
        else:
            flow["acc"] = (got.astype(F32) + flow["parts"](flow["at"])).astype(BF)

    def ring_total(flow):
        return flow["got"].astype(F32) + flow["parts"](ne - 1)

    def token_parts(parts):
        return lambda i: parts[(i + 1) % ne].astype(F32)

    def dense_parts(mine, others):
        def part(i):
            at = i
            for group in others:
                if at < group.shape[0]:
                    return mine[i].astype(F32) + group[at].astype(F32)
                at -= group.shape[0]

        return part

    down_shapes = (hbm((n_loc, ff, d), F32),)
    gu_shapes = (hbm((n_loc, d, ff), F32),) * 2
    n_down, n_gu = 4, 8
    waiting, landed, shared_out = [], [], []
    finished = {"down": (), "gu": ()}

    def queue(name, low, count):
        height = low.shape[0] // count
        for j in range(count):
            waiting.append((name, j * height, lax.slice_in_dim(low, j * height, (j + 1) * height)))

    def across(low):
        return swap(low, 2) if nd > 2 else low * 0

    def summed(low, more):
        total = low.astype(F32) + more.astype(F32)
        bit = 4
        while bit < nd:
            low = total.astype(BF)
            total = low.astype(F32) + swap(low, bit).astype(F32)
            bit *= 2
        return total.astype(BF)

    def emit():
        names = set()
        for name, start, mine, other in shared_out:
            if name not in finished:
                held[name] = (start, mine, other)
                continue
            shapes = down_shapes if name == "down" else gu_shapes
            finished[name] = emit_call(start, scal, mine, other, shapes, finished[name])
            names.add(name)
        shared_out.clear()
        return sorted(names)

    held = {}

    def slot(flows=(), sends=(), swaps=(), cross=0, compute=None, keep=(), ready=None, write=True, joint=True):
        chunks = waiting[:cross]
        del waiting[:cross]
        summing = [(name, start, summed(low, more)) for (name, start, low), more in landed]
        landed.clear()
        moved = [ring(f["acc"]) for f in flows] + [ring(v) for v in sends]
        moved += [across(low) for _, _, low in chunks]
        moved += [swap(v, 1) for v in swaps]
        moved += [swap(mine, 1) for _, _, mine in summing]
        names = emit() if write else []
        done = list(compute()) if compute is not None else []
        late = [v for name in names for v in finished[name]]
        if joint:
            out = fence(*moved, *done, *keep, *late)
        else:
            done = fence(*done)
            out = [fence(v, done[0])[0] for v in moved] + done

        def pop(count):
            first = out[:count]
            del out[:count]
            return first

        arrived = pop(len(flows))
        sent = pop(len(sends))
        landed.extend(zip(chunks, pop(len(chunks))))
        swapped = pop(len(swaps))
        if ready is not None:
            ready(swapped)
        for f, got in zip(flows, arrived):
            advance(f, got)
        for (name, start, mine), other in zip(summing, pop(len(summing))):
            shared_out.append((name, start, mine, other))
        done = pop(len(done))
        kept = pop(len(keep))
        for name in names:
            finished[name] = tuple(pop(len(finished[name])))
        return sent, swapped, done, kept

    pays = [pay]
    saved = ()
    in_parts, out_parts = [], []
    flow_in = None
    for i in range(ne):
        sends = []
        if i + 1 < ne:
            sends.append(pays[i])
        if i + 2 < ne:
            sends.append(grads[i + 1])
        if i == ne - 2:
            flow_in = start_flow(token_parts(in_parts))

        def block(i=i):
            new, ins, outs = expert_call(
                i, 1, cap, n_exp, scal, pays[i : i + 1], grads[i : i + 1],
                (expert_gate, expert_up, expert_down, sgu, sdn), saved,
            )
            held["saved"] = new
            return [ins[0], outs[0]]

        sent, _, done, _ = slot([flow_in] if flow_in else [], sends, compute=block, joint=False)
        saved = held["saved"]
        in_parts.append(done[0])
        out_parts.append(done[1])
        if i + 1 < ne:
            pays.append(sent[0])
        if i + 2 < ne:
            grads.append(sent[-1])

    xr, gr, gh, dgu, sum_gu, sum_dn = saved
    hw = d // 2
    gu_halves = sum_gu.astype(BF).reshape(ne, 2, hr, 2 * wide_f).transpose(1, 0, 2, 3)
    dn_halves = sum_dn[0:units].astype(BF).reshape(units, 2, hw).transpose(1, 0, 2)

    def of_side(v, side):
        return lax.dynamic_index_in_dim(v, side, 0, False)

    flow_out = start_flow(token_parts(out_parts))
    _, (gu_more, dn_more), (down_t,), _ = slot(
        [flow_in, flow_out],
        swaps=[of_side(gu_halves, 1 - core), of_side(dn_halves, 1 - core)],
        compute=lambda: [dot_tn(gh[0], gr[0]).astype(BF)],
    )

    def add(left, right):
        return (left.astype(F32) + right.astype(F32)).astype(BF)

    _, (down_got,), (down_m,), _ = slot(
        [flow_in, flow_out], swaps=[down_t], compute=lambda: [dot_tn(gh[1], gr[1]).astype(BF)]
    )
    queue("down", add(down_m, down_got), n_down)
    _, _, (gu_t,), _ = slot(
        [flow_in, flow_out], cross=1, compute=lambda: [dot_tn(xr[0], dgu[0]).astype(BF)]
    )
    _, _, (gu_m,), _ = slot(
        [flow_in, flow_out], cross=1, compute=lambda: [dot_tn(xr[1], dgu[1]).astype(BF)]
    )
    _, (gu_got,), _, _ = slot([flow_in], swaps=[gu_t], cross=1, write=False)
    while flow_in["at"] < ne - 1:
        slot([flow_in])
    height = d // n_gu
    for j in range(n_gu):
        cut_rows = slice(j * height, (j + 1) * height)
        waiting.append(("gu", j * height, add(gu_m[cut_rows], gu_got[cut_rows])))
    waiting.insert(2, ("sgu", 0, add(of_side(gu_halves, core), gu_more)))
    waiting.insert(3, ("sdn", 0, add(of_side(dn_halves, core), dn_more)))
    rs_in = flow_in["got"]

    soon = 3

    def backward():
        return pl.pallas_call(
            functools.partial(attn_backward, n_exp),
            out_shape=(
                shape((tok, d), F32),
                hbm((ne, hr, wide), BF),
                hbm((hr, wide), BF),
                hbm((soon, hr, wide), BF),
                hbm((ne - 1 - soon, hr, wide), BF),
            ),
            in_specs=[whole(SMEM)] + [whole()] * 10 + [far()] * 3,
            out_specs=[whole()] + [far()] * 4,
            scratch_shapes=[
                VMEM((d, wide), BF),
                VMEM((d, wide), BF),
            ]
            + [VMEM((tok, d), BF)] * 8
            + [
                VMEM((extra, d), BF),
                VMEM((tok, d), F32),
                pltpu.SemaphoreType.DMA((9,)),
                pltpu.SemaphoreType.DMA((2 * ne,)),
            ],
            compiler_params=params(56),
            cost_estimate=cost(2 * tok * d * d * 8, 2 * d * wide * 2),
            name="attn_backward",
        )(
            gidx, hidden_in, out_grad, seg_col, seg_row, cos, sin, gate, gains, rs_in, in_parts[0],
            store, pay, res,
        )

    _, _, (input_grad, d_mine, d_first, d_soon, d_later), _ = slot(
        [flow_out], cross=2, compute=backward, write=False
    )
    others = [swap(d_first, 1)[None]]
    flow_d = start_flow(dense_parts(d_mine, others))
    slot([flow_d], swaps=[d_soon], cross=2, ready=others.extend)
    slot([flow_d], swaps=[d_later], cross=1, ready=others.extend)

    def shared_exchange():
        if "sgu" in held and "sgu_sent" not in held:
            _, mine, _ = held["sgu"]
            held["sgu_sent"] = True
            return [exchange(mine)]
        return []

    pick = core == 0

    def sides(name):
        _, mine, other = held[name]
        mine = mine.astype(F32)
        other = other.astype(F32)
        return jnp.where(pick, mine, other), jnp.where(pick, other, mine)

    def row_halves():
        held["rows"] = (0, held["spread"], held["spread_other"])
        both_rows = jnp.concatenate(sides("rows"), axis=1)
        g_gate = both_rows[:, :, 0:units].transpose(1, 0, 2).reshape(2 * hr, ff)
        g_up = both_rows[:, :, wide_f : wide_f + units].transpose(1, 0, 2).reshape(2 * hr, ff)
        return [g_gate, g_up]

    while flow_d["at"] < ne - 1:
        ready_rows = "spread_other" in held and "gate_up" not in held
        swaps = [held["spread"]] if "spread" in held and "spread_other" not in held else []
        _, swapped, got, _ = slot(
            [flow_d], swaps=swaps, cross=1, compute=row_halves if ready_rows else shared_exchange
        )
        if ready_rows:
            held["gate_up"] = got
        elif got:
            held["spread"] = got[0]
        if swapped:
            held["spread_other"] = swapped[0]
    low = ring_total(flow_d).astype(BF)
    first_rows = -(-hr // 32) * 16
    waiting.append(("dense0", 0, low[0:first_rows]))
    waiting.append(("dense1", 0, low[first_rows:hr]))
    while waiting or landed or flow_out["at"] < ne - 1:
        slot([flow_out] if flow_out["at"] < ne - 1 else [], cross=1)
    emit()

    output = res + flow_out["got"].astype(F32) + out_parts[0].astype(F32)
    upper, lower = sides("dense0"), sides("dense1")
    g_d = jnp.concatenate([upper[0], lower[0], upper[1], lower[1]], axis=0)
    g_gate, g_up = held["gate_up"]
    g_dn = jnp.concatenate(sides("sdn"), axis=1)
    (down_w,) = finished["down"]
    gate_w, up_w = finished["gu"]
    return (
        output,
        input_grad,
        g_d[:, 4 * d + n_exp],
        g_d[:, 0:d],
        g_d[:, d : 2 * d],
        g_d[:, 2 * d : 3 * d],
        g_d[:, 3 * d : 4 * d],
        g_d[:, 4 * d + n_exp + 1],
        g_d[:, 4 * d : 4 * d + n_exp],
        g_gate,
        g_up,
        g_dn,
        gate_w,
        up_w,
        down_w,
    )


def solution(mesh):
    nd = mesh.shape["dp"]
    ne = mesh.shape["expert"]
    tokens = P(("dp", "expert"), None)
    vector = P("expert")
    matrix = P("expert", None)
    cube = P("expert", None, None)
    return jax.shard_map(
        functools.partial(body, nd, ne),
        mesh=mesh,
        in_specs=(tokens,) * 4
        + (vector, matrix, matrix, matrix, matrix, vector)
        + (matrix,) * 4
        + (cube,) * 3,
        out_specs=(tokens, tokens, vector, matrix, matrix, matrix, matrix, vector)
        + (matrix,) * 4
        + (cube,) * 3,
        check_vma=False,
    )
```
